32 devices in a mesh: lat: 8 (over z, x), lon: 4 (over y, core).
Axes of the slice: x: 2, y: 2, z: 4, core: 2. Of those that a mesh axis runs over, the one named last changes fastest.
Arguments:
- departure_in: float32 [16384, 256], P(('lat', 'lon')), may hold values from -20 to 20
- obs_owner: int32 [16384, 1], P(('lat', 'lon')), may hold values from 0 to 31; in each aligned block of 512 rows (0 to 511, 512 to 1023, ...) at most 24 rows name the same one
- obs_cell: int32 [16384], P(('lat', 'lon')), may hold values from 0 to 12287
- obs_count: int32 [32], P(('lat', 'lon')), may hold values from 256 to 512, as said below
- qc_mask: int32 [16384], P(('lat', 'lon')), may hold values 0 or 1
- channel_weight: float32 [256], replicated, may hold values from 0.2 to 2
- jacobian: float32 [69, 256], replicated, may hold values from -0.75 to 0.75
- conv_taps: bfloat16 [9, 64, 69], replicated, may hold values from -0.25 to 0.25
- projection: bfloat16 [69, 64], replicated, may hold values from -0.75 to 0.75
- slope: bfloat16 [64, 384, 1024], P(None, 'lat', 'lon'), may hold values from 0 to 1.09375
Outputs:
- increment: float32 [69, 384, 1024], P(None, 'lat', 'lon')
- departures: float32 [16384, 256], P(('lat', 'lon'))
The draws below stay inside these ranges and needn't reach their ends.
Inputs may be any that keep to these rules, and one draw needn't show every extreme that they name: `obs_owner`: in the rows of one device at most 24 name one tile, a bound that some block reaches. `obs_count`: some device uses all 512 rows.
All inputs are finite; a program needn't handle non-finite values. No bound on the sum of `qc_mask` on one device may be relied on, other than what follows from the above.
Results may differ from the reference program's by a relative error of at most 0.009.
Values may be sent and summed in bfloat16 or wider, within the bound.
No kernel may reach another device: no remote copies, remote signals or barrier semaphores. Data moves between devices by JAX's collectives and lax.ppermute only.
A program may use at most 128 MiB of HBM per device.

```python
import math
import jax
import jax.numpy as jnp
import numpy as np
from jax import lax

C = 69
F = 64
RAD = 256
TLAT = 48
TLON = 256
OBS_DEV = 512
ITERS = 2
TILES = 32
NLAT = 384
NLON = 1024
OBS_ALL = 16384
CAP = 24
N_LON = 4


def draw_departure_in(key, part):
    key = jax.random.fold_in(key, 7)
    key_base, key_scale = jax.random.split(key, 2)
    device_of = (jnp.arange(OBS_ALL) // OBS_DEV).astype(jnp.float32)
    rise = 3.0 ** (device_of / max(TILES - 1, 1))
    row_scale = jnp.exp(jax.random.uniform(key_scale, (OBS_ALL, 1), minval=0.0, maxval=math.log(3.0)))
    base = jax.random.normal(key_base, (OBS_ALL, RAD))
    base = jnp.clip(base, -5.0, 5.0)
    return (0.4 * base * row_scale * rise[:, None]).astype(jnp.float32)


def draw_obs_count(key, part):
    key = jax.random.fold_in(key, 11)
    key_count, key_full = jax.random.split(key)
    counts = jax.random.randint(key_count, (TILES,), OBS_DEV // 2, OBS_DEV + 1)
    full_device = jax.random.randint(key_full, (), 0, TILES)
    return jnp.where(jnp.arange(TILES) == full_device, OBS_DEV, counts).astype(jnp.int32)


def plant(values, rng, least, top_value):
    dims = values.shape
    index_at = [jax.random.randint(jax.random.fold_in(rng, axis), (), 0, dims[axis]) for axis in range(len(dims))]
    values = values.at[tuple(index_at)].set(least)
    longest = dims.index(max(dims))
    index_at[longest] = (index_at[longest] + 1) % dims[longest]
    return values.at[tuple(index_at)].set(top_value)


def block_levels(rng, shape, cuts, smallest, high):
    def one(dim, shards_of):
        draws = jax.random.uniform(jax.random.fold_in(jax.random.fold_in(rng, 6), dim), (shards_of,), jnp.float32, smallest / len(cuts), high / len(cuts))
        return jnp.repeat(jnp.exp(draws), shape[dim] // shards_of).reshape((-1,) + (1,) * (len(shape) - dim - 1))

    loudness = one(*cuts[0])
    for cut in cuts[1:]:
        loudness = loudness * one(*cut)
    return loudness


def deal_out(key, own, number, rows, number_of, top, reach, skew):
    ranking = jax.random.permutation(key, number_of)
    heavy_load, common = portions_of(number_of, rows * top, reach, skew, True), portions_of(number_of, rows * top, reach, skew, False)
    places = jnp.arange(number_of)

    def named(sizes, turn):
        used = int((sizes > 0).sum())
        fixed = max(1, used // 4)
        passed = fixed + (places - fixed + turn * (used - fixed)) % max(1, number_of - fixed)
        return jnp.zeros((number_of,), jnp.int32).at[ranking[jnp.where(places < fixed, places, passed)]].set(jnp.asarray(sizes, jnp.int32))

    sizes = jnp.where(number % 4 == 0, named(heavy_load, number // 4), named(common, number - number // 4 - 1))
    mixed = jax.random.permutation(jax.random.fold_in(own, 3), number_of)
    giver, taker = mixed[0:number_of // 2 * 2:2], mixed[1:number_of // 2 * 2:2]
    room = jnp.minimum(sizes[giver] - 1, reach - sizes[taker]) // 2
    room = jnp.where((giver == ranking[0]) | (taker == ranking[0]) | (sizes[taker] == 0), 0, jnp.maximum(room, 0))
    passed = jax.random.randint(jax.random.fold_in(own, 4), (number_of // 2,), 0, 1 << 20) % (room + 1)
    sizes = sizes.at[giver].add(-passed).at[taker].add(passed)
    items = jnp.searchsorted(jnp.cumsum(sizes), jnp.arange(rows * top), side="right").astype(jnp.int32)
    table = items.reshape(top, rows).T
    table = table[jax.random.permutation(jax.random.fold_in(own, 1), rows)]
    turn = jax.random.randint(jax.random.fold_in(own, 2), (rows, 1), 0, top)
    return jnp.take_along_axis(table, (jnp.arange(top)[None, :] + turn) % top, axis=1)


def portions_of(count, total, reach, skew, full):
    loads = [(1 << 20) // math.isqrt(standing ** skew) + 1 for standing in range(1, count + 1)]
    largest = reach if full else min(reach, max(-(-total // count), total * loads[0] // sum(loads)))
    least = 1 if total - largest >= count - 1 else 0
    given, spare = [largest] + [least] * (count - 1), total - largest - least * (count - 1)
    while spare > 0:
        movable = [i for i in range(1, count) if given[i] < largest] or [i for i in range(1, count) if given[i] < reach]
        pool, left = sum([loads[i] for i in movable]), spare
        for i in movable:
            extra = min(reach - given[i], max(1, left * loads[i] // pool), spare)
            given[i] = given[i] + extra
            spare = spare - extra
    return np.array(given)


def scatter_about(key, dims, width, most, kind=jnp.bfloat16):
    values = jax.random.normal(key, dims, jnp.float32) * width
    return jnp.minimum(jnp.maximum(values, -most), most).astype(kind)


def setup_inputs(seed: int = 0) -> dict:
    key_list = jax.random.split(jax.random.key(seed), 11)
    departure_in = draw_departure_in(jax.random.fold_in(key_list[10], 71), 0)
    obs_owner_keys = jax.random.split(jax.random.fold_in(key_list[1], 1), OBS_ALL // OBS_DEV)
    obs_owner_turns = jax.random.permutation(jax.random.fold_in(key_list[1], 3), OBS_ALL // OBS_DEV)
    obs_owner = jax.vmap(lambda own, number: deal_out(jax.random.fold_in(key_list[1], 2), own, number, OBS_DEV, TILES, 1, CAP, 2))(obs_owner_keys, obs_owner_turns).reshape((OBS_ALL, 1))
    obs_cell = plant(jax.random.randint(key_list[2], (OBS_ALL,), 0, TLAT * TLON), jax.random.fold_in(key_list[2], 1), 0, (TLAT * TLON) - 1).astype(jnp.int32)
    obs_count = draw_obs_count(jax.random.fold_in(key_list[10], 71), 0)
    qc_mask = plant((jax.random.randint(key_list[4], (OBS_ALL,), 0, 4) < 3).astype(jnp.int32), jax.random.fold_in(key_list[4], 1), 0, 1)
    channel_weight = jnp.clip(jnp.exp(jax.random.uniform(key_list[5], (RAD,), jnp.float32, math.log(0.2), math.log(2.0))), 0.2, 2.0)
    jacobian = scatter_about(key_list[6], (C, RAD), C ** -0.5, 0.75, jnp.float32)
    conv_taps = scatter_about(key_list[7], (9, F, C), (9 * C) ** -0.5, 0.25)
    projection = scatter_about(key_list[8], (C, F), F ** -0.5, 0.75)
    slope = jnp.clip(1.09375 * jax.random.uniform(key_list[9], (F, NLAT, NLON), jnp.float32) ** block_levels(key_list[9], (F, NLAT, NLON), ((1, 8), (2, 4)), -0.2, 0.2), 0.0, 1.09375).astype(jnp.bfloat16)
    return dict(departure_in=departure_in, obs_owner=obs_owner, obs_cell=obs_cell, obs_count=obs_count, qc_mask=qc_mask, channel_weight=channel_weight, jacobian=jacobian, conv_taps=conv_taps, projection=projection, slope=slope)


def padded_field(field_in):
    taller = jnp.pad(field_in, ((0, 0), (1, 1), (0, 0)))
    return jnp.concatenate([taller[:, :, -1:], taller, taller[:, :, :1]], axis=2)


def tangent(vector, conv_taps, projection, slope):
    height, breadth = vector.shape[1], vector.shape[2]
    rounded = lax.optimization_barrier(vector.astype(jnp.bfloat16))
    widened = padded_field(rounded).astype(jnp.float32)
    hidden = jnp.zeros((conv_taps.shape[1], height, breadth), jnp.float32)
    for number in range(9):
        row_shift, col_shift = number // 3, number % 3
        hidden = hidden + jnp.einsum("fc,cij->fij", conv_taps[number].astype(jnp.float32),
                                     widened[:, row_shift:row_shift + height, col_shift:col_shift + breadth],
                                     precision=lax.Precision.HIGHEST)
    active = lax.optimization_barrier((slope.astype(jnp.float32) * hidden).astype(jnp.bfloat16)).astype(jnp.float32)
    return vector + jnp.einsum("cf,fij->cij", projection.astype(jnp.float32), active, precision=lax.Precision.HIGHEST)


def adjoint(adjoint_in, conv_taps, projection, slope):
    height, breadth = adjoint_in.shape[1], adjoint_in.shape[2]
    rounded = lax.optimization_barrier(adjoint_in.astype(jnp.bfloat16)).astype(jnp.float32)
    pulled = jnp.einsum("cf,cij->fij", projection.astype(jnp.float32), rounded, precision=lax.Precision.HIGHEST)
    spread = lax.optimization_barrier((slope.astype(jnp.float32) * pulled).astype(jnp.bfloat16))
    widened = padded_field(spread).astype(jnp.float32)
    result = adjoint_in
    for number in range(9):
        row_shift, col_shift = 2 - number // 3, 2 - number % 3
        result = result + jnp.einsum("fc,fij->cij", conv_taps[number].astype(jnp.float32),
                                     widened[:, row_shift:row_shift + height, col_shift:col_shift + breadth],
                                     precision=lax.Precision.HIGHEST)
    return result


def reference(departure_in, obs_owner, obs_cell, obs_count, qc_mask, channel_weight, jacobian, conv_taps, projection, slope):
    rows_all = departure_in.shape[0]
    index = jnp.arange(rows_all, dtype=jnp.int32)
    valid = (index % OBS_DEV) < obs_count[index // OBS_DEV]
    row_weight = qc_mask.astype(jnp.float32) * valid.astype(jnp.float32)
    owners = obs_owner[:, 0]
    lat_pos = (owners // N_LON) * TLAT + obs_cell // TLON
    lon_pos = (owners % N_LON) * TLON + obs_cell % TLON
    global_cell = (lat_pos * NLON + lon_pos).astype(jnp.int32)
    row_terms = row_weight[:, None] * jnp.dot(departure_in * channel_weight[None, :], jacobian.T,
                                              precision=lax.Precision.HIGHEST)
    cell_sums = jax.ops.segment_sum(row_terms, global_cell, num_segments=NLAT * NLON)
    forcing = cell_sums.T.reshape(C, NLAT, NLON)
    cell_weight = jax.ops.segment_sum(row_weight, global_cell, num_segments=NLAT * NLON).reshape(1, NLAT, NLON)
    gram_matrix = jnp.dot(jacobian * channel_weight[None, :], jacobian.T, precision=lax.Precision.HIGHEST)

    def hessian(vector):
        state = tangent(vector, conv_taps, projection, slope)
        weighted = cell_weight * jnp.einsum("ck,kij->cij", gram_matrix, state, precision=lax.Precision.HIGHEST)
        return vector + adjoint(weighted, conv_taps, projection, slope)

    solution = jnp.zeros((C, NLAT, NLON), jnp.float32)
    residual = adjoint(forcing, conv_taps, projection, slope)
    direction = residual
    norm_now = jnp.sum(residual * residual)
    for sweep in range(ITERS):
        curved = hessian(direction)
        step_size = norm_now / jnp.sum(direction * curved)
        solution = solution + step_size * direction
        residual = residual - step_size * curved
        norm_next = jnp.sum(residual * residual)
        direction = residual + (norm_next / norm_now) * direction
        norm_now = norm_next
    final_state = tangent(solution, conv_taps, projection, slope).reshape(C, NLAT * NLON)
    columns = final_state[:, global_cell].T
    evolved = jnp.dot(columns, jacobian, precision=lax.Precision.HIGHEST)
    return solution, departure_in - evolved
```

```python
import functools

import jax
import jax.numpy as jnp
import numpy as np
from jax import lax
from jax.experimental import pallas as pl
from jax.experimental.pallas import tpu as pltpu
from jax.sharding import PartitionSpec as P

ITERS = 2
HALO = 4
LANES = 128
SIDE = 2 * HALO
BF = jnp.bfloat16
F32 = jnp.float32
INTERPRET = False


def mxu(a, b, dims=((1,), (0,)), precision=None):
    return lax.dot_general(a, b, (dims, ((), ())), precision=precision, preferred_element_type=F32)


def call(kernel, outs, args, scratch=(), smem=0, vmem=100):
    def space(i):
        return pl.BlockSpec(memory_space=pltpu.SMEM if i < smem else pltpu.VMEM)

    return pl.pallas_call(
        kernel,
        out_shape=outs,
        in_specs=[space(i) for i in range(len(args))],
        out_specs=jax.tree.map(lambda _: pl.BlockSpec(memory_space=pltpu.VMEM), outs),
        scratch_shapes=scratch,
        interpret=INTERPRET,
        compiler_params=pltpu.CompilerParams(vmem_limit_bytes=vmem * 2**20 // 2),
    )(*args)


def split3(x):
    hi = x.astype(BF)
    rest = x - hi.astype(F32)
    mid = rest.astype(BF)
    return hi, mid, (rest - mid.astype(F32)).astype(BF)


def pack_kernel(tiles, cap, lon_size, channels, count, dep, owner_row, owner_col, cell_row, qc_row,
                weight, jac, send, slot_out):
    rows = dep.shape[0]
    slots = send.shape[0]
    hit = (lax.broadcasted_iota(jnp.int32, (tiles, rows), 0) == owner_row[...]).astype(BF)
    before = (lax.broadcasted_iota(jnp.int32, (rows, rows), 0)
              < lax.broadcasted_iota(jnp.int32, (rows, rows), 1)).astype(BF)
    earlier = mxu(hit, before)
    rank = jnp.sum(earlier * hit.astype(F32), axis=0, keepdims=True)
    slot = owner_row[...] * cap + rank.astype(jnp.int32)
    place = (lax.broadcasted_iota(jnp.int32, (slots, rows), 0) == slot).astype(BF)

    hit_c = (lax.broadcasted_iota(jnp.int32, (rows, tiles), 1) == owner_col[...]).astype(BF)
    before_c = (lax.broadcasted_iota(jnp.int32, (rows, rows), 1)
                < lax.broadcasted_iota(jnp.int32, (rows, rows), 0)).astype(BF)
    rank_c = jnp.sum(mxu(before_c, hit_c) * hit_c.astype(F32), axis=1, keepdims=True)
    slot_out[...] = owner_col[...] * cap + rank_c.astype(jnp.int32)

    used = (lax.broadcasted_iota(jnp.int32, (1, rows), 1) < count[0]).astype(F32)
    row_weight = used * qc_row[...].astype(F32)
    terms = mxu(jac[...], dep[...] * weight[...], ((1,), (1,)), lax.Precision.HIGHEST) * row_weight
    lat = cell_row[...] // lon_size
    lon = cell_row[...] - lat * lon_size
    wide = lax.broadcasted_iota(jnp.int32, (LANES, rows), 0)
    terms = jnp.concatenate([terms, jnp.zeros((LANES - terms.shape[0], rows), F32)], axis=0)
    terms = jnp.where(wide == channels, row_weight, terms)
    terms = jnp.where(wide == channels + 1, lat.astype(F32), terms)
    terms = jnp.where(wide == channels + 2, lon.astype(F32), terms)
    send[...] = mxu(place, terms.astype(BF), ((1,), (1,))).astype(BF)


def turned(got, channels, padded):
    flat = got[...].astype(F32)
    turn = flat.T
    lat_row = turn[channels + 1 : channels + 2].astype(jnp.int32)
    lon_row = turn[channels + 2 : channels + 3].astype(jnp.int32)
    lat_col = flat[:, channels + 1 : channels + 2].astype(jnp.int32)
    lon_col = flat[:, channels + 2 : channels + 3].astype(jnp.int32)
    keep = lax.broadcasted_iota(jnp.int32, (padded, turn.shape[1]), 0) <= channels
    return jnp.where(keep, turn[:padded], 0.0), lat_row, lon_row, lat_col, lon_col


def edge_kernel(channels, height, breadth, got, north, south, west, east, nw, sw, ne, se):
    padded = north.shape[1]
    slots = got.shape[0]
    turn, lat_row, lon_row, lat, lon = turned(got, channels, padded)
    values = turn.astype(BF)
    col_hot = (lax.broadcasted_iota(jnp.int32, (slots, breadth), 1) == lon).astype(BF)
    for out, first in ((north, 0), (south, height - HALO)):
        lhs = jnp.concatenate(
            [values * (lat_row == first + k).astype(F32).astype(BF) for k in range(HALO)], axis=0)
        out[...] = mxu(lhs, col_hot).reshape(HALO, padded, breadth).astype(BF)
    at_west, at_east = lon < HALO, lon >= breadth - HALO
    at_north, at_south = lat < HALO, lat >= height - HALO
    col_west, col_east = HALO + lon, lon - (breadth - HALO)
    base = (height + HALO) * SIDE // LANES * LANES
    for out, mask, row, col, offset in (
        (west, at_west, lat + HALO, col_west, 0),
        (east, at_east, lat + HALO, col_east, 0),
        (nw, at_west & at_north, lat + height + HALO, col_west, base),
        (sw, at_west & at_south, lat - (height - HALO), col_west, 0),
        (ne, at_east & at_north, lat + height + HALO, col_east, base),
        (se, at_east & at_south, lat - (height - HALO), col_east, 0),
    ):
        target = jnp.where(mask, row * SIDE + col - offset, -1)
        hot = (lax.broadcasted_iota(jnp.int32, (slots, out.shape[1]), 1) == target).astype(BF)
        out[...] = mxu(values, hot).astype(BF)


def grid_kernel(channels, got, out):
    height, padded, breadth = out.shape
    slots = got.shape[0]
    turn, lat_row, _, _, lon = turned(got, channels, padded)
    values = turn.astype(BF)
    col_hot = (lax.broadcasted_iota(jnp.int32, (slots, breadth), 1) == lon).astype(BF)
    step = 8

    def body(block, _):
        lhs = jnp.concatenate(
            [values * (lat_row == block * step + k).astype(F32).astype(BF) for k in range(step)], axis=0)
        out[pl.ds(block * step, step)] = mxu(lhs, col_hot).reshape(step, padded, breadth)
        return 0

    lax.fori_loop(0, height // step, body, 0)


def main_kernel(channels, hidden, flags, got, inner, north, south, from_east, from_west, from_ne, from_se,
                from_nw, from_sw, slope, w_n, w_m, p_t, p_j, g3, first_out, second_out, reply,
                field, strip, ga, xb, vec, hi, y1):
    height, padded, breadth = inner.shape
    wide = breadth + LANES
    ext = height + 2 * HALO

    def is_in(i):
        above = (i >= HALO) | (flags[0] == 1)
        below = (i < height + HALO) | (flags[1] == 1)
        return (above & below).astype(F32)

    blocks = strip.shape[0]
    last = (height + HALO) * SIDE // LANES
    for k in range(blocks):
        part = pl.ds(k * LANES, LANES)
        q = from_east[:, part].astype(F32) + from_west[:, part].astype(F32)
        if k == 0:
            q = q + from_nw[...].astype(F32) + from_ne[...].astype(F32)
        if k == last:
            q = q + from_sw[...].astype(F32) + from_se[...].astype(F32)
        strip[k] = q

    per = LANES // SIDE

    def pull(i, y):
        u = mxu(p_t[...], y.astype(BF))
        ga[i] = (slope[i].astype(F32) * u).astype(BF)

    def begin(i, main):
        shift = LANES - (i % per) * SIDE - HALO
        shift = jnp.where(shift < 0, shift + LANES, shift)
        edge = pltpu.roll(strip[i // per], shift, 1)
        whole = jnp.concatenate([main, edge], axis=1)
        field[i] = whole
        pull(i, whole)

    def from_north(i, _):
        begin(i, north[i].astype(F32))
        return 0

    def from_inner(i, _):
        begin(i, inner[i - HALO])
        return 0

    def from_south(i, _):
        begin(i, south[i - (HALO + height)].astype(F32))
        return 0

    lax.fori_loop(0, HALO, from_north, 0, unroll=True)
    lax.fori_loop(HALO, HALO + height, from_inner, 0, unroll=2)
    lax.fori_loop(HALO + height, ext, from_south, 0, unroll=True)

    def spread(i, y):
        rows = ga[pl.ds(i - 1, 3)].reshape(3 * hidden, wide)
        o = mxu(w_n[...], rows)
        return (y + o[padded : 2 * padded] + pltpu.roll(o[:padded], wide - 1, 1)
                + pltpu.roll(o[2 * padded :], 1, 1))

    def tangent(i, v):
        rows = xb[pl.ds(i - 1, 3)].reshape(3 * padded, wide)
        o = mxu(w_m[...], rows)
        h = (o[hidden : 2 * hidden] + pltpu.roll(o[:hidden], 1, 1)
             + pltpu.roll(o[2 * hidden :], wide - 1, 1))
        act = (slope[i].astype(F32) * h).astype(BF)
        return v + mxu(p_j[...], act)

    def gram_of(s):
        s_hi = s.astype(BF)
        s_lo = (s - s_hi.astype(F32)).astype(BF)
        return mxu(g3[...], jnp.concatenate([s_hi, s_hi, s_lo], axis=0))

    def n_first(i, _):
        v = spread(i, field[i])
        vec[i] = v
        xb[i] = (v * is_in(i)).astype(BF)
        return 0

    lax.fori_loop(1, ext - 1, n_first, 0, unroll=2)

    def m_first(i, _):
        s = tangent(i, vec[i])
        cell_weight = field[i][channels : channels + 1]
        y = cell_weight * gram_of(s)
        hi[i, :padded] = s[:, :breadth].astype(BF)
        y1[i] = y
        pull(i, y)
        return 0

    lax.fori_loop(2, ext - 2, m_first, 0, unroll=2)

    def keep_first(i, _):
        first_out[i] = vec[i + HALO][:, :breadth]
        return 0

    lax.fori_loop(0, height, keep_first, 0, unroll=2)

    def n_second(i, _):
        v = spread(i, y1[i])
        vec[i] = v
        xb[i] = (v * is_in(i)).astype(BF)
        return 0

    lax.fori_loop(3, ext - 3, n_second, 0, unroll=2)

    turn, lat_row, lon_row, _, _ = turned(got, channels, padded)
    slots = got.shape[0]
    col_hot = (lax.broadcasted_iota(jnp.int32, (breadth, slots), 0) == lon_row).astype(BF)

    def m_second(i, rows):
        v = vec[i]
        s = tangent(i, v)
        second_out[i - HALO] = v[:, :breadth]
        hi[i, padded:] = s[:, :breadth].astype(BF)
        return rows + mxu(hi[i], col_hot) * (lat_row == i - HALO).astype(F32)

    rows = lax.fori_loop(HALO, HALO + height, m_second, jnp.zeros((2 * padded, slots), F32))
    row0, row1 = rows[:padded], rows[padded:]
    weight = turn[channels : channels + 1]
    curved0 = gram_of(row0) * weight
    curved1 = gram_of(row1) * weight
    real = lax.broadcasted_iota(jnp.int32, (padded, slots), 0) < channels
    first = jnp.where(real, turn, 0.0)

    def total(x):
        return jnp.sum(jnp.sum(x, axis=0, keepdims=True), axis=1, keepdims=True)

    sums = (total(first * row0), total(curved0 * row0), total(curved0 * row1), total(curved1 * row1))
    lane = lax.broadcasted_iota(jnp.int32, (1, LANES), 1)
    pieces = jnp.zeros((1, LANES), F32)
    for number, value in enumerate(sums):
        for part, piece in enumerate(split3(value)):
            pieces = jnp.where(lane == channels + 3 + 3 * number + part, piece.astype(F32), pieces)
    filler = jnp.zeros((LANES - padded, slots), F32)
    turned0 = jnp.concatenate([row0, filler], axis=0).T
    turned1 = jnp.concatenate([row1, filler], axis=0).T
    cap = reply_cap(slots, flags)
    leads = lax.broadcasted_iota(jnp.int32, (slots, LANES), 0)
    is_lead = (leads - (leads // cap) * cap) == 0
    lanes = lax.broadcasted_iota(jnp.int32, (slots, LANES), 1)
    reply[:, :LANES] = jnp.where(lanes < channels, turned0, jnp.where(is_lead, pieces, 0.0)).astype(BF)
    reply[:, LANES:] = turned1.astype(BF)


def reply_cap(slots, flags):
    return flags[2]


def scalars(reply, channels):
    sums = jnp.sum(reply[:, :LANES].astype(F32), axis=0, keepdims=True)

    def value(number):
        at = channels + 3 + 3 * number
        return sums[:, at : at + 1] + sums[:, at + 1 : at + 2] + sums[:, at + 2 : at + 3]

    a00, a01, a11, d11 = (value(n) for n in range(4))
    step0 = a00 / (a00 + a01)
    keep = 1.0 - step0
    norm1 = keep * keep * a00 - 2.0 * step0 * keep * a01 + step0 * step0 * a11
    c0 = keep + norm1 / a00
    c1 = -step0
    curve = (c0 * c0 * (a00 + a01) + 2.0 * c0 * c1 * (a01 + a11) + c1 * c1 * (a11 + d11))
    step1 = norm1 / curve
    return step0 + step1 * c0, step1 * c1


def final_kernel(channels, back, slot, dep, jac, first, second, increment, departures):
    slots = back.shape[0]
    rows = dep.shape[0]
    a, b = scalars(back, channels)
    place = (lax.broadcasted_iota(jnp.int32, (rows, slots), 1) == slot[...]).astype(BF)
    own = mxu(place, back[...])
    padded = jac.shape[0]
    state = a * own[:, :padded] + b * own[:, LANES : LANES + padded]
    departures[...] = dep[...] - mxu(state, jac[...], precision=lax.Precision.HIGHEST)
    increment[...] = a[None] * first[...] + b[None] * second[...]


def neighbours(axis, by, periodic):
    count = lax.axis_size(axis)
    pairs = [(i, (i + by)) for i in range(count)]
    return [(i, j % count) for i, j in pairs if periodic or 0 <= j < count]


def shift2(x, by_lat, by_lon):
    n_lat, n_lon = lax.axis_size("lat"), lax.axis_size("lon")
    pairs = [(i * n_lon + j, (i + by_lat) * n_lon + (j + by_lon) % n_lon)
             for i in range(n_lat) for j in range(n_lon) if 0 <= i + by_lat < n_lat]
    return lax.ppermute(x, ("lat", "lon"), pairs)


def wide_slope(slope):
    x = jnp.transpose(slope, (1, 0, 2))
    low = shift2(x[-HALO:], 1, 0)
    high = shift2(x[:HALO], -1, 0)
    x = jnp.concatenate([low, x, high], axis=0)
    left = shift2(x[:, :, -HALO:], 0, 1)
    right = shift2(x[:, :, :HALO], 0, -1)
    gap = jnp.zeros(x.shape[:2] + (LANES - 2 * HALO,), x.dtype)
    return jnp.concatenate([x, right, gap, left], axis=2)


def on_device(departure_in, obs_owner, obs_cell, obs_count, qc_mask, channel_weight, jacobian,
              conv_taps, projection, slope):
    channels, hidden = projection.shape
    height, breadth = slope.shape[1], slope.shape[2]
    tiles = lax.axis_size(("lat", "lon"))
    rows, radiances = departure_in.shape
    cap = max(2, 3 * rows // (2 * tiles))
    slots = tiles * cap
    padded = -(-channels // 16) * 16
    wide = breadth + LANES
    ext = height + 2 * HALO
    strip = -(-(ext * SIDE) // LANES) * LANES
    more = padded - channels

    def shape(dims, kind=F32):
        return jax.ShapeDtypeStruct(dims, kind)

    jac = jnp.pad(jacobian, ((0, more), (0, 0)))
    weight = channel_weight[None, :]
    send, slot = call(
        functools.partial(pack_kernel, tiles, cap, breadth, channels),
        (shape((slots, LANES), BF), shape((rows, 1), jnp.int32)),
        (obs_count, departure_in, obs_owner.reshape(1, rows), obs_owner, obs_cell[None, :],
         qc_mask[None, :], weight, jac),
        smem=1,
    )

    def swap(x):
        return lax.all_to_all(x.reshape(tiles, cap, -1), ("lat", "lon"), split_axis=0, concat_axis=0,
                              tiled=True).reshape(slots, -1)

    got = swap(send)

    gram = jnp.dot(jac * weight, jac.T, precision=lax.Precision.HIGHEST)
    gram_hi = gram.astype(BF)
    gram_lo = (gram - gram_hi.astype(F32)).astype(BF)
    g3 = jnp.concatenate([gram_hi, gram_lo, gram_hi], axis=1)
    taps = jnp.pad(conv_taps, ((0, 0), (0, 0), (0, more))).reshape(3, 3, hidden, padded)
    w_m = jnp.transpose(taps, (1, 2, 0, 3)).reshape(3 * hidden, 3 * padded)
    w_n = jnp.transpose(taps[::-1], (1, 3, 0, 2)).reshape(3 * padded, 3 * hidden)
    p_j = jnp.pad(projection, ((0, more), (0, 0)))
    p_t = p_j.T
    slope_wide = wide_slope(slope)

    edge = (HALO, padded, breadth)
    north, south, west, east, nw, sw, ne, se = call(
        functools.partial(edge_kernel, channels, height, breadth),
        (shape(edge, BF),) * 2 + (shape((padded, strip), BF),) * 2 + (shape((padded, LANES), BF),) * 4,
        (got,),
    )
    from_south = shift2(north, -1, 0)
    from_north = shift2(south, 1, 0)
    from_east = shift2(west, 0, -1)
    from_west = shift2(east, 0, 1)
    from_se = shift2(nw, -1, -1)
    from_ne = shift2(sw, 1, -1)
    from_sw = shift2(ne, -1, 1)
    from_nw = shift2(se, 1, 1)
    inner = call(functools.partial(grid_kernel, channels), shape((height, padded, breadth)), (got,))

    at = lax.axis_index("lat")
    flags = jnp.stack([at > 0, at < lax.axis_size("lat") - 1, cap]).astype(jnp.int32)
    first, second, reply = call(
        functools.partial(main_kernel, channels, hidden),
        (shape((height, padded, breadth)),) * 2 + (shape((slots, 2 * LANES), BF),),
        (flags, got, inner, from_north, from_south, from_east, from_west, from_ne, from_se, from_nw,
         from_sw, slope_wide, w_n, w_m, p_t, p_j, g3),
        scratch=[
            pltpu.VMEM((ext, padded, wide), F32),
            pltpu.VMEM((strip // LANES, padded, LANES), F32),
            pltpu.VMEM((ext, hidden, wide), BF),
            pltpu.VMEM((ext, padded, wide), BF),
            pltpu.VMEM((ext, padded, wide), F32),
            pltpu.VMEM((ext, 2 * padded, breadth), BF),
            pltpu.VMEM((ext, padded, wide), F32),
        ],
        smem=1,
        vmem=116,
    )
    back = swap(reply)
    first = jnp.transpose(first, (1, 0, 2))[:channels]
    second = jnp.transpose(second, (1, 0, 2))[:channels]
    return call(
        functools.partial(final_kernel, channels),
        (shape((channels, height, breadth)), shape((rows, radiances))),
        (back, slot, departure_in, jac, first, second),
    )


def solution(mesh):
    placed = (
        P(("lat", "lon"), None),
        P(("lat", "lon"), None),
        P(("lat", "lon")),
        P(("lat", "lon")),
        P(("lat", "lon")),
        P(),
        P(),
        P(),
        P(),
        P(None, "lat", "lon"),
    )
    return jax.shard_map(
        on_device,
        mesh=mesh,
        in_specs=placed,
        out_specs=(P(None, "lat", "lon"), P(("lat", "lon"), None)),
        check_vma=False,
    )
```

```python
import functools

import jax
import jax.numpy as jnp
import numpy as np
from jax import lax
from jax.experimental import pallas as pl
from jax.experimental.pallas import tpu as pltpu
from jax.sharding import PartitionSpec as P

ITERS = 2
HALO = 4
LANES = 128
SIDE = 2 * HALO
BF = jnp.bfloat16
F32 = jnp.float32
INTERPRET = False
G = (9, 13, 10, 12, 16)


def mxu(a, b, dims=((1,), (0,)), precision=None):
    return lax.dot_general(a, b, (dims, ((), ())), precision=precision, preferred_element_type=F32)


def call(kernel, outs, args, scratch=(), smem=0, vmem=100):
    def space(i):
        return pl.BlockSpec(memory_space=pltpu.SMEM if i < smem else pltpu.VMEM)

    return pl.pallas_call(
        kernel,
        out_shape=outs,
        in_specs=[space(i) for i in range(len(args))],
        out_specs=jax.tree.map(lambda _: pl.BlockSpec(memory_space=pltpu.VMEM), outs),
        scratch_shapes=scratch,
        interpret=INTERPRET,
        compiler_params=pltpu.CompilerParams(vmem_limit_bytes=vmem * 2**20 // 2),
    )(*args)


def split3(x):
    hi = x.astype(BF)
    rest = x - hi.astype(F32)
    mid = rest.astype(BF)
    return hi, mid, (rest - mid.astype(F32)).astype(BF)


def pack_kernel(tiles, cap, lon_size, channels, count, dep, owner_row, owner_col, cell_row, qc_row,
                weight, jac, send, slot_out):
    rows = dep.shape[0]
    slots = send.shape[0]
    hit = (lax.broadcasted_iota(jnp.int32, (tiles, rows), 0) == owner_row[...]).astype(BF)
    before = (lax.broadcasted_iota(jnp.int32, (rows, rows), 0)
              < lax.broadcasted_iota(jnp.int32, (rows, rows), 1)).astype(BF)
    earlier = mxu(hit, before)
    rank = jnp.sum(earlier * hit.astype(F32), axis=0, keepdims=True)
    slot = owner_row[...] * cap + rank.astype(jnp.int32)
    place = (lax.broadcasted_iota(jnp.int32, (slots, rows), 0) == slot).astype(BF)

    hit_c = (lax.broadcasted_iota(jnp.int32, (rows, tiles), 1) == owner_col[...]).astype(BF)
    before_c = (lax.broadcasted_iota(jnp.int32, (rows, rows), 1)
                < lax.broadcasted_iota(jnp.int32, (rows, rows), 0)).astype(BF)
    rank_c = jnp.sum(mxu(before_c, hit_c) * hit_c.astype(F32), axis=1, keepdims=True)
    slot_out[...] = owner_col[...] * cap + rank_c.astype(jnp.int32)

    used = (lax.broadcasted_iota(jnp.int32, (1, rows), 1) < count[0]).astype(F32)
    row_weight = used * qc_row[...].astype(F32)
    terms = mxu(jac[...], dep[...] * weight[...], ((1,), (1,)), lax.Precision.HIGHEST) * row_weight
    lat = cell_row[...] // lon_size
    lon = cell_row[...] - lat * lon_size
    wide = lax.broadcasted_iota(jnp.int32, (LANES, rows), 0)
    terms = jnp.concatenate([terms, jnp.zeros((LANES - terms.shape[0], rows), F32)], axis=0)
    terms = jnp.where(wide == channels, row_weight, terms)
    terms = jnp.where(wide == channels + 1, lat.astype(F32), terms)
    terms = jnp.where(wide == channels + 2, lon.astype(F32), terms)
    send[...] = mxu(place, terms.astype(BF), ((1,), (1,))).astype(BF)


def turned(got, channels, padded):
    flat = got[...].astype(F32)
    turn = flat.T
    lat_row = turn[channels + 1 : channels + 2].astype(jnp.int32)
    lon_row = turn[channels + 2 : channels + 3].astype(jnp.int32)
    lat_col = flat[:, channels + 1 : channels + 2].astype(jnp.int32)
    lon_col = flat[:, channels + 2 : channels + 3].astype(jnp.int32)
    keep = lax.broadcasted_iota(jnp.int32, (padded, turn.shape[1]), 0) <= channels
    return jnp.where(keep, turn[:padded], 0.0), lat_row, lon_row, lat_col, lon_col


def edge_kernel(channels, height, breadth, got, north, south, west, east):
    padded = north.shape[1]
    slots = got.shape[0]
    turn, lat_row, lon_row, lat, lon = turned(got, channels, padded)
    values = turn.astype(BF)
    col_hot = (lax.broadcasted_iota(jnp.int32, (slots, breadth), 1) == lon).astype(BF)
    for out, first in ((north, 0), (south, height - HALO)):
        lhs = jnp.concatenate(
            [values * (lat_row == first + k).astype(F32).astype(BF) for k in range(HALO)], axis=0)
        out[:HALO] = mxu(lhs, col_hot).reshape(HALO, padded, breadth).astype(BF)
    at_west, at_east = lon < HALO, lon >= breadth - HALO
    at_north, at_south = lat < HALO, lat >= height - HALO
    col_west, col_east = HALO + lon, lon - (breadth - HALO)

    def place(mask, row, col, lanes):
        target = jnp.where(mask, row * SIDE + col, -1)
        hot = (lax.broadcasted_iota(jnp.int32, (slots, lanes), 1) == target).astype(BF)
        return mxu(values, hot).astype(BF)

    west[...] = place(at_west, lat + HALO, col_west, west.shape[1])
    east[...] = place(at_east, lat + HALO, col_east, east.shape[1])
    below = (height + HALO) % (LANES // SIDE)
    for out, mask, row in ((north, at_north, lat + below), (south, at_south, lat - (height - HALO))):
        out[HALO, :, :LANES] = place(mask & at_west, row, col_west, LANES)
        out[HALO, :, LANES : 2 * LANES] = place(mask & at_east, row, col_east, LANES)


def grid_kernel(channels, got, out):
    height, padded, breadth = out.shape
    slots = got.shape[0]
    turn, lat_row, _, _, lon = turned(got, channels, padded)
    values = turn.astype(BF)
    col_hot = (lax.broadcasted_iota(jnp.int32, (slots, breadth), 1) == lon).astype(BF)
    step = 8

    def body(block, _):
        lhs = jnp.concatenate(
            [values * (lat_row == block * step + k).astype(F32).astype(BF) for k in range(step)], axis=0)
        out[pl.ds(block * step, step)] = mxu(lhs, col_hot).reshape(step, padded, breadth)
        return 0

    lax.fori_loop(0, height // step, body, 0)


def strip_kernel(inner, north, south, west, east):
    height, hidden, breadth = inner.shape
    per = LANES // SIDE
    lane = lax.broadcasted_iota(jnp.int32, (hidden, LANES), 1)
    for block in range(west.shape[1] // LANES):
        left = jnp.zeros((hidden, LANES), F32)
        right = jnp.zeros((hidden, LANES), F32)
        for k in range(per):
            i = block * per + k
            if i < HALO:
                row = north[i]
            elif i < HALO + height:
                row = inner[i - HALO]
            elif i < height + 2 * HALO:
                row = south[i - HALO - height]
            else:
                break
            row = row.astype(F32)
            mine = (lane >= k * SIDE) & (lane < (k + 1) * SIDE)
            left = jnp.where(mine, pltpu.roll(row[:, :LANES], (k * SIDE + HALO) % LANES, 1), left)
            right = jnp.where(mine, pltpu.roll(row[:, breadth - LANES :], (k * SIDE + HALO) % LANES, 1), right)
        west[:, block * LANES : (block + 1) * LANES] = left.astype(BF)
        east[:, block * LANES : (block + 1) * LANES] = right.astype(BF)


def join_kernel(height, west, east, from_north, from_south, slope_west, slope_east, to_west, to_east):
    padded, strip = west.shape
    last = (height + HALO) * SIDE // LANES
    for k, own, slope, out in ((0, west, slope_west, to_west), (1, east, slope_east, to_east)):
        corner = pl.ds(k * LANES, LANES)
        for block in range(strip // LANES):
            part = pl.ds(block * LANES, LANES)
            q = own[:, part]
            if block == 0:
                q = q + from_north[HALO, :, corner]
            if block == last:
                q = q + from_south[HALO, :, corner]
            out[:padded, part] = q
        out[padded:] = slope[...]


def main_kernel(channels, hidden, cap, flags, got, inner, north, south, from_east, from_west, slope_inner,
                slope_north, slope_south, w_n, w_m, p_t, p_j, g3, first_out, second_out, reply,
                field, slope, ga, xb, vec, hi, y1, found):
    height, padded, breadth = inner.shape
    wide = breadth + LANES
    ext = height + 2 * HALO
    per = LANES // SIDE

    def is_in(i):
        above = (i >= HALO) | (flags[0] == 1)
        below = (i < height + HALO) | (flags[1] == 1)
        return (above & below).astype(F32)

    def join(parts):
        return jnp.concatenate(parts, axis=1)

    def part(x, k):
        return x[:, k * wide : (k + 1) * wide]

    def pull(i, ys):
        u = mxu(p_t[...], join([y.astype(BF) for y in ys]))
        for k in range(len(ys)):
            ga[i + k] = (slope[i + k].astype(F32) * part(u, k)).astype(BF)

    lane = lax.broadcasted_iota(jnp.int32, (padded + hidden, LANES), 1)
    from_the_west = lane % SIDE < HALO

    def begin(i, mains, slopes, count):
        at = pl.ds(pl.multiple_of(i // per * LANES, LANES), LANES)
        both = jnp.where(from_the_west, from_west[:, at].astype(F32), from_east[:, at].astype(F32))
        ys = []
        for k in range(count):
            shift = 2 * LANES - ((i % per) + k) * SIDE - HALO
            edge = pltpu.roll(both, shift % LANES, 1)
            y = join([mains[k].astype(F32), edge[:padded]])
            field[i + k] = y
            slope[i + k] = join([slopes[k], edge[padded:].astype(BF)])
            ys.append(y)
        pull(i, ys)

    begin(0, [north[k] for k in range(HALO)], [slope_north[k] for k in range(HALO)], HALO)
    begin(HALO + height, [south[k] for k in range(HALO)], [slope_south[k] for k in range(HALO)], HALO)

    def middle(n, _):
        i = n * HALO
        begin(i + HALO, [inner[i + k] for k in range(HALO)], [slope_inner[i + k] for k in range(HALO)], HALO)
        return 0

    lax.fori_loop(0, height // HALO, middle, 0)

    def spread(i, ys):
        o = mxu(w_n[...], join([ga[pl.ds(i + k - 1, 3)].reshape(3 * hidden, wide) for k in range(len(ys))]))
        out = []
        for k, y in enumerate(ys):
            p = part(o, k)
            out.append(y + p[padded : 2 * padded] + pltpu.roll(p[:padded], wide - 1, 1)
                       + pltpu.roll(p[2 * padded :], 1, 1))
        return out

    def tangent(i, vs):
        o = mxu(w_m[...], join([xb[pl.ds(i + k - 1, 3)].reshape(3 * padded, wide) for k in range(len(vs))]))
        acts = []
        for k in range(len(vs)):
            p = part(o, k)
            h = (p[hidden : 2 * hidden] + pltpu.roll(p[:hidden], 1, 1)
                 + pltpu.roll(p[2 * hidden :], wide - 1, 1))
            acts.append((slope[i + k].astype(F32) * h).astype(BF))
        back = mxu(p_j[...], join(acts))
        return [v + part(back, k) for k, v in enumerate(vs)]

    def gram_of(s):
        s_hi = s.astype(BF)
        s_lo = (s - s_hi.astype(F32)).astype(BF)
        return mxu(g3[...], jnp.concatenate([s_hi, s_hi, s_lo], axis=0))

    def loop(first, last, size, body):
        assert (last - first) % size == 0

        def step(n, _):
            body(first + n * size)
            return 0

        lax.fori_loop(0, (last - first) // size, step, 0)

    def n_first(i):
        for k, v in enumerate(spread(i, [field[i + k] for k in range(G[0])])):
            vec[i + k] = v
            xb[i + k] = (v * is_in(i + k)).astype(BF)

    loop(1, ext - 1, G[0], n_first)

    def m_first(i):
        ss = tangent(i, [vec[i + k] for k in range(G[1])])
        gs = gram_of(join(ss))
        ys = []
        for k, s in enumerate(ss):
            y = field[i + k][channels : channels + 1] * part(gs, k)
            hi[i + k, :padded] = s[:, :breadth].astype(BF)
            y1[i + k] = y
            ys.append(y)
        pull(i, ys)

    loop(2, ext - 2, G[1], m_first)

    def keep_first(i):
        first_out[i] = vec[i + HALO][:, :breadth]

    loop(0, height, 1, keep_first)

    def n_second(i):
        for k, v in enumerate(spread(i, [y1[i + k] for k in range(G[2])])):
            vec[i + k] = v
            xb[i + k] = (v * is_in(i + k)).astype(BF)

    loop(3, ext - 3, G[2], n_second)

    def m_second(i):
        vs = [vec[i + k] for k in range(G[3])]
        for k, s in enumerate(tangent(i, vs)):
            second_out[i + k - HALO] = vs[k][:, :breadth]
            hi[i + k, padded:] = s[:, :breadth].astype(BF)

    loop(HALO, ext - HALO, G[3], m_second)

    turn, lat_row, lon_row, _, _ = turned(got, channels, padded)
    slots = got.shape[0]
    piece = 256
    for c in range(slots // piece):
        here = slice(c * piece, (c + 1) * piece)
        col_hot = (lax.broadcasted_iota(jnp.int32, (breadth, piece), 0) == lon_row[:, here]).astype(BF)
        found[:, here] = jnp.zeros((2 * padded, piece), F32)

        def gather(i, col_hot=col_hot, here=here):
            out = mxu(hi[pl.ds(i, G[4])].reshape(G[4] * 2 * padded, breadth), col_hot)
            total = found[:, here]
            for k in range(G[4]):
                mine = (lat_row[:, here] == i + k - HALO)
                total = total + jnp.where(mine, out[k * 2 * padded : (k + 1) * 2 * padded], 0.0)
            found[:, here] = total

        loop(HALO, ext - HALO, G[4], gather)

    row0, row1 = found[:padded], found[padded:]
    weight = turn[channels : channels + 1]
    curved0 = gram_of(row0) * weight
    curved1 = gram_of(row1) * weight
    real = lax.broadcasted_iota(jnp.int32, (padded, slots), 0) < channels
    first = jnp.where(real, turn, 0.0)

    def total(x):
        return jnp.sum(jnp.sum(x, axis=0, keepdims=True), axis=1, keepdims=True)

    sums = (total(first * row0), total(curved0 * row0), total(curved0 * row1), total(curved1 * row1))
    lane = lax.broadcasted_iota(jnp.int32, (1, LANES), 1)
    pieces = jnp.zeros((1, LANES), F32)
    for number, value in enumerate(sums):
        for third, piece in enumerate(split3(value)):
            pieces = jnp.where(lane == channels + 3 + 3 * number + third, piece.astype(F32), pieces)
    filler = jnp.zeros((LANES - padded, slots), F32)
    turned0 = jnp.concatenate([row0, filler], axis=0).T
    turned1 = jnp.concatenate([row1, filler], axis=0).T
    leads = lax.broadcasted_iota(jnp.int32, (slots, LANES), 0)
    is_lead = leads % cap == 0
    lanes = lax.broadcasted_iota(jnp.int32, (slots, LANES), 1)
    reply[:, :LANES] = jnp.where(lanes < channels, turned0, jnp.where(is_lead, pieces, 0.0)).astype(BF)
    reply[:, LANES:] = turned1.astype(BF)


def scalars(reply, channels):
    sums = jnp.sum(reply[:, :LANES].astype(F32), axis=0, keepdims=True)

    def value(number):
        at = channels + 3 + 3 * number
        return sums[:, at : at + 1] + sums[:, at + 1 : at + 2] + sums[:, at + 2 : at + 3]

    a00, a01, a11, d11 = (value(n) for n in range(4))
    step0 = a00 / (a00 + a01)
    keep = 1.0 - step0
    norm1 = keep * keep * a00 - 2.0 * step0 * keep * a01 + step0 * step0 * a11
    c0 = keep + norm1 / a00
    c1 = -step0
    curve = (c0 * c0 * (a00 + a01) + 2.0 * c0 * c1 * (a01 + a11) + c1 * c1 * (a11 + d11))
    step1 = norm1 / curve
    return step0 + step1 * c0, step1 * c1


def final_kernel(channels, back, slot, dep, jac, first, second, increment, departures):
    slots = back.shape[0]
    rows = dep.shape[0]
    a, b = scalars(back, channels)
    place = (lax.broadcasted_iota(jnp.int32, (rows, slots), 1) == slot[...]).astype(BF)
    own = mxu(place, back[...])
    padded = jac.shape[0]
    state = a * own[:, :padded] + b * own[:, LANES : LANES + padded]
    departures[...] = dep[...] - mxu(state, jac[...], precision=lax.Precision.HIGHEST)
    increment[...] = a[None] * first[...] + b[None] * second[...]


def shift2(x, by_lat, by_lon):
    n_lat, n_lon = lax.axis_size("lat"), lax.axis_size("lon")
    pairs = [(i * n_lon + j, (i + by_lat) * n_lon + (j + by_lon) % n_lon)
             for i in range(n_lat) for j in range(n_lon) if 0 <= i + by_lat < n_lat]
    return lax.ppermute(x, ("lat", "lon"), pairs)


def on_device(departure_in, obs_owner, obs_cell, obs_count, qc_mask, channel_weight, jacobian,
              conv_taps, projection, slope):
    channels, hidden = projection.shape
    height, breadth = slope.shape[1], slope.shape[2]
    tiles = lax.axis_size(("lat", "lon"))
    rows, radiances = departure_in.shape
    cap = max(2, 3 * rows // (2 * tiles))
    slots = tiles * cap
    padded = -(-channels // 16) * 16
    wide = breadth + LANES
    ext = height + 2 * HALO
    strip = -(-(ext * SIDE) // LANES) * LANES
    more = padded - channels

    def shape(dims, kind=F32):
        return jax.ShapeDtypeStruct(dims, kind)

    jac = jnp.pad(jacobian, ((0, more), (0, 0)))
    weight = channel_weight[None, :]
    send, slot = call(
        functools.partial(pack_kernel, tiles, cap, breadth, channels),
        (shape((slots, LANES), BF), shape((rows, 1), jnp.int32)),
        (obs_count, departure_in, obs_owner.reshape(1, rows), obs_owner, obs_cell[None, :],
         qc_mask[None, :], weight, jac),
        smem=1,
    )

    def swap(x):
        return lax.all_to_all(x.reshape(tiles, cap, -1), ("lat", "lon"), split_axis=0, concat_axis=0,
                              tiled=True).reshape(slots, -1)

    got = swap(send)

    gram = jnp.dot(jac * weight, jac.T, precision=lax.Precision.HIGHEST)
    gram_hi = gram.astype(BF)
    gram_lo = (gram - gram_hi.astype(F32)).astype(BF)
    g3 = jnp.concatenate([gram_hi, gram_lo, gram_hi], axis=1)
    taps = jnp.pad(conv_taps, ((0, 0), (0, 0), (0, more))).reshape(3, 3, hidden, padded)
    w_m = jnp.transpose(taps, (1, 2, 0, 3)).reshape(3 * hidden, 3 * padded)
    w_n = jnp.transpose(taps[::-1], (1, 3, 0, 2)).reshape(3 * padded, 3 * hidden)
    p_j = jnp.pad(projection, ((0, more), (0, 0)))
    p_t = p_j.T

    slope_inner = jnp.transpose(slope, (1, 0, 2))
    slope_north = shift2(slope_inner[-HALO:], 1, 0)
    slope_south = shift2(slope_inner[:HALO], -1, 0)
    slope_west, slope_east = call(strip_kernel, (shape((hidden, strip), BF),) * 2,
                                  (slope_inner, slope_north, slope_south))

    edge = (HALO + 1, padded, breadth)
    north, south, west, east = call(
        functools.partial(edge_kernel, channels, height, breadth),
        (shape(edge, BF),) * 2 + (shape((padded, strip), BF),) * 2,
        (got,),
    )
    from_south = shift2(north, -1, 0)
    from_north = shift2(south, 1, 0)
    to_west, to_east = call(
        functools.partial(join_kernel, height),
        (shape((padded + hidden, strip), BF),) * 2,
        (west, east, from_north, from_south, slope_west, slope_east),
    )
    from_east = shift2(to_west, 0, -1)
    from_west = shift2(to_east, 0, 1)
    inner = call(functools.partial(grid_kernel, channels), shape((height, padded, breadth)), (got,))

    at = lax.axis_index("lat")
    flags = jnp.stack([at > 0, at < lax.axis_size("lat") - 1]).astype(jnp.int32)
    first, second, reply = call(
        functools.partial(main_kernel, channels, hidden, cap),
        (shape((height, padded, breadth)),) * 2 + (shape((slots, 2 * LANES), BF),),
        (flags, got, inner, from_north, from_south, from_east, from_west, slope_inner, slope_north,
         slope_south, w_n, w_m, p_t, p_j, g3),
        scratch=[
            pltpu.VMEM((ext, padded, wide), F32),
            pltpu.VMEM((ext, hidden, wide), BF),
            pltpu.VMEM((ext, hidden, wide), BF),
            pltpu.VMEM((ext, padded, wide), BF),
            pltpu.VMEM((ext, padded, wide), F32),
            pltpu.VMEM((ext, 2 * padded, breadth), BF),
            pltpu.VMEM((ext, padded, wide), F32),
            pltpu.VMEM((2 * padded, slots), F32),
        ],
        smem=1,
        vmem=120,
    )
    back = swap(reply)
    first = jnp.transpose(first, (1, 0, 2))[:channels]
    second = jnp.transpose(second, (1, 0, 2))[:channels]
    return call(
        functools.partial(final_kernel, channels),
        (shape((channels, height, breadth)), shape((rows, radiances))),
        (back, slot, departure_in, jac, first, second),
    )


def solution(mesh):
    placed = (
        P(("lat", "lon"), None),
        P(("lat", "lon"), None),
        P(("lat", "lon")),
        P(("lat", "lon")),
        P(("lat", "lon")),
        P(),
        P(),
        P(),
        P(),
        P(None, "lat", "lon"),
    )
    return jax.shard_map(
        on_device,
        mesh=mesh,
        in_specs=placed,
        out_specs=(P(None, "lat", "lon"), P(("lat", "lon"), None)),
        check_vma=False,
    )
```

```python
import functools

import jax
import jax.numpy as jnp
import numpy as np
from jax import lax
from jax.experimental import pallas as pl
from jax.experimental.pallas import tpu as pltpu
from jax.sharding import PartitionSpec as P

ITERS = 2
HALO = 4
LANES = 128
SIDE = 2 * HALO
BF = jnp.bfloat16
F32 = jnp.float32
INTERPRET = False
G = (9, 13, 10, 12, 16)


def mxu(a, b, dims=((1,), (0,)), precision=None):
    return lax.dot_general(a, b, (dims, ((), ())), precision=precision, preferred_element_type=F32)


def call(kernel, outs, args, scratch=(), smem=0, vmem=24, unread=0, staged=False, away=()):
    def space(i, x):
        if i < smem:
            return pl.BlockSpec(memory_space=pltpu.SMEM)
        if i >= len(args) - unread:
            return pl.BlockSpec(memory_space=pl.ANY)
        if staged:
            return pl.BlockSpec(x.shape, lambda _: (0,) * x.ndim)
        return pl.BlockSpec(memory_space=pltpu.VMEM)

    leaves, tree = jax.tree.flatten(outs)
    out_specs = [pl.BlockSpec(memory_space=pl.ANY if i in away else pltpu.VMEM) for i in range(len(leaves))]
    return pl.pallas_call(
        kernel,
        out_shape=outs,
        grid=(1,) if staged else (),
        in_specs=[space(i, x) for i, x in enumerate(args)],
        out_specs=jax.tree.unflatten(tree, out_specs),
        scratch_shapes=scratch,
        interpret=INTERPRET,
        compiler_params=pltpu.CompilerParams(vmem_limit_bytes=vmem * 2**20 // 2),
    )(*args)


def split3(x):
    hi = x.astype(BF)
    rest = x - hi.astype(F32)
    mid = rest.astype(BF)
    return hi, mid, (rest - mid.astype(F32)).astype(BF)


def pack_kernel(tiles, cap, lon_size, channels, count, dep, owner_row, cell_row, qc_row,
                weight, jac, send, slot_out):
    rows = dep.shape[0]
    slots = send.shape[0]
    hit = (lax.broadcasted_iota(jnp.int32, (tiles, rows), 0) == owner_row[...]).astype(BF)
    before = (lax.broadcasted_iota(jnp.int32, (rows, rows), 0)
              < lax.broadcasted_iota(jnp.int32, (rows, rows), 1)).astype(BF)
    earlier = mxu(hit, before)
    rank = jnp.sum(earlier * hit.astype(F32), axis=0, keepdims=True)
    slot = owner_row[...] * cap + rank.astype(jnp.int32)
    slot_out[...] = slot
    place = (lax.broadcasted_iota(jnp.int32, (slots, rows), 0) == slot).astype(BF)

    used = (lax.broadcasted_iota(jnp.int32, (1, rows), 1) < count[0]).astype(F32)
    row_weight = used * qc_row[...].astype(F32)
    terms = mxu(jac[...], dep[...] * weight[...], ((1,), (1,)), lax.Precision.HIGHEST) * row_weight
    lat = cell_row[...] // lon_size
    lon = cell_row[...] - lat * lon_size
    wide = lax.broadcasted_iota(jnp.int32, (LANES, rows), 0)
    terms = jnp.concatenate([terms, jnp.zeros((LANES - channels, rows), F32)], axis=0)
    terms = jnp.where(wide == channels, row_weight, terms)
    terms = jnp.where(wide == channels + 1, lat.astype(F32), terms)
    terms = jnp.where(wide == channels + 2, lon.astype(F32), terms)
    send[...] = mxu(place, terms.astype(BF), ((1,), (1,))).astype(BF)


def weights_kernel(taps, projection, jac, weight, w_m, w_n, p_t, p_j, g3):
    _, hidden, channels = taps.shape
    padded = p_j.shape[0]

    def shifted(rows, columns, by):
        return (lax.broadcasted_iota(jnp.int32, (rows, columns), 0) + by
                == lax.broadcasted_iota(jnp.int32, (rows, columns), 1)).astype(BF)

    wider = shifted(channels, padded, 0)
    for b in range(3):
        total_m, total_n = 0.0, 0.0
        for a in range(3):
            tap = taps[3 * a + b]
            total_m = total_m + mxu(tap, shifted(channels, 3 * padded, a * padded))
            turned_tap = mxu(wider, tap, ((0,), (1,))).astype(BF)
            total_n = total_n + mxu(turned_tap, shifted(hidden, 3 * hidden, (2 - a) * hidden))
        w_m[b * hidden : (b + 1) * hidden] = total_m.astype(BF)
        w_n[b * padded : (b + 1) * padded] = total_n.astype(BF)
    p_j[...] = mxu(wider, projection[...], ((0,), (0,))).astype(BF)
    p_t[...] = mxu(projection[...], wider, ((0,), (0,))).astype(BF)
    tall = jnp.concatenate([jac[...], jnp.zeros((padded - channels, jac.shape[1]), F32)], axis=0)
    gram = mxu(tall * weight[...], tall, ((1,), (1,)), lax.Precision.HIGHEST)
    hi = gram.astype(BF)
    lo = (gram - hi.astype(F32)).astype(BF)
    total = 0.0
    for k, value in enumerate((hi, lo, hi)):
        total = total + mxu(value, shifted(padded, 3 * padded, k * padded))
    g3[...] = total.astype(BF)


def turned(got, channels, padded):
    flat = got[...].astype(F32)
    turn = flat.T
    lat_row = turn[channels + 1 : channels + 2].astype(jnp.int32)
    lon_row = turn[channels + 2 : channels + 3].astype(jnp.int32)
    lat_col = flat[:, channels + 1 : channels + 2].astype(jnp.int32)
    lon_col = flat[:, channels + 2 : channels + 3].astype(jnp.int32)
    keep = lax.broadcasted_iota(jnp.int32, (padded, turn.shape[1]), 0) <= channels
    return jnp.where(keep, turn[:padded], 0.0), lat_row, lon_row, lat_col, lon_col


def edge_kernel(channels, height, breadth, got, north, south, west, east):
    padded = north.shape[1]
    slots = got.shape[0]
    turn, lat_row, lon_row, lat, lon = turned(got, channels, padded)
    values = turn.astype(BF)
    col_hot = (lax.broadcasted_iota(jnp.int32, (slots, breadth), 1) == lon).astype(BF)
    for out, first in ((north, 0), (south, height - HALO)):
        lhs = jnp.concatenate(
            [values * (lat_row == first + k).astype(F32).astype(BF) for k in range(HALO)], axis=0)
        out[:HALO] = mxu(lhs, col_hot).reshape(HALO, padded, breadth).astype(BF)
    at_west, at_east = lon < HALO, lon >= breadth - HALO
    at_north, at_south = lat < HALO, lat >= height - HALO
    col_west, col_east = HALO + lon, lon - (breadth - HALO)

    def place(mask, row, col, lanes):
        target = jnp.where(mask, row * SIDE + col, -1)
        hot = (lax.broadcasted_iota(jnp.int32, (slots, lanes), 1) == target).astype(BF)
        return mxu(values, hot).astype(BF)

    west[...] = place(at_west, lat + HALO, col_west, west.shape[1])
    east[...] = place(at_east, lat + HALO, col_east, east.shape[1])
    below = (height + HALO) % (LANES // SIDE)
    for out, mask, row in ((north, at_north, lat + below), (south, at_south, lat - (height - HALO))):
        out[HALO, :, :LANES] = place(mask & at_west, row, col_west, LANES)
        out[HALO, :, LANES : 2 * LANES] = place(mask & at_east, row, col_east, LANES)


def grid_kernel(channels, got, out):
    height, padded, breadth = out.shape
    slots = got.shape[0]
    turn, lat_row, _, _, lon = turned(got, channels, padded)
    values = turn.astype(BF)
    col_hot = (lax.broadcasted_iota(jnp.int32, (slots, breadth), 1) == lon).astype(BF)
    step = 8

    def body(block, _):
        lhs = jnp.concatenate(
            [values * (lat_row == block * step + k).astype(F32).astype(BF) for k in range(step)], axis=0)
        out[pl.ds(block * step, step)] = mxu(lhs, col_hot).reshape(step, padded, breadth)
        return 0

    lax.fori_loop(0, height // step, body, 0)


def strip_kernel(inner, north, south, west, east):
    height, hidden, breadth = inner.shape
    per = LANES // SIDE
    lane = lax.broadcasted_iota(jnp.int32, (hidden, LANES), 1)
    for block in range(west.shape[1] // LANES):
        left = jnp.zeros((hidden, LANES), F32)
        right = jnp.zeros((hidden, LANES), F32)
        for k in range(per):
            i = block * per + k
            if i < HALO:
                row = north[i]
            elif i < HALO + height:
                row = inner[i - HALO]
            elif i < height + 2 * HALO:
                row = south[i - HALO - height]
            else:
                break
            row = row.astype(F32)
            mine = (lane >= k * SIDE) & (lane < (k + 1) * SIDE)
            left = jnp.where(mine, pltpu.roll(row[:, :LANES], (k * SIDE + HALO) % LANES, 1), left)
            right = jnp.where(mine, pltpu.roll(row[:, breadth - LANES :], (k * SIDE + HALO) % LANES, 1), right)
        west[:, block * LANES : (block + 1) * LANES] = left.astype(BF)
        east[:, block * LANES : (block + 1) * LANES] = right.astype(BF)


def join_kernel(height, west, east, from_north, from_south, slope_west, slope_east, _inner, _weights,
                to_west, to_east):
    padded, strip = west.shape
    last = (height + HALO) * SIDE // LANES
    for k, own, slope, out in ((0, west, slope_west, to_west), (1, east, slope_east, to_east)):
        corner = pl.ds(k * LANES, LANES)
        for block in range(strip // LANES):
            part = pl.ds(block * LANES, LANES)
            q = own[:, part]
            if block == 0:
                q = q + from_north[HALO, :, corner]
            if block == last:
                q = q + from_south[HALO, :, corner]
            out[:padded, part] = q
        out[padded:] = slope[...]


def main_kernel(channels, hidden, cap, flags, got, inner, north, south, from_east, from_west, slope_inner,
                slope_north, slope_south, w_n, w_m, p_t, p_j, g3, first_out, second_out, reply,
                field, slope, ga, xb, vec, hi, found):
    height, padded, breadth = inner.shape
    wide = breadth + LANES
    ext = height + 2 * HALO
    per = LANES // SIDE

    def is_in(i):
        above = (i >= HALO) | (flags[0] == 1)
        below = (i < height + HALO) | (flags[1] == 1)
        return (above & below).astype(F32)

    def join(parts):
        return jnp.concatenate(parts, axis=1)

    def part(x, k):
        return x[:, k * wide : (k + 1) * wide]

    def pull(i, ys):
        u = mxu(p_t[...], join([y.astype(BF) for y in ys]))
        for k in range(len(ys)):
            ga[i + k] = (slope[i + k].astype(F32) * part(u, k)).astype(BF)

    lane = lax.broadcasted_iota(jnp.int32, (padded + hidden, LANES), 1)
    from_the_west = lane % SIDE < HALO

    def begin(i, mains, slopes, count):
        at = pl.ds(pl.multiple_of(i // per * LANES, LANES), LANES)
        both = jnp.where(from_the_west, from_west[:, at].astype(F32), from_east[:, at].astype(F32))
        ys = []
        for k in range(count):
            shift = 2 * LANES - ((i % per) + k) * SIDE - HALO
            edge = pltpu.roll(both, shift % LANES, 1)
            y = join([mains[k].astype(F32), edge[:padded]])
            field[i + k] = y
            slope[i + k] = join([slopes[k], edge[padded:].astype(BF)])
            ys.append(y)
        pull(i, ys)

    begin(0, [north[k] for k in range(HALO)], [slope_north[k] for k in range(HALO)], HALO)
    begin(HALO + height, [south[k] for k in range(HALO)], [slope_south[k] for k in range(HALO)], HALO)

    def middle(n, _):
        i = n * HALO
        begin(i + HALO, [inner[i + k] for k in range(HALO)], [slope_inner[i + k] for k in range(HALO)], HALO)
        return 0

    lax.fori_loop(0, height // HALO, middle, 0)

    def spread(i, ys):
        o = mxu(w_n[...], join([ga[pl.ds(i + k - 1, 3)].reshape(3 * hidden, wide) for k in range(len(ys))]))
        out = []
        for k, y in enumerate(ys):
            p = part(o, k)
            out.append(y + p[padded : 2 * padded] + pltpu.roll(p[:padded], wide - 1, 1)
                       + pltpu.roll(p[2 * padded :], 1, 1))
        return out

    def tangent(i, vs):
        o = mxu(w_m[...], join([xb[pl.ds(i + k - 1, 3)].reshape(3 * padded, wide) for k in range(len(vs))]))
        acts = []
        for k in range(len(vs)):
            p = part(o, k)
            h = (p[hidden : 2 * hidden] + pltpu.roll(p[:hidden], 1, 1)
                 + pltpu.roll(p[2 * hidden :], wide - 1, 1))
            acts.append((slope[i + k].astype(F32) * h).astype(BF))
        back = mxu(p_j[...], join(acts))
        return [v + part(back, k) for k, v in enumerate(vs)]

    def gram_of(s):
        s_hi = s.astype(BF)
        s_lo = (s - s_hi.astype(F32)).astype(BF)
        return mxu(g3[...], jnp.concatenate([s_hi, s_hi, s_lo], axis=0))

    def loop(first, last, size, body):
        assert (last - first) % size == 0

        def step(n, _):
            body(first + n * size)
            return 0

        lax.fori_loop(0, (last - first) // size, step, 0)

    def n_first(i):
        for k, v in enumerate(spread(i, [field[i + k] for k in range(G[0])])):
            vec[i + k] = v
            xb[i + k] = (v * is_in(i + k)).astype(BF)

    loop(1, ext - 1, G[0], n_first)

    def m_first(i):
        ss = tangent(i, [vec[i + k] for k in range(G[1])])
        gs = gram_of(join(ss))
        ys = []
        for k, s in enumerate(ss):
            y = field[i + k][channels : channels + 1] * part(gs, k)
            hi[i + k, :padded] = s[:, :breadth].astype(BF)
            field[i + k] = y
            ys.append(y)
        pull(i, ys)

    loop(2, ext - 2, G[1], m_first)

    def keep_first(i):
        first_out[i] = vec[i + HALO][:, :breadth]

    loop(0, height, 1, keep_first)

    def n_second(i):
        for k, v in enumerate(spread(i, [field[i + k] for k in range(G[2])])):
            vec[i + k] = v
            xb[i + k] = (v * is_in(i + k)).astype(BF)

    loop(3, ext - 3, G[2], n_second)

    def m_second(i):
        vs = [vec[i + k] for k in range(G[3])]
        for k, s in enumerate(tangent(i, vs)):
            second_out[i + k - HALO] = vs[k][:, :breadth]
            hi[i + k, padded:] = s[:, :breadth].astype(BF)

    loop(HALO, ext - HALO, G[3], m_second)

    turn, lat_row, lon_row, _, _ = turned(got, channels, padded)
    slots = got.shape[0]
    piece = 256
    for c in range(slots // piece):
        here = slice(c * piece, (c + 1) * piece)
        col_hot = (lax.broadcasted_iota(jnp.int32, (breadth, piece), 0) == lon_row[:, here]).astype(BF)
        found[:, here] = jnp.zeros((2 * padded, piece), F32)

        def gather(i, col_hot=col_hot, here=here):
            out = mxu(hi[pl.ds(i, G[4])].reshape(G[4] * 2 * padded, breadth), col_hot)
            total = found[:, here]
            for k in range(G[4]):
                mine = (lat_row[:, here] == i + k - HALO)
                total = total + jnp.where(mine, out[k * 2 * padded : (k + 1) * 2 * padded], 0.0)
            found[:, here] = total

        loop(HALO, ext - HALO, G[4], gather)

    row0, row1 = found[:padded], found[padded:]
    weight = turn[channels : channels + 1]
    curved0 = gram_of(row0) * weight
    curved1 = gram_of(row1) * weight
    real = lax.broadcasted_iota(jnp.int32, (padded, slots), 0) < channels
    first = jnp.where(real, turn, 0.0)

    def total(x):
        return jnp.sum(jnp.sum(x, axis=0, keepdims=True), axis=1, keepdims=True)

    sums = (total(first * row0), total(curved0 * row0), total(curved0 * row1), total(curved1 * row1))
    lane = lax.broadcasted_iota(jnp.int32, (1, LANES), 1)
    pieces = jnp.zeros((1, LANES), F32)
    for number, value in enumerate(sums):
        for third, piece in enumerate(split3(value)):
            pieces = jnp.where(lane == channels + 3 + 3 * number + third, piece.astype(F32), pieces)
    filler = jnp.zeros((LANES - padded, slots), F32)
    turned0 = jnp.concatenate([row0, filler], axis=0).T
    turned1 = jnp.concatenate([row1, filler], axis=0).T
    leads = lax.broadcasted_iota(jnp.int32, (slots, LANES), 0)
    is_lead = leads % cap == 0
    lanes = lax.broadcasted_iota(jnp.int32, (slots, LANES), 1)
    reply[:, :LANES] = jnp.where(lanes < channels, turned0, jnp.where(is_lead, pieces, 0.0)).astype(BF)
    reply[:, LANES:] = turned1.astype(BF)


def scalars(reply, channels):
    sums = jnp.sum(reply[:, :LANES].astype(F32), axis=0, keepdims=True)

    def value(number):
        at = channels + 3 + 3 * number
        return sums[:, at : at + 1] + sums[:, at + 1 : at + 2] + sums[:, at + 2 : at + 3]

    a00, a01, a11, d11 = (value(n) for n in range(4))
    step0 = a00 / (a00 + a01)
    keep = 1.0 - step0
    norm1 = keep * keep * a00 - 2.0 * step0 * keep * a01 + step0 * step0 * a11
    c0 = keep + norm1 / a00
    c1 = -step0
    curve = (c0 * c0 * (a00 + a01) + 2.0 * c0 * c1 * (a01 + a11) + c1 * c1 * (a11 + d11))
    step1 = norm1 / curve
    return step0 + step1 * c0, step1 * c1


def final_kernel(channels, back, slot, dep, jac, first, second, increment, departures, mixed, sems):
    slots = back.shape[0]
    rows = dep.shape[0]
    height = mixed.shape[0]
    a, b = scalars(back, channels)

    def copy(i):
        return pltpu.make_async_copy(mixed.at[i], increment.at[:, i], sems.at[i])

    for i in range(height):
        mixed[i] = a * first[i, :channels] + b * second[i, :channels]
        copy(i).start()
    slots_of = lax.broadcasted_iota(jnp.int32, (slots, rows), 0)
    place = (slots_of == slot[...]).astype(BF)
    own = mxu(place, back[...], ((0,), (0,)))
    state = a * own[:, :channels] + b * own[:, LANES : LANES + channels]
    departures[...] = dep[...] - mxu(state, jac[...], precision=lax.Precision.HIGHEST)
    for i in range(height):
        copy(i).wait()


def shift2(x, by_lat, by_lon):
    n_lat, n_lon = lax.axis_size("lat"), lax.axis_size("lon")
    pairs = [(i * n_lon + j, (i + by_lat) * n_lon + (j + by_lon) % n_lon)
             for i in range(n_lat) for j in range(n_lon) if 0 <= i + by_lat < n_lat]
    return lax.ppermute(x, ("lat", "lon"), pairs)


def on_device(departure_in, obs_owner, obs_cell, obs_count, qc_mask, channel_weight, jacobian,
              conv_taps, projection, slope):
    channels, hidden = projection.shape
    height, breadth = slope.shape[1], slope.shape[2]
    tiles = lax.axis_size(("lat", "lon"))
    rows, radiances = departure_in.shape
    cap = max(2, 3 * rows // (2 * tiles))
    slots = tiles * cap
    padded = -(-channels // 16) * 16
    wide = breadth + LANES
    ext = height + 2 * HALO
    strip = -(-(ext * SIDE) // LANES) * LANES

    def shape(dims, kind=F32):
        return jax.ShapeDtypeStruct(dims, kind)

    weight = channel_weight[None, :]
    send, slot = call(
        functools.partial(pack_kernel, tiles, cap, breadth, channels),
        (shape((slots, LANES), BF), shape((1, rows), jnp.int32)),
        (obs_count, departure_in, obs_owner.reshape(1, rows), obs_cell[None, :],
         qc_mask[None, :], weight, jacobian),
        smem=1,
        staged=True,
    )

    def swap(x):
        return lax.all_to_all(x.reshape(tiles, cap, -1), ("lat", "lon"), split_axis=0, concat_axis=0,
                              tiled=True).reshape(slots, -1)

    got = swap(send)

    w_m, w_n, p_t, p_j, g3 = call(
        weights_kernel,
        (shape((3 * hidden, 3 * padded), BF), shape((3 * padded, 3 * hidden), BF), shape((hidden, padded), BF),
         shape((padded, hidden), BF), shape((padded, 3 * padded), BF)),
        (conv_taps, projection, jacobian, weight),
        staged=True,
    )

    slope_inner = jnp.transpose(slope, (1, 0, 2))
    slope_north = shift2(slope_inner[-HALO:], 1, 0)
    slope_south = shift2(slope_inner[:HALO], -1, 0)
    slope_west, slope_east = call(strip_kernel, (shape((hidden, strip), BF),) * 2,
                                  (slope_inner, slope_north, slope_south))

    edge = (HALO + 1, padded, breadth)
    north, south, west, east = call(
        functools.partial(edge_kernel, channels, height, breadth),
        (shape(edge, BF),) * 2 + (shape((padded, strip), BF),) * 2,
        (got,),
    )
    from_south = shift2(north, -1, 0)
    from_north = shift2(south, 1, 0)
    inner = call(functools.partial(grid_kernel, channels), shape((height, padded, breadth)), (got,))
    to_west, to_east = call(
        functools.partial(join_kernel, height),
        (shape((padded + hidden, strip), BF),) * 2,
        (west, east, from_north, from_south, slope_west, slope_east, inner, w_m),
        unread=2,
    )
    from_east = shift2(to_west, 0, -1)
    from_west = shift2(to_east, 0, 1)

    at = lax.axis_index("lat")
    flags = jnp.stack([at > 0, at < lax.axis_size("lat") - 1]).astype(jnp.int32)
    first, second, reply = call(
        functools.partial(main_kernel, channels, hidden, cap),
        (shape((height, padded, breadth)),) * 2 + (shape((slots, 2 * LANES), BF),),
        (flags, got, inner, from_north, from_south, from_east, from_west, slope_inner, slope_north,
         slope_south, w_n, w_m, p_t, p_j, g3),
        scratch=[
            pltpu.VMEM((ext, padded, wide), F32),
            pltpu.VMEM((ext, hidden, wide), BF),
            pltpu.VMEM((ext, hidden, wide), BF),
            pltpu.VMEM((ext, padded, wide), BF),
            pltpu.VMEM((ext, padded, wide), F32),
            pltpu.VMEM((ext, 2 * padded, breadth), BF),
            pltpu.VMEM((2 * padded, slots), F32),
        ],
        smem=1,
        vmem=64,
    )
    back = swap(reply)
    return call(
        functools.partial(final_kernel, channels),
        (shape((channels, height, breadth)), shape((rows, radiances))),
        (back, slot, departure_in, jacobian, first, second),
        scratch=[pltpu.VMEM((height, channels, breadth), F32), pltpu.SemaphoreType.DMA((height,))],
        away=(0,),
        vmem=32,
    )


def solution(mesh):
    placed = (
        P(("lat", "lon"), None),
        P(("lat", "lon"), None),
        P(("lat", "lon")),
        P(("lat", "lon")),
        P(("lat", "lon")),
        P(),
        P(),
        P(),
        P(),
        P(None, "lat", "lon"),
    )
    return jax.shard_map(
        on_device,
        mesh=mesh,
        in_specs=placed,
        out_specs=(P(None, "lat", "lon"), P(("lat", "lon"), None)),
        check_vma=False,
    )
```

```python
import functools

import jax
import jax.numpy as jnp
import numpy as np
from jax import lax
from jax.experimental import pallas as pl
from jax.experimental.pallas import tpu as pltpu
from jax.sharding import PartitionSpec as P

ITERS = 2
HALO = 4
LANES = 128
SIDE = 2 * HALO
BF = jnp.bfloat16
F32 = jnp.float32
INTERPRET = False
G = (9, 13, 10, 12, 16)


def mxu(a, b, dims=((1,), (0,)), precision=None):
    return lax.dot_general(a, b, (dims, ((), ())), precision=precision, preferred_element_type=F32)


def call(kernel, outs, args, scratch=(), smem=0, vmem=24, unread=0, staged=False, away=()):
    def space(i, x):
        if i < smem:
            return pl.BlockSpec(memory_space=pltpu.SMEM)
        if i >= len(args) - unread:
            return pl.BlockSpec(memory_space=pltpu.HBM if scratch else pl.ANY)
        if staged:
            return pl.BlockSpec(x.shape, lambda _: (0,) * x.ndim)
        return pl.BlockSpec(memory_space=pltpu.VMEM)

    leaves, tree = jax.tree.flatten(outs)
    out_specs = [pl.BlockSpec(memory_space=pl.ANY if i in away else pltpu.VMEM) for i in range(len(leaves))]
    return pl.pallas_call(
        kernel,
        out_shape=outs,
        grid=(1,) if staged else (),
        in_specs=[space(i, x) for i, x in enumerate(args)],
        out_specs=jax.tree.unflatten(tree, out_specs),
        scratch_shapes=scratch,
        interpret=INTERPRET,
        compiler_params=pltpu.CompilerParams(vmem_limit_bytes=vmem * 2**20 // 2),
    )(*args)


def split3(x):
    hi = x.astype(BF)
    rest = x - hi.astype(F32)
    mid = rest.astype(BF)
    return hi, mid, (rest - mid.astype(F32)).astype(BF)


def pack_kernel(tiles, cap, lon_size, channels, count, *refs):
    sources, (send, slot_out), held, sems = refs[:6], refs[6:8], refs[8:14], refs[14]
    copies = [pltpu.make_async_copy(src, dst, sems.at[k]) for k, (src, dst) in enumerate(zip(sources, held))]
    for copy in copies:
        copy.start()
    for copy in copies:
        copy.wait()
    dep, owner_row, cell_row, qc_row, weight, jac = held
    rows = dep.shape[0]
    slots = send.shape[0]
    hit = (lax.broadcasted_iota(jnp.int32, (tiles, rows), 0) == owner_row[...]).astype(BF)
    before = (lax.broadcasted_iota(jnp.int32, (rows, rows), 0)
              < lax.broadcasted_iota(jnp.int32, (rows, rows), 1)).astype(BF)
    earlier = mxu(hit, before)
    rank = jnp.sum(earlier * hit.astype(F32), axis=0, keepdims=True)
    slot = owner_row[...] * cap + rank.astype(jnp.int32)
    slot_out[...] = slot
    place = (lax.broadcasted_iota(jnp.int32, (slots, rows), 0) == slot).astype(BF)

    used = (lax.broadcasted_iota(jnp.int32, (1, rows), 1) < count[0]).astype(F32)
    row_weight = used * qc_row[...].astype(F32)
    terms = mxu(jac[...], dep[...] * weight[...], ((1,), (1,)), lax.Precision.HIGHEST) * row_weight
    lat = cell_row[...] // lon_size
    lon = cell_row[...] - lat * lon_size
    wide = lax.broadcasted_iota(jnp.int32, (LANES, rows), 0)
    terms = jnp.concatenate([terms, jnp.zeros((LANES - channels, rows), F32)], axis=0)
    terms = jnp.where(wide == channels, row_weight, terms)
    terms = jnp.where(wide == channels + 1, lat.astype(F32), terms)
    terms = jnp.where(wide == channels + 2, lon.astype(F32), terms)
    send[...] = mxu(place, terms.astype(BF), ((1,), (1,))).astype(BF)


def weights_kernel(taps, projection, jac, weight, w_m, w_n, p_t, p_j, g3):
    _, hidden, channels = taps.shape
    padded = p_j.shape[0]

    def shifted(rows, columns, by):
        return (lax.broadcasted_iota(jnp.int32, (rows, columns), 0) + by
                == lax.broadcasted_iota(jnp.int32, (rows, columns), 1)).astype(BF)

    wider = shifted(channels, padded, 0)
    for b in range(3):
        total_m, total_n = 0.0, 0.0
        for a in range(3):
            tap = taps[3 * a + b]
            total_m = total_m + mxu(tap, shifted(channels, 3 * padded, a * padded))
            turned_tap = mxu(wider, tap, ((0,), (1,))).astype(BF)
            total_n = total_n + mxu(turned_tap, shifted(hidden, 3 * hidden, (2 - a) * hidden))
        w_m[b * hidden : (b + 1) * hidden] = total_m.astype(BF)
        w_n[b * padded : (b + 1) * padded] = total_n.astype(BF)
    p_j[...] = mxu(wider, projection[...], ((0,), (0,))).astype(BF)
    p_t[...] = mxu(projection[...], wider, ((0,), (0,))).astype(BF)
    tall = jnp.concatenate([jac[...], jnp.zeros((padded - channels, jac.shape[1]), F32)], axis=0)
    gram = mxu(tall * weight[...], tall, ((1,), (1,)), lax.Precision.HIGHEST)
    hi = gram.astype(BF)
    lo = (gram - hi.astype(F32)).astype(BF)
    total = 0.0
    for k, value in enumerate((hi, lo, hi)):
        total = total + mxu(value, shifted(padded, 3 * padded, k * padded))
    g3[...] = total.astype(BF)


def turned(got, channels, padded):
    flat = got[...].astype(F32)
    turn = flat.T
    lat_row = turn[channels + 1 : channels + 2].astype(jnp.int32)
    lon_row = turn[channels + 2 : channels + 3].astype(jnp.int32)
    lat_col = flat[:, channels + 1 : channels + 2].astype(jnp.int32)
    lon_col = flat[:, channels + 2 : channels + 3].astype(jnp.int32)
    keep = lax.broadcasted_iota(jnp.int32, (padded, turn.shape[1]), 0) <= channels
    return jnp.where(keep, turn[:padded], 0.0), lat_row, lon_row, lat_col, lon_col


def edge_kernel(channels, height, got, _slope_north, _slope_south, north, south):
    tall, breadth = north.shape
    trim = tall // HALO
    slots = got.shape[0]
    turn, lat_row, _, _, lon = turned(got, channels, -(-trim // 16) * 16)
    values = turn.astype(BF)
    col_hot = (lax.broadcasted_iota(jnp.int32, (slots, breadth), 1) == lon).astype(BF)
    for out, first in ((north, 0), (south, height - HALO)):
        lhs = jnp.concatenate(
            [values * (lat_row == first + k).astype(F32).astype(BF) for k in range(HALO)], axis=0)
        rows = mxu(lhs, col_hot).reshape(HALO, values.shape[0], breadth)[:, :trim]
        out[...] = rows.reshape(tall, breadth).astype(BF)


def rows_of(message, padded):
    tall, breadth = message.shape
    rows = message[...].astype(F32).reshape(HALO, tall // HALO, breadth)
    return jnp.concatenate([rows, jnp.zeros((HALO, padded - tall // HALO, breadth), F32)], axis=1)


def side_kernel(channels, height, breadth, got, west, east):
    padded, strip = west.shape
    slots = got.shape[0]
    turn, _, _, lat, lon = turned(got, channels, padded)
    values = turn.astype(BF)
    for out, mask, col in (
        (west, lon < HALO, HALO + lon),
        (east, lon >= breadth - HALO, lon - (breadth - HALO)),
    ):
        target = jnp.where(mask, (lat + HALO) * SIDE + col, -1)
        hot = (lax.broadcasted_iota(jnp.int32, (slots, strip), 1) == target).astype(BF)
        out[...] = mxu(values, hot).astype(BF)


def grid_kernel(channels, got, out):
    height, padded, breadth = out.shape
    slots = got.shape[0]
    turn, lat_row, _, _, lon = turned(got, channels, padded)
    values = turn.astype(BF)
    col_hot = (lax.broadcasted_iota(jnp.int32, (slots, breadth), 1) == lon).astype(BF)
    step = 8

    def body(block, _):
        lhs = jnp.concatenate(
            [values * (lat_row == block * step + k).astype(F32).astype(BF) for k in range(step)], axis=0)
        out[pl.ds(block * step, step)] = mxu(lhs, col_hot).reshape(step, padded, breadth)
        return 0

    lax.fori_loop(0, height // step, body, 0)


def to_strip(rows, base, block):
    per = LANES // SIDE
    shape = (rows[0].shape[0], LANES)
    lane = lax.broadcasted_iota(jnp.int32, shape, 1)
    left, right = jnp.zeros(shape, F32), jnp.zeros(shape, F32)
    for k, row in enumerate(rows):
        at = base + k - block * per
        if not 0 <= at < per:
            continue
        row = row.astype(F32)
        by = (at * SIDE + HALO) % LANES
        mine = (lane >= at * SIDE) & (lane < (at + 1) * SIDE)
        left = jnp.where(mine & (lane % SIDE >= HALO), pltpu.roll(row[:, :LANES], by, 1), left)
        right = jnp.where(mine & (lane % SIDE < HALO), pltpu.roll(row[:, -LANES:], by, 1), right)
    return left, right


def strip_kernel(inner, north, south, west, east):
    height = inner.shape[0]
    rows = [north[k] for k in range(HALO)] + [inner[k] for k in range(height)] + [south[k] for k in range(HALO)]
    for block in range(west.shape[1] // LANES):
        left, right = to_strip(rows, 0, block)
        west[:, block * LANES : (block + 1) * LANES] = left.astype(BF)
        east[:, block * LANES : (block + 1) * LANES] = right.astype(BF)


def join_kernel(height, west, east, from_north, from_south, slope_west, slope_east, _token, to_west, to_east):
    padded, strip = west.shape
    last = (height + HALO) * SIDE // LANES
    above, below = rows_of(from_north, padded), rows_of(from_south, padded)
    above = to_strip([above[k] for k in range(HALO)], 0, 0)
    below = to_strip([below[k] for k in range(HALO)], HALO + height, last)
    for k, own, slope, out in ((0, west, slope_west, to_west), (1, east, slope_east, to_east)):
        for block in range(strip // LANES):
            part = pl.ds(block * LANES, LANES)
            q = own[:, part]
            if block == 0:
                q = q + above[k].astype(BF)
            if block == last:
                q = q + below[k].astype(BF)
            out[:padded, part] = q
        out[padded:] = slope[...]


def main_kernel(channels, hidden, cap, flags, got, inner, north, south, from_east, from_west, slope_inner,
                slope_north, slope_south, w_n, w_m, p_t, p_j, g3, first_out, second_out, reply,
                field, slope, ga, xb, vec, hi, found):
    height, padded, breadth = inner.shape
    wide = breadth + LANES
    ext = height + 2 * HALO
    per = LANES // SIDE

    def is_in(i):
        above = (i >= HALO) | (flags[0] == 1)
        below = (i < height + HALO) | (flags[1] == 1)
        return (above & below).astype(F32)

    def join(parts):
        return jnp.concatenate(parts, axis=1)

    def part(x, k):
        return x[:, k * wide : (k + 1) * wide]

    def pull(i, ys):
        u = mxu(p_t[...], join([y.astype(BF) for y in ys]))
        for k in range(len(ys)):
            ga[i + k] = (slope[i + k].astype(F32) * part(u, k)).astype(BF)

    lane = lax.broadcasted_iota(jnp.int32, (padded + hidden, LANES), 1)
    from_the_west = lane % SIDE < HALO

    def begin(i, mains, slopes, count):
        at = pl.ds(pl.multiple_of(i // per * LANES, LANES), LANES)
        both = jnp.where(from_the_west, from_west[:, at].astype(F32), from_east[:, at].astype(F32))
        ys = []
        for k in range(count):
            shift = 2 * LANES - ((i % per) + k) * SIDE - HALO
            edge = pltpu.roll(both, shift % LANES, 1)
            y = join([mains[k].astype(F32), edge[:padded]])
            field[i + k] = y
            slope[i + k] = join([slopes[k], edge[padded:].astype(BF)])
            ys.append(y)
        pull(i, ys)

    above, below = rows_of(north, padded), rows_of(south, padded)
    begin(0, [above[k] for k in range(HALO)], [slope_north[k] for k in range(HALO)], HALO)
    begin(HALO + height, [below[k] for k in range(HALO)], [slope_south[k] for k in range(HALO)], HALO)

    def middle(n, _):
        i = n * HALO
        begin(i + HALO, [inner[i + k] for k in range(HALO)], [slope_inner[i + k] for k in range(HALO)], HALO)
        return 0

    lax.fori_loop(0, height // HALO, middle, 0)

    def spread(i, ys):
        o = mxu(w_n[...], join([ga[pl.ds(i + k - 1, 3)].reshape(3 * hidden, wide) for k in range(len(ys))]))
        out = []
        for k, y in enumerate(ys):
            p = part(o, k)
            out.append(y + p[padded : 2 * padded] + pltpu.roll(p[:padded], wide - 1, 1)
                       + pltpu.roll(p[2 * padded :], 1, 1))
        return out

    def tangent(i, vs):
        o = mxu(w_m[...], join([xb[pl.ds(i + k - 1, 3)].reshape(3 * padded, wide) for k in range(len(vs))]))
        acts = []
        for k in range(len(vs)):
            p = part(o, k)
            h = (p[hidden : 2 * hidden] + pltpu.roll(p[:hidden], 1, 1)
                 + pltpu.roll(p[2 * hidden :], wide - 1, 1))
            acts.append((slope[i + k].astype(F32) * h).astype(BF))
        back = mxu(p_j[...], join(acts))
        return [v + part(back, k) for k, v in enumerate(vs)]

    def gram_of(s):
        s_hi = s.astype(BF)
        s_lo = (s - s_hi.astype(F32)).astype(BF)
        return mxu(g3[...], jnp.concatenate([s_hi, s_hi, s_lo], axis=0))

    def loop(first, last, size, body):
        assert (last - first) % size == 0

        def step(n, _):
            body(first + n * size)
            return 0

        lax.fori_loop(0, (last - first) // size, step, 0)

    def n_first(i):
        for k, v in enumerate(spread(i, [field[i + k] for k in range(G[0])])):
            vec[i + k] = v
            xb[i + k] = (v * is_in(i + k)).astype(BF)

    loop(1, ext - 1, G[0], n_first)

    def m_first(i):
        ss = tangent(i, [vec[i + k] for k in range(G[1])])
        gs = gram_of(join(ss))
        ys = []
        for k, s in enumerate(ss):
            y = field[i + k][channels : channels + 1] * part(gs, k)
            hi[i + k, :padded] = s[:, :breadth].astype(BF)
            field[i + k] = y
            ys.append(y)
        pull(i, ys)

    loop(2, ext - 2, G[1], m_first)

    def keep_first(i):
        first_out[i] = vec[i + HALO][:, :breadth]

    loop(0, height, 1, keep_first)

    def n_second(i):
        for k, v in enumerate(spread(i, [field[i + k] for k in range(G[2])])):
            vec[i + k] = v
            xb[i + k] = (v * is_in(i + k)).astype(BF)

    loop(3, ext - 3, G[2], n_second)

    def m_second(i):
        vs = [vec[i + k] for k in range(G[3])]
        for k, s in enumerate(tangent(i, vs)):
            second_out[i + k - HALO] = vs[k][:, :breadth]
            hi[i + k, padded:] = s[:, :breadth].astype(BF)

    loop(HALO, ext - HALO, G[3], m_second)

    turn, lat_row, lon_row, _, _ = turned(got, channels, padded)
    slots = got.shape[0]
    piece = 256
    for c in range(slots // piece):
        here = slice(c * piece, (c + 1) * piece)
        col_hot = (lax.broadcasted_iota(jnp.int32, (breadth, piece), 0) == lon_row[:, here]).astype(BF)
        found[:, here] = jnp.zeros((2 * padded, piece), F32)

        def gather(i, col_hot=col_hot, here=here):
            out = mxu(hi[pl.ds(i, G[4])].reshape(G[4] * 2 * padded, breadth), col_hot)
            total = found[:, here]
            for k in range(G[4]):
                mine = (lat_row[:, here] == i + k - HALO)
                total = total + jnp.where(mine, out[k * 2 * padded : (k + 1) * 2 * padded], 0.0)
            found[:, here] = total

        loop(HALO, ext - HALO, G[4], gather)

    row0, row1 = found[:padded], found[padded:]
    weight = turn[channels : channels + 1]
    curved0 = gram_of(row0) * weight
    curved1 = gram_of(row1) * weight
    real = lax.broadcasted_iota(jnp.int32, (padded, slots), 0) < channels
    first = jnp.where(real, turn, 0.0)

    def total(x):
        return jnp.sum(jnp.sum(x, axis=0, keepdims=True), axis=1, keepdims=True)

    sums = (total(first * row0), total(curved0 * row0), total(curved0 * row1), total(curved1 * row1))
    lane = lax.broadcasted_iota(jnp.int32, (1, LANES), 1)
    pieces = jnp.zeros((1, LANES), F32)
    for number, value in enumerate(sums):
        for third, piece in enumerate(split3(value)):
            pieces = jnp.where(lane == channels + 3 + 3 * number + third, piece.astype(F32), pieces)
    filler = jnp.zeros((LANES - padded, slots), F32)
    turned0 = jnp.concatenate([row0, filler], axis=0).T
    turned1 = jnp.concatenate([row1, filler], axis=0).T
    leads = lax.broadcasted_iota(jnp.int32, (slots, LANES), 0)
    is_lead = leads % cap == 0
    lanes = lax.broadcasted_iota(jnp.int32, (slots, LANES), 1)
    reply[:, :LANES] = jnp.where(lanes < channels, turned0, jnp.where(is_lead, pieces, 0.0)).astype(BF)
    reply[:, LANES:] = turned1.astype(BF)


def scalars(reply, channels):
    sums = jnp.sum(reply[:, :LANES].astype(F32), axis=0, keepdims=True)

    def value(number):
        at = channels + 3 + 3 * number
        return sums[:, at : at + 1] + sums[:, at + 1 : at + 2] + sums[:, at + 2 : at + 3]

    a00, a01, a11, d11 = (value(n) for n in range(4))
    step0 = a00 / (a00 + a01)
    keep = 1.0 - step0
    norm1 = keep * keep * a00 - 2.0 * step0 * keep * a01 + step0 * step0 * a11
    c0 = keep + norm1 / a00
    c1 = -step0
    curve = (c0 * c0 * (a00 + a01) + 2.0 * c0 * c1 * (a01 + a11) + c1 * c1 * (a11 + d11))
    step1 = norm1 / curve
    return step0 + step1 * c0, step1 * c1


def final_kernel(channels, back, slot, dep, jac, first, second, increment, departures, mixed, sems):
    slots = back.shape[0]
    rows = dep.shape[0]
    height = mixed.shape[0]
    a, b = scalars(back, channels)

    def copy(i):
        return pltpu.make_async_copy(mixed.at[i], increment.at[:, i], sems.at[i])

    for i in range(height):
        mixed[i] = a * first[i, :channels] + b * second[i, :channels]
        copy(i).start()
    slots_of = lax.broadcasted_iota(jnp.int32, (slots, rows), 0)
    place = (slots_of == slot[...]).astype(BF)
    own = mxu(place, back[...], ((0,), (0,)))
    state = a * own[:, :channels] + b * own[:, LANES : LANES + channels]
    departures[...] = dep[...] - mxu(state, jac[...], precision=lax.Precision.HIGHEST)
    for i in range(height):
        copy(i).wait()


def shift2(x, by_lat, by_lon):
    n_lat, n_lon = lax.axis_size("lat"), lax.axis_size("lon")
    pairs = [(i * n_lon + j, (i + by_lat) * n_lon + (j + by_lon) % n_lon)
             for i in range(n_lat) for j in range(n_lon) if 0 <= i + by_lat < n_lat]
    return lax.ppermute(x, ("lat", "lon"), pairs)


def on_device(departure_in, obs_owner, obs_cell, obs_count, qc_mask, channel_weight, jacobian,
              conv_taps, projection, slope):
    channels, hidden = projection.shape
    height, breadth = slope.shape[1], slope.shape[2]
    tiles = lax.axis_size(("lat", "lon"))
    rows, radiances = departure_in.shape
    cap = max(2, 3 * rows // (2 * tiles))
    slots = tiles * cap
    padded = -(-channels // 16) * 16
    wide = breadth + LANES
    ext = height + 2 * HALO
    strip = -(-(ext * SIDE) // LANES) * LANES

    def shape(dims, kind=F32):
        return jax.ShapeDtypeStruct(dims, kind)

    weight = channel_weight[None, :]
    inputs = (departure_in, obs_owner.reshape(1, rows), obs_cell[None, :], qc_mask[None, :], weight, jacobian)
    send, slot = call(
        functools.partial(pack_kernel, tiles, cap, breadth, channels),
        (shape((slots, LANES), BF), shape((1, rows), jnp.int32)),
        (obs_count,) + inputs,
        scratch=[pltpu.VMEM(x.shape, x.dtype) for x in inputs] + [pltpu.SemaphoreType.DMA((len(inputs),))],
        smem=1,
        unread=len(inputs),
    )

    def swap(x):
        return lax.all_to_all(x.reshape(tiles, cap, -1), ("lat", "lon"), split_axis=0, concat_axis=0,
                              tiled=True).reshape(slots, -1)

    got = swap(send)

    w_m, w_n, p_t, p_j, g3 = call(
        weights_kernel,
        (shape((3 * hidden, 3 * padded), BF), shape((3 * padded, 3 * hidden), BF), shape((hidden, padded), BF),
         shape((padded, hidden), BF), shape((padded, 3 * padded), BF)),
        (conv_taps, projection, jacobian, weight),
        staged=True,
    )

    slope_inner = jnp.transpose(slope, (1, 0, 2))
    slope_north = shift2(slope_inner[-HALO:], 1, 0)
    slope_south = shift2(slope_inner[:HALO], -1, 0)
    slope_west, slope_east = call(strip_kernel, (shape((hidden, strip), BF),) * 2,
                                  (slope_inner, slope_north, slope_south))

    trim = -(-(channels + 1) // 8) * 8
    north, south = call(
        functools.partial(edge_kernel, channels, height),
        (shape((HALO * trim, breadth), BF),) * 2,
        (got, slope_north, slope_south),
        unread=2,
    )
    from_south = shift2(north, -1, 0)
    from_north = shift2(south, 1, 0)
    west, east = call(
        functools.partial(side_kernel, channels, height, breadth), (shape((padded, strip), BF),) * 2, (got,))
    to_west, to_east = call(
        functools.partial(join_kernel, height),
        (shape((padded + hidden, strip), BF),) * 2,
        (west, east, from_north, from_south, slope_west, slope_east, p_t),
        unread=1,
    )
    from_east = shift2(to_west, 0, -1)
    from_west = shift2(to_east, 0, 1)
    inner = call(functools.partial(grid_kernel, channels), shape((height, padded, breadth)), (got,))

    at = lax.axis_index("lat")
    flags = jnp.stack([at > 0, at < lax.axis_size("lat") - 1]).astype(jnp.int32)
    first, second, reply = call(
        functools.partial(main_kernel, channels, hidden, cap),
        (shape((height, padded, breadth)),) * 2 + (shape((slots, 2 * LANES), BF),),
        (flags, got, inner, from_north, from_south, from_east, from_west, slope_inner, slope_north,
         slope_south, w_n, w_m, p_t, p_j, g3),
        scratch=[
            pltpu.VMEM((ext, padded, wide), F32),
            pltpu.VMEM((ext, hidden, wide), BF),
            pltpu.VMEM((ext, hidden, wide), BF),
            pltpu.VMEM((ext, padded, wide), BF),
            pltpu.VMEM((ext, padded, wide), F32),
            pltpu.VMEM((ext, 2 * padded, breadth), BF),
            pltpu.VMEM((2 * padded, slots), F32),
        ],
        smem=1,
        vmem=64,
    )
    back = swap(reply)
    return call(
        functools.partial(final_kernel, channels),
        (shape((channels, height, breadth)), shape((rows, radiances))),
        (back, slot, departure_in, jacobian, first, second),
        scratch=[pltpu.VMEM((height, channels, breadth), F32), pltpu.SemaphoreType.DMA((height,))],
        away=(0,),
        vmem=32,
    )


def solution(mesh):
    placed = (
        P(("lat", "lon"), None),
        P(("lat", "lon"), None),
        P(("lat", "lon")),
        P(("lat", "lon")),
        P(("lat", "lon")),
        P(),
        P(),
        P(),
        P(),
        P(None, "lat", "lon"),
    )
    return jax.shard_map(
        on_device,
        mesh=mesh,
        in_specs=placed,
        out_specs=(P(None, "lat", "lon"), P(("lat", "lon"), None)),
        check_vma=False,
    )
```

```python
import functools

import jax
import jax.numpy as jnp
import numpy as np
from jax import lax
from jax.experimental import pallas as pl
from jax.experimental.pallas import tpu as pltpu
from jax.sharding import PartitionSpec as P

ITERS = 2
HALO = 4
LANES = 128
SIDE = 2 * HALO
BF = jnp.bfloat16
F32 = jnp.float32
INTERPRET = False
G = (18, 26, 25, 24, 24, 24)


def mxu(a, b, dims=((1,), (0,)), precision=None):
    return lax.dot_general(a, b, (dims, ((), ())), precision=precision, preferred_element_type=F32)


def call(kernel, outs, args, scratch=(), smem=0, vmem=24, unread=0, staged=False, away=()):
    def space(i, x):
        if i < smem:
            return pl.BlockSpec(memory_space=pltpu.SMEM)
        if i >= len(args) - unread:
            return pl.BlockSpec(memory_space=pltpu.HBM if scratch else pl.ANY)
        if staged:
            return pl.BlockSpec(x.shape, lambda _: (0,) * x.ndim)
        return pl.BlockSpec(memory_space=pltpu.VMEM)

    leaves, tree = jax.tree.flatten(outs)
    out_specs = [pl.BlockSpec(memory_space=pl.ANY if i in away else pltpu.VMEM) for i in range(len(leaves))]
    return pl.pallas_call(
        kernel,
        out_shape=outs,
        grid=(1,) if staged else (),
        in_specs=[space(i, x) for i, x in enumerate(args)],
        out_specs=jax.tree.unflatten(tree, out_specs),
        scratch_shapes=scratch,
        interpret=INTERPRET,
        compiler_params=pltpu.CompilerParams(vmem_limit_bytes=vmem * 2**20 // 2),
    )(*args)


def split3(x):
    hi = x.astype(BF)
    rest = x - hi.astype(F32)
    mid = rest.astype(BF)
    return hi, mid, (rest - mid.astype(F32)).astype(BF)


def pack_kernel(tiles, cap, lon_size, channels, count, *refs):
    sources, (send, slot_out), held, sems = refs[:6], refs[6:8], refs[8:14], refs[14]
    copies = [pltpu.make_async_copy(src, dst, sems.at[k]) for k, (src, dst) in enumerate(zip(sources, held))]
    for copy in copies:
        copy.start()
    for copy in copies:
        copy.wait()
    dep, owner_row, cell_row, qc_row, weight, jac = held
    rows = dep.shape[0]
    slots = send.shape[0]
    hit = (lax.broadcasted_iota(jnp.int32, (tiles, rows), 0) == owner_row[...]).astype(BF)
    before = (lax.broadcasted_iota(jnp.int32, (rows, rows), 0)
              < lax.broadcasted_iota(jnp.int32, (rows, rows), 1)).astype(BF)
    earlier = mxu(hit, before)
    rank = jnp.sum(earlier * hit.astype(F32), axis=0, keepdims=True)
    slot = owner_row[...] * cap + rank.astype(jnp.int32)
    slot_out[...] = slot
    place = (lax.broadcasted_iota(jnp.int32, (slots, rows), 0) == slot).astype(BF)

    used = (lax.broadcasted_iota(jnp.int32, (1, rows), 1) < count[0]).astype(F32)
    row_weight = used * qc_row[...].astype(F32)
    terms = mxu(jac[...], dep[...] * weight[...], ((1,), (1,)), lax.Precision.HIGHEST) * row_weight
    lat = cell_row[...] // lon_size
    lon = cell_row[...] - lat * lon_size
    wide = lax.broadcasted_iota(jnp.int32, (LANES, rows), 0)
    terms = jnp.concatenate([terms, jnp.zeros((LANES - channels, rows), F32)], axis=0)
    terms = jnp.where(wide == channels, row_weight, terms)
    terms = jnp.where(wide == channels + 1, lat.astype(F32), terms)
    terms = jnp.where(wide == channels + 2, lon.astype(F32), terms)
    send[...] = mxu(place, terms.astype(BF), ((1,), (1,))).astype(BF)


def weights_kernel(taps, projection, jac, weight, w_m, w_n, p_t, p_j, g3):
    _, hidden, channels = taps.shape
    trim, padded = p_j.shape[0], p_t.shape[1]

    def shifted(rows, columns, by):
        return (lax.broadcasted_iota(jnp.int32, (rows, columns), 0) + by
                == lax.broadcasted_iota(jnp.int32, (rows, columns), 1)).astype(BF)

    wider, fuller = shifted(channels, padded, 0), shifted(channels, trim, 0)
    for b in range(3):
        total_m, total_n = 0.0, 0.0
        for a in range(3):
            tap = taps[3 * a + b]
            total_m = total_m + mxu(tap, shifted(channels, 3 * padded, a * padded))
            turned_tap = mxu(fuller, tap, ((0,), (1,))).astype(BF)
            total_n = total_n + mxu(turned_tap, shifted(hidden, 3 * hidden, (2 - a) * hidden))
        w_m[b * hidden : (b + 1) * hidden] = total_m.astype(BF)
        w_n[b * trim : (b + 1) * trim] = total_n.astype(BF)
    p_j[...] = mxu(fuller, projection[...], ((0,), (0,))).astype(BF)
    p_t[...] = mxu(projection[...], wider, ((0,), (0,))).astype(BF)
    tall = jnp.concatenate([jac[...], jnp.zeros((padded - channels, jac.shape[1]), F32)], axis=0)
    gram = mxu(tall * weight[...], tall, ((1,), (1,)), lax.Precision.HIGHEST)
    hi = gram.astype(BF)
    lo = (gram - hi.astype(F32)).astype(BF)
    total = 0.0
    for k, value in enumerate((hi, lo, hi)):
        total = total + mxu(value, shifted(padded, 3 * padded, k * padded))
    g3[...] = total[:trim].astype(BF)


def turned(got, channels, padded):
    flat = got[...].astype(F32)
    turn = flat.T
    lat_row = turn[channels + 1 : channels + 2].astype(jnp.int32)
    lon_row = turn[channels + 2 : channels + 3].astype(jnp.int32)
    lat_col = flat[:, channels + 1 : channels + 2].astype(jnp.int32)
    lon_col = flat[:, channels + 2 : channels + 3].astype(jnp.int32)
    keep = lax.broadcasted_iota(jnp.int32, (padded, turn.shape[1]), 0) <= channels
    return jnp.where(keep, turn[:padded], 0.0), lat_row, lon_row, lat_col, lon_col


def edge_kernel(channels, height, got, _slope_north, _slope_south, north, south):
    tall, breadth = north.shape
    trim = tall // HALO
    slots = got.shape[0]
    turn, lat_row, _, _, lon = turned(got, channels, -(-trim // 16) * 16)
    values = turn.astype(BF)
    col_hot = (lax.broadcasted_iota(jnp.int32, (slots, breadth), 1) == lon).astype(BF)
    for out, first in ((north, 0), (south, height - HALO)):
        lhs = jnp.concatenate(
            [values * (lat_row == first + k).astype(F32).astype(BF) for k in range(HALO)], axis=0)
        rows = mxu(lhs, col_hot).reshape(HALO, values.shape[0], breadth)[:, :trim]
        out[...] = rows.reshape(tall, breadth).astype(BF)


def rows_of(message, padded):
    tall, breadth = message.shape
    rows = message[...].astype(F32).reshape(HALO, tall // HALO, breadth)
    if padded == tall // HALO:
        return rows
    return jnp.concatenate([rows, jnp.zeros((HALO, padded - tall // HALO, breadth), F32)], axis=1)


def side_kernel(channels, height, breadth, got, west, east):
    padded, strip = west.shape
    slots = got.shape[0]
    turn, _, _, lat, lon = turned(got, channels, padded)
    values = turn.astype(BF)
    for out, mask, col in (
        (west, lon < HALO, HALO + lon),
        (east, lon >= breadth - HALO, lon - (breadth - HALO)),
    ):
        target = jnp.where(mask, (lat + HALO) * SIDE + col, -1)
        hot = (lax.broadcasted_iota(jnp.int32, (slots, strip), 1) == target).astype(BF)
        out[...] = mxu(values, hot).astype(BF)


def grid_kernel(channels, got, out):
    height, trim, breadth = out.shape
    padded = -(-trim // 16) * 16
    slots = got.shape[0]
    turn, lat_row, _, _, lon = turned(got, channels, padded)
    values = turn.astype(BF)
    col_hot = (lax.broadcasted_iota(jnp.int32, (slots, breadth), 1) == lon).astype(BF)
    step = 8

    def body(block, _):
        lhs = jnp.concatenate(
            [values * (lat_row == block * step + k).astype(F32).astype(BF) for k in range(step)], axis=0)
        out[pl.ds(block * step, step)] = mxu(lhs, col_hot).reshape(step, padded, breadth)[:, :trim]
        return 0

    lax.fori_loop(0, height // step, body, 0)


def to_strip(rows, base, block):
    per = LANES // SIDE
    shape = (rows[0].shape[0], LANES)
    lane = lax.broadcasted_iota(jnp.int32, shape, 1)
    left, right = jnp.zeros(shape, F32), jnp.zeros(shape, F32)
    for k, row in enumerate(rows):
        at = base + k - block * per
        if not 0 <= at < per:
            continue
        row = row.astype(F32)
        by = (at * SIDE + HALO) % LANES
        mine = (lane >= at * SIDE) & (lane < (at + 1) * SIDE)
        left = jnp.where(mine & (lane % SIDE >= HALO), pltpu.roll(row[:, :LANES], by, 1), left)
        right = jnp.where(mine & (lane % SIDE < HALO), pltpu.roll(row[:, -LANES:], by, 1), right)
    return left, right


def strip_kernel(inner, north, south, west, east):
    height = inner.shape[0]
    rows = [north[k] for k in range(HALO)] + [inner[k] for k in range(height)] + [south[k] for k in range(HALO)]
    for block in range(west.shape[1] // LANES):
        left, right = to_strip(rows, 0, block)
        west[:, block * LANES : (block + 1) * LANES] = left.astype(BF)
        east[:, block * LANES : (block + 1) * LANES] = right.astype(BF)


def join_kernel(height, west, east, from_north, from_south, slope_west, slope_east, _token, to_west, to_east):
    padded, strip = west.shape
    last = (height + HALO) * SIDE // LANES
    above, below = rows_of(from_north, padded), rows_of(from_south, padded)
    above = to_strip([above[k] for k in range(HALO)], 0, 0)
    below = to_strip([below[k] for k in range(HALO)], HALO + height, last)
    for k, own, slope, out in ((0, west, slope_west, to_west), (1, east, slope_east, to_east)):
        for block in range(strip // LANES):
            part = pl.ds(block * LANES, LANES)
            q = own[:, part]
            if block == 0:
                q = q + above[k].astype(BF)
            if block == last:
                q = q + below[k].astype(BF)
            out[:padded, part] = q
        out[padded:] = slope[...]


def main_kernel(channels, hidden, cap, flags, got, inner, north, south, from_east, from_west, slope_inner,
                slope_north, slope_south, w_n, w_m, p_t, p_j, g3, first_out, second_out, reply,
                field, slope, ga, xb, vec, hi, found):
    height, trim, breadth = inner.shape
    padded = xb.shape[1]
    wide = breadth + LANES
    ext = height + 2 * HALO
    per = LANES // SIDE

    def is_in(i):
        above = (i >= HALO) | (flags[0] == 1)
        below = (i < height + HALO) | (flags[1] == 1)
        return (above & below).astype(F32)

    def join(parts):
        return jnp.concatenate(parts, axis=1)

    def part(x, k):
        return x[:, k * wide : (k + 1) * wide]

    def fill(x):
        return jnp.concatenate([x, jnp.zeros((padded - trim, x.shape[1]), F32)], axis=0).astype(BF)

    def pull(i, ys):
        u = mxu(p_t[...], join([fill(y) for y in ys]))
        for k in range(len(ys)):
            ga[i + k] = (slope[i + k].astype(F32) * part(u, k)).astype(BF)

    lane = lax.broadcasted_iota(jnp.int32, (padded + hidden, LANES), 1)
    from_the_west = lane % SIDE < HALO

    def begin(i, mains, slopes):
        ys = []
        for k in range(len(mains)):
            if k % HALO == 0:
                at = pl.ds(pl.multiple_of((i + k) // per * LANES, LANES), LANES)
                both = jnp.where(from_the_west, from_west[:, at].astype(F32), from_east[:, at].astype(F32))
            shift = 2 * LANES - (i + k) % per * SIDE - HALO
            edge = pltpu.roll(both, shift % LANES, 1)
            y = join([mains[k].astype(F32), edge[:trim]])
            field[i + k] = y
            slope[i + k] = join([slopes[k], edge[padded:].astype(BF)])
            ys.append(y)
        pull(i, ys)

    above, below = rows_of(north, trim), rows_of(south, trim)
    begin(0, [above[k] for k in range(HALO)], [slope_north[k] for k in range(HALO)])
    begin(HALO + height, [below[k] for k in range(HALO)], [slope_south[k] for k in range(HALO)])

    def middle(n, _):
        i = n * G[5]
        begin(i + HALO, [inner[i + k] for k in range(G[5])], [slope_inner[i + k] for k in range(G[5])])
        return 0

    lax.fori_loop(0, height // G[5], middle, 0)

    def spread(i, ys):
        o = mxu(w_n[...], join([ga[pl.ds(i + k - 1, 3)].reshape(3 * hidden, wide) for k in range(len(ys))]))
        out = []
        for k, y in enumerate(ys):
            p = part(o, k)
            out.append(y + p[trim : 2 * trim] + pltpu.roll(p[:trim], wide - 1, 1)
                       + pltpu.roll(p[2 * trim :], 1, 1))
        return out

    def tangent(i, vs):
        o = mxu(w_m[...], join([xb[pl.ds(i + k - 1, 3)].reshape(3 * padded, wide) for k in range(len(vs))]))
        acts = []
        for k in range(len(vs)):
            p = part(o, k)
            h = (p[hidden : 2 * hidden] + pltpu.roll(p[:hidden], 1, 1)
                 + pltpu.roll(p[2 * hidden :], wide - 1, 1))
            acts.append((slope[i + k].astype(F32) * h).astype(BF))
        back = mxu(p_j[...], join(acts))
        return [v + part(back, k) for k, v in enumerate(vs)]

    def gram_of(s):
        s_hi = s.astype(BF).astype(F32)
        s_lo = fill(s - s_hi)
        s_hi = fill(s_hi)
        return mxu(g3[...], jnp.concatenate([s_hi, s_hi, s_lo], axis=0))

    def loop(first, last, size, body):
        assert (last - first) % size == 0

        def step(n, _):
            body(first + n * size)
            return 0

        lax.fori_loop(0, (last - first) // size, step, 0)

    def n_first(i):
        for k, v in enumerate(spread(i, [field[i + k] for k in range(G[0])])):
            vec[i + k] = v
            xb[i + k] = fill(v * is_in(i + k))

    loop(1, ext - 1, G[0], n_first)

    def m_first(i):
        ss = tangent(i, [vec[i + k] for k in range(G[1])])
        gs = gram_of(join(ss))
        ys = []
        for k, s in enumerate(ss):
            y = field[i + k][channels : channels + 1] * part(gs, k)
            hi[i + k, :padded] = fill(s[:, :breadth])
            field[i + k] = y
            ys.append(y)
        pull(i, ys)

    loop(2, ext - 2, G[1], m_first)

    def keep_first(i):
        first_out[i] = vec[i + HALO][:, :breadth]

    loop(0, height, 1, keep_first)

    def n_second(i):
        for k, v in enumerate(spread(i, [field[i + k] for k in range(G[2])])):
            vec[i + k] = v
            xb[i + k] = fill(v * is_in(i + k))

    loop(3, ext - 3, G[2], n_second)

    def m_second(i):
        vs = [vec[i + k] for k in range(G[3])]
        for k, s in enumerate(tangent(i, vs)):
            second_out[i + k - HALO] = vs[k][:, :breadth]
            hi[i + k, padded:] = fill(s[:, :breadth])

    loop(HALO, ext - HALO, G[3], m_second)

    turn, lat_row, lon_row, _, _ = turned(got, channels, padded)
    slots = got.shape[0]
    piece = 256
    for c in range(slots // piece):
        here = slice(c * piece, (c + 1) * piece)
        col_hot = (lax.broadcasted_iota(jnp.int32, (breadth, piece), 0) == lon_row[:, here]).astype(BF)
        found[:, here] = jnp.zeros((2 * padded, piece), F32)

        def gather(i, col_hot=col_hot, here=here):
            out = mxu(hi[pl.ds(i, G[4])].reshape(G[4] * 2 * padded, breadth), col_hot)
            total = found[:, here]
            for k in range(G[4]):
                mine = (lat_row[:, here] == i + k - HALO)
                total = total + jnp.where(mine, out[k * 2 * padded : (k + 1) * 2 * padded], 0.0)
            found[:, here] = total

        loop(HALO, ext - HALO, G[4], gather)

    row0, row1 = found[:trim], found[padded : padded + trim]
    weight = turn[channels : channels + 1]
    curved0 = gram_of(row0) * weight
    curved1 = gram_of(row1) * weight
    real = lax.broadcasted_iota(jnp.int32, (trim, slots), 0) < channels
    first = jnp.where(real, turn[:trim], 0.0)

    def total(x):
        return jnp.sum(jnp.sum(x, axis=0, keepdims=True), axis=1, keepdims=True)

    sums = (total(first * row0), total(curved0 * row0), total(curved0 * row1), total(curved1 * row1))
    lane = lax.broadcasted_iota(jnp.int32, (1, LANES), 1)
    pieces = jnp.zeros((1, LANES), F32)
    for number, value in enumerate(sums):
        for third, piece in enumerate(split3(value)):
            pieces = jnp.where(lane == channels + 3 + 3 * number + third, piece.astype(F32), pieces)
    filler = jnp.zeros((LANES - trim, slots), F32)
    turned0 = jnp.concatenate([row0, filler], axis=0).T
    turned1 = jnp.concatenate([row1, filler], axis=0).T
    leads = lax.broadcasted_iota(jnp.int32, (slots, LANES), 0)
    is_lead = leads % cap == 0
    lanes = lax.broadcasted_iota(jnp.int32, (slots, LANES), 1)
    reply[:, :LANES] = jnp.where(lanes < channels, turned0, jnp.where(is_lead, pieces, 0.0)).astype(BF)
    reply[:, LANES:] = turned1.astype(BF)


def scalars(reply, channels):
    sums = jnp.sum(reply[:, :LANES].astype(F32), axis=0, keepdims=True)

    def value(number):
        at = channels + 3 + 3 * number
        return sums[:, at : at + 1] + sums[:, at + 1 : at + 2] + sums[:, at + 2 : at + 3]

    a00, a01, a11, d11 = (value(n) for n in range(4))
    step0 = a00 / (a00 + a01)
    keep = 1.0 - step0
    norm1 = keep * keep * a00 - 2.0 * step0 * keep * a01 + step0 * step0 * a11
    c0 = keep + norm1 / a00
    c1 = -step0
    curve = (c0 * c0 * (a00 + a01) + 2.0 * c0 * c1 * (a01 + a11) + c1 * c1 * (a11 + d11))
    step1 = norm1 / curve
    return step0 + step1 * c0, step1 * c1


def final_kernel(channels, back, slot, dep, jac, first, second, increment, departures, mixed, sems):
    slots = back.shape[0]
    rows = dep.shape[0]
    height = mixed.shape[0]
    a, b = scalars(back, channels)

    def copy(i):
        return pltpu.make_async_copy(mixed.at[i], increment.at[:, i], sems.at[i])

    for i in range(height):
        mixed[i] = a * first[i, :channels] + b * second[i, :channels]
        copy(i).start()
    slots_of = lax.broadcasted_iota(jnp.int32, (slots, rows), 0)
    place = (slots_of == slot[...]).astype(BF)
    own = mxu(place, back[...], ((0,), (0,)))
    state = a * own[:, :channels] + b * own[:, LANES : LANES + channels]
    departures[...] = dep[...] - mxu(state, jac[...], precision=lax.Precision.HIGHEST)
    for i in range(height):
        copy(i).wait()


def shift2(x, by_lat, by_lon):
    n_lat, n_lon = lax.axis_size("lat"), lax.axis_size("lon")
    pairs = [(i * n_lon + j, (i + by_lat) * n_lon + (j + by_lon) % n_lon)
             for i in range(n_lat) for j in range(n_lon) if 0 <= i + by_lat < n_lat]
    return lax.ppermute(x, ("lat", "lon"), pairs)


def on_device(departure_in, obs_owner, obs_cell, obs_count, qc_mask, channel_weight, jacobian,
              conv_taps, projection, slope):
    channels, hidden = projection.shape
    height, breadth = slope.shape[1], slope.shape[2]
    tiles = lax.axis_size(("lat", "lon"))
    rows, radiances = departure_in.shape
    cap = max(2, 3 * rows // (2 * tiles))
    slots = tiles * cap
    padded = -(-(channels + 1) // 16) * 16
    trim = -(-(channels + 1) // 8) * 8
    wide = breadth + LANES
    ext = height + 2 * HALO
    strip = -(-(ext * SIDE) // LANES) * LANES

    def shape(dims, kind=F32):
        return jax.ShapeDtypeStruct(dims, kind)

    weight = channel_weight[None, :]
    inputs = (departure_in, obs_owner.reshape(1, rows), obs_cell[None, :], qc_mask[None, :], weight, jacobian)
    send, slot = call(
        functools.partial(pack_kernel, tiles, cap, breadth, channels),
        (shape((slots, LANES), BF), shape((1, rows), jnp.int32)),
        (obs_count,) + inputs,
        scratch=[pltpu.VMEM(x.shape, x.dtype) for x in inputs] + [pltpu.SemaphoreType.DMA((len(inputs),))],
        smem=1,
        unread=len(inputs),
    )

    def swap(x):
        return lax.all_to_all(x.reshape(tiles, cap, -1), ("lat", "lon"), split_axis=0, concat_axis=0,
                              tiled=True).reshape(slots, -1)

    got = swap(send)

    w_m, w_n, p_t, p_j, g3 = call(
        weights_kernel,
        (shape((3 * hidden, 3 * padded), BF), shape((3 * trim, 3 * hidden), BF), shape((hidden, padded), BF),
         shape((trim, hidden), BF), shape((trim, 3 * padded), BF)),
        (conv_taps, projection, jacobian, weight),
        staged=True,
    )

    slope_inner = jnp.transpose(slope, (1, 0, 2))
    slope_north = shift2(slope_inner[-HALO:], 1, 0)
    slope_south = shift2(slope_inner[:HALO], -1, 0)
    slope_west, slope_east = call(strip_kernel, (shape((hidden, strip), BF),) * 2,
                                  (slope_inner, slope_north, slope_south))

    north, south = call(
        functools.partial(edge_kernel, channels, height),
        (shape((HALO * trim, breadth), BF),) * 2,
        (got, slope_north, slope_south),
        unread=2,
    )
    from_south = shift2(north, -1, 0)
    from_north = shift2(south, 1, 0)
    west, east = call(
        functools.partial(side_kernel, channels, height, breadth), (shape((padded, strip), BF),) * 2, (got,))
    to_west, to_east = call(
        functools.partial(join_kernel, height),
        (shape((padded + hidden, strip), BF),) * 2,
        (west, east, from_north, from_south, slope_west, slope_east, p_t),
        unread=1,
    )
    from_east = shift2(to_west, 0, -1)
    from_west = shift2(to_east, 0, 1)
    inner = call(functools.partial(grid_kernel, channels), shape((height, trim, breadth)), (got,))

    at = lax.axis_index("lat")
    flags = jnp.stack([at > 0, at < lax.axis_size("lat") - 1]).astype(jnp.int32)
    first, second, reply = call(
        functools.partial(main_kernel, channels, hidden, cap),
        (shape((height, trim, breadth)),) * 2 + (shape((slots, 2 * LANES), BF),),
        (flags, got, inner, from_north, from_south, from_east, from_west, slope_inner, slope_north,
         slope_south, w_n, w_m, p_t, p_j, g3),
        scratch=[
            pltpu.VMEM((ext, trim, wide), F32),
            pltpu.VMEM((ext, hidden, wide), BF),
            pltpu.VMEM((ext, hidden, wide), BF),
            pltpu.VMEM((ext, padded, wide), BF),
            pltpu.VMEM((ext, trim, wide), F32),
            pltpu.VMEM((ext, 2 * padded, breadth), BF),
            pltpu.VMEM((2 * padded, slots), F32),
        ],
        smem=1,
        vmem=76,
    )
    back = swap(reply)
    return call(
        functools.partial(final_kernel, channels),
        (shape((channels, height, breadth)), shape((rows, radiances))),
        (back, slot, departure_in, jacobian, first, second),
        scratch=[pltpu.VMEM((height, channels, breadth), F32), pltpu.SemaphoreType.DMA((height,))],
        away=(0,),
        vmem=32,
    )


def solution(mesh):
    placed = (
        P(("lat", "lon"), None),
        P(("lat", "lon"), None),
        P(("lat", "lon")),
        P(("lat", "lon")),
        P(("lat", "lon")),
        P(),
        P(),
        P(),
        P(),
        P(None, "lat", "lon"),
    )
    return jax.shard_map(
        on_device,
        mesh=mesh,
        in_specs=placed,
        out_specs=(P(None, "lat", "lon"), P(("lat", "lon"), None)),
        check_vma=False,
    )
```

```python
import functools

import jax
import jax.numpy as jnp
import numpy as np
from jax import lax
from jax.experimental import pallas as pl
from jax.experimental.pallas import tpu as pltpu
from jax.sharding import PartitionSpec as P

ITERS = 2
HALO = 4
LANES = 128
SIDE = 2 * HALO
BF = jnp.bfloat16
F32 = jnp.float32
INTERPRET = False
G = (18, 26, 25, 24, 24, 24)


def mxu(a, b, dims=((1,), (0,)), precision=None):
    return lax.dot_general(a, b, (dims, ((), ())), precision=precision, preferred_element_type=F32)


def call(kernel, outs, args, scratch=(), smem=0, vmem=24, unread=0, staged=False, away=()):
    def space(i, x):
        if i < smem:
            return pl.BlockSpec(memory_space=pltpu.SMEM)
        if i >= len(args) - unread:
            return pl.BlockSpec(memory_space=pl.ANY)
        if staged:
            return pl.BlockSpec(x.shape, lambda _: (0,) * x.ndim)
        return pl.BlockSpec(memory_space=pltpu.VMEM)

    leaves, tree = jax.tree.flatten(outs)
    out_specs = [pl.BlockSpec(memory_space=pl.ANY if i in away else pltpu.VMEM) for i in range(len(leaves))]
    return pl.pallas_call(
        kernel,
        out_shape=outs,
        grid=(1,) if staged else (),
        in_specs=[space(i, x) for i, x in enumerate(args)],
        out_specs=jax.tree.unflatten(tree, out_specs),
        scratch_shapes=scratch,
        interpret=INTERPRET,
        compiler_params=pltpu.CompilerParams(vmem_limit_bytes=vmem * 2**20 // 2),
    )(*args)


def split3(x):
    hi = x.astype(BF)
    rest = x - hi.astype(F32)
    mid = rest.astype(BF)
    return hi, mid, (rest - mid.astype(F32)).astype(BF)


def pack_kernel(tiles, cap, lon_size, channels, count, dep, meta, tables, send, slot_out):
    owner_row, cell_row, qc_row = meta[0:1], meta[1:2], meta[2:3]
    jac, weight = tables[:channels], tables[channels : channels + 1]
    rows = dep.shape[0]
    slots = send.shape[0]
    hit = (lax.broadcasted_iota(jnp.int32, (tiles, rows), 0) == owner_row).astype(BF)
    before = (lax.broadcasted_iota(jnp.int32, (rows, rows), 0)
              < lax.broadcasted_iota(jnp.int32, (rows, rows), 1)).astype(BF)
    earlier = mxu(hit, before)
    rank = jnp.sum(earlier * hit.astype(F32), axis=0, keepdims=True)
    slot = owner_row * cap + rank.astype(jnp.int32)
    slot_out[...] = slot
    place = (lax.broadcasted_iota(jnp.int32, (slots, rows), 0) == slot).astype(BF)

    used = (lax.broadcasted_iota(jnp.int32, (1, rows), 1) < count[0]).astype(F32)
    row_weight = used * qc_row.astype(F32)
    terms = mxu(jac, dep[...] * weight, ((1,), (1,)), lax.Precision.HIGHEST) * row_weight
    lat = cell_row // lon_size
    lon = cell_row - lat * lon_size
    wide = lax.broadcasted_iota(jnp.int32, (LANES, rows), 0)
    terms = jnp.concatenate([terms, jnp.zeros((LANES - channels, rows), F32)], axis=0)
    terms = jnp.where(wide == channels, row_weight, terms)
    terms = jnp.where(wide == channels + 1, lat.astype(F32), terms)
    terms = jnp.where(wide == channels + 2, lon.astype(F32), terms)
    send[...] = mxu(place, terms.astype(BF), ((1,), (1,))).astype(BF)


def weights_kernel(taps, projection, jac, weight, w_m, w_n, p_t, p_j, g3):
    _, hidden, channels = taps.shape
    trim, padded = p_j.shape[0], p_t.shape[1]

    def shifted(rows, columns, by):
        return (lax.broadcasted_iota(jnp.int32, (rows, columns), 0) + by
                == lax.broadcasted_iota(jnp.int32, (rows, columns), 1)).astype(BF)

    wider, fuller = shifted(channels, padded, 0), shifted(channels, trim, 0)
    for b in range(3):
        total_m, total_n = 0.0, 0.0
        for a in range(3):
            tap = taps[3 * a + b]
            total_m = total_m + mxu(tap, shifted(channels, 3 * padded, a * padded))
            turned_tap = mxu(fuller, tap, ((0,), (1,))).astype(BF)
            total_n = total_n + mxu(turned_tap, shifted(hidden, 3 * hidden, (2 - a) * hidden))
        w_m[b * hidden : (b + 1) * hidden] = total_m.astype(BF)
        w_n[b * trim : (b + 1) * trim] = total_n.astype(BF)
    p_j[...] = mxu(fuller, projection[...], ((0,), (0,))).astype(BF)
    p_t[...] = mxu(projection[...], wider, ((0,), (0,))).astype(BF)
    tall = jnp.concatenate([jac[...], jnp.zeros((padded - channels, jac.shape[1]), F32)], axis=0)
    gram = mxu(tall * weight[...], tall, ((1,), (1,)), lax.Precision.HIGHEST)
    pulled = mxu(p_t[...].astype(F32), gram, precision=lax.Precision.HIGHEST)
    both = jnp.concatenate([gram[:trim], pulled], axis=0)
    hi = both.astype(BF)
    lo = (both - hi.astype(F32)).astype(BF)
    total = 0.0
    for k, value in enumerate((hi, lo, hi)):
        total = total + mxu(value, shifted(padded, 3 * padded, k * padded))
    g3[...] = total.astype(BF)


def turned(got, channels, padded):
    flat = got[...].astype(F32)
    turn = flat.T
    lat_row = turn[channels + 1 : channels + 2].astype(jnp.int32)
    lon_row = turn[channels + 2 : channels + 3].astype(jnp.int32)
    lat_col = flat[:, channels + 1 : channels + 2].astype(jnp.int32)
    lon_col = flat[:, channels + 2 : channels + 3].astype(jnp.int32)
    keep = lax.broadcasted_iota(jnp.int32, (padded, turn.shape[1]), 0) <= channels
    return jnp.where(keep, turn[:padded], 0.0), lat_row, lon_row, lat_col, lon_col


def edge_kernel(channels, height, got, _slope_north, _slope_south, north, south):
    tall, breadth = north.shape
    trim = tall // HALO
    slots = got.shape[0]
    turn, lat_row, _, _, lon = turned(got, channels, -(-trim // 16) * 16)
    values = turn.astype(BF)
    col_hot = (lax.broadcasted_iota(jnp.int32, (slots, breadth), 1) == lon).astype(BF)
    for out, first in ((north, 0), (south, height - HALO)):
        lhs = jnp.concatenate(
            [values * (lat_row == first + k).astype(F32).astype(BF) for k in range(HALO)], axis=0)
        rows = mxu(lhs, col_hot).reshape(HALO, values.shape[0], breadth)[:, :trim]
        out[...] = rows.reshape(tall, breadth).astype(BF)


def rows_of(message, padded):
    tall, breadth = message.shape
    rows = message[...].astype(F32).reshape(HALO, tall // HALO, breadth)
    if padded == tall // HALO:
        return rows
    return jnp.concatenate([rows, jnp.zeros((HALO, padded - tall // HALO, breadth), F32)], axis=1)


def side_kernel(channels, height, breadth, got, west, east):
    padded, strip = west.shape
    slots = got.shape[0]
    turn, _, _, lat, lon = turned(got, channels, padded)
    values = turn.astype(BF)
    for out, mask, col in (
        (west, lon < HALO, HALO + lon),
        (east, lon >= breadth - HALO, lon - (breadth - HALO)),
    ):
        target = jnp.where(mask, (lat + HALO) * SIDE + col, -1)
        hot = (lax.broadcasted_iota(jnp.int32, (slots, strip), 1) == target).astype(BF)
        out[...] = mxu(values, hot).astype(BF)


def grid_kernel(channels, got, out):
    height, trim, breadth = out.shape
    padded = -(-trim // 16) * 16
    slots = got.shape[0]
    turn, lat_row, _, _, lon = turned(got, channels, padded)
    values = turn.astype(BF)
    col_hot = (lax.broadcasted_iota(jnp.int32, (slots, breadth), 1) == lon).astype(BF)
    step = 8

    def body(block, _):
        lhs = jnp.concatenate(
            [values * (lat_row == block * step + k).astype(F32).astype(BF) for k in range(step)], axis=0)
        out[pl.ds(block * step, step)] = mxu(lhs, col_hot).reshape(step, padded, breadth)[:, :trim]
        return 0

    lax.fori_loop(0, height // step, body, 0)


def to_strip(rows, base, block):
    per = LANES // SIDE
    shape = (rows[0].shape[0], LANES)
    lane = lax.broadcasted_iota(jnp.int32, shape, 1)
    left, right = jnp.zeros(shape, F32), jnp.zeros(shape, F32)
    for k, row in enumerate(rows):
        at = base + k - block * per
        if not 0 <= at < per:
            continue
        row = row.astype(F32)
        by = (at * SIDE + HALO) % LANES
        mine = (lane >= at * SIDE) & (lane < (at + 1) * SIDE)
        left = jnp.where(mine & (lane % SIDE >= HALO), pltpu.roll(row[:, :LANES], by, 1), left)
        right = jnp.where(mine & (lane % SIDE < HALO), pltpu.roll(row[:, -LANES:], by, 1), right)
    return left, right


def strip_kernel(inner, north, south, west, east):
    height = inner.shape[0]
    rows = [north[k] for k in range(HALO)] + [inner[k] for k in range(height)] + [south[k] for k in range(HALO)]
    for block in range(west.shape[1] // LANES):
        left, right = to_strip(rows, 0, block)
        west[:, block * LANES : (block + 1) * LANES] = left.astype(BF)
        east[:, block * LANES : (block + 1) * LANES] = right.astype(BF)


def join_kernel(height, west, east, from_north, from_south, slope_west, slope_east, _token, to_west, to_east):
    padded, strip = west.shape
    last = (height + HALO) * SIDE // LANES
    above, below = rows_of(from_north, padded), rows_of(from_south, padded)
    above = to_strip([above[k] for k in range(HALO)], 0, 0)
    below = to_strip([below[k] for k in range(HALO)], HALO + height, last)
    for k, own, slope, out in ((0, west, slope_west, to_west), (1, east, slope_east, to_east)):
        for block in range(strip // LANES):
            part = pl.ds(block * LANES, LANES)
            q = own[:, part]
            if block == 0:
                q = q + above[k].astype(BF)
            if block == last:
                q = q + below[k].astype(BF)
            out[:padded, part] = q
        out[padded:] = slope[...]


def main_kernel(channels, hidden, cap, flags, got, inner, north, south, from_east, from_west, slope_inner,
                slope_north, slope_south, w_n, w_m, p_t, p_j, g3, first_out, second_out, reply,
                field, slope, ga, xb, vec, hi, found):
    height, trim, breadth = inner.shape
    padded = xb.shape[1]
    wide = breadth + LANES
    ext = height + 2 * HALO
    per = LANES // SIDE

    def is_in(i):
        above = (i >= HALO) | (flags[0] == 1)
        below = (i < height + HALO) | (flags[1] == 1)
        return (above & below).astype(F32)

    def join(parts):
        return jnp.concatenate(parts, axis=1)

    def part(x, k):
        return x[:, k * wide : (k + 1) * wide]

    def fill(x):
        return jnp.concatenate([x, jnp.zeros((padded - trim, x.shape[1]), F32)], axis=0).astype(BF)

    def pull(i, ys):
        u = mxu(p_t[...], join([fill(y) for y in ys]))
        for k in range(len(ys)):
            ga[i + k] = (slope[i + k].astype(F32) * part(u, k)).astype(BF)

    lane = lax.broadcasted_iota(jnp.int32, (padded + hidden, LANES), 1)
    from_the_west = lane % SIDE < HALO

    def begin(i, mains, slopes):
        ys = []
        for k in range(len(mains)):
            if k % HALO == 0:
                at = pl.ds(pl.multiple_of((i + k) // per * LANES, LANES), LANES)
                both = jnp.where(from_the_west, from_west[:, at].astype(F32), from_east[:, at].astype(F32))
            shift = 2 * LANES - (i + k) % per * SIDE - HALO
            edge = pltpu.roll(both, shift % LANES, 1)
            y = join([mains[k].astype(F32), edge[:trim]])
            field[i + k] = y
            slope[i + k] = join([slopes[k], edge[padded:].astype(BF)])
            ys.append(y)
        pull(i, ys)

    above, below = rows_of(north, trim), rows_of(south, trim)
    begin(0, [above[k] for k in range(HALO)], [slope_north[k] for k in range(HALO)])
    begin(HALO + height, [below[k] for k in range(HALO)], [slope_south[k] for k in range(HALO)])

    def middle(n, _):
        i = n * G[5]
        begin(i + HALO, [inner[i + k] for k in range(G[5])], [slope_inner[i + k] for k in range(G[5])])
        return 0

    lax.fori_loop(0, height // G[5], middle, 0)

    def spread(i, ys):
        o = mxu(w_n[...], join([ga[pl.ds(i + k - 1, 3)].reshape(3 * hidden, wide) for k in range(len(ys))]))
        out = []
        for k, y in enumerate(ys):
            p = part(o, k)
            out.append(y + p[trim : 2 * trim] + pltpu.roll(p[:trim], wide - 1, 1)
                       + pltpu.roll(p[2 * trim :], 1, 1))
        return out

    def tangent(i, vs):
        o = mxu(w_m[...], join([xb[pl.ds(i + k - 1, 3)].reshape(3 * padded, wide) for k in range(len(vs))]))
        acts = []
        for k in range(len(vs)):
            p = part(o, k)
            h = (p[hidden : 2 * hidden] + pltpu.roll(p[:hidden], 1, 1)
                 + pltpu.roll(p[2 * hidden :], wide - 1, 1))
            acts.append((slope[i + k].astype(F32) * h).astype(BF))
        back = mxu(p_j[...], join(acts))
        return [v + part(back, k) for k, v in enumerate(vs)]

    def gram_of(s, matrix):
        s_hi = s.astype(BF).astype(F32)
        s_lo = fill(s - s_hi)
        s_hi = fill(s_hi)
        return mxu(matrix, jnp.concatenate([s_hi, s_hi, s_lo], axis=0))

    def loop(first, last, size, body):
        assert (last - first) % size == 0

        def step(n, _):
            body(first + n * size)
            return 0

        lax.fori_loop(0, (last - first) // size, step, 0)

    def n_first(i):
        for k, v in enumerate(spread(i, [field[i + k] for k in range(G[0])])):
            vec[i + k] = v
            xb[i + k] = fill(v * is_in(i + k))

    loop(1, ext - 1, G[0], n_first)

    def m_first(i):
        ss = tangent(i, [vec[i + k] for k in range(G[1])])
        gs = gram_of(join(ss), g3[...])
        for k, s in enumerate(ss):
            cell_weight = field[i + k][channels : channels + 1]
            both = part(gs, k)
            hi[i + k, :padded] = fill(s[:, :breadth])
            field[i + k] = cell_weight * both[:trim]
            ga[i + k] = (slope[i + k].astype(F32) * (cell_weight * both[trim:])).astype(BF)

    loop(2, ext - 2, G[1], m_first)

    def keep_first(i):
        first_out[i] = vec[i + HALO][:, :breadth]

    loop(0, height, 1, keep_first)

    def n_second(i):
        for k, v in enumerate(spread(i, [field[i + k] for k in range(G[2])])):
            vec[i + k] = v
            xb[i + k] = fill(v * is_in(i + k))

    loop(3, ext - 3, G[2], n_second)

    def m_second(i):
        vs = [vec[i + k] for k in range(G[3])]
        for k, s in enumerate(tangent(i, vs)):
            second_out[i + k - HALO] = vs[k][:, :breadth]
            hi[i + k, padded:] = fill(s[:, :breadth])

    loop(HALO, ext - HALO, G[3], m_second)

    turn, lat_row, lon_row, _, _ = turned(got, channels, padded)
    slots = got.shape[0]
    piece = 256
    for c in range(slots // piece):
        here = slice(c * piece, (c + 1) * piece)
        col_hot = (lax.broadcasted_iota(jnp.int32, (breadth, piece), 0) == lon_row[:, here]).astype(BF)
        found[:, here] = jnp.zeros((2 * padded, piece), F32)

        def gather(i, col_hot=col_hot, here=here):
            out = mxu(hi[pl.ds(i, G[4])].reshape(G[4] * 2 * padded, breadth), col_hot)
            total = found[:, here]
            for k in range(G[4]):
                mine = (lat_row[:, here] == i + k - HALO)
                total = total + jnp.where(mine, out[k * 2 * padded : (k + 1) * 2 * padded], 0.0)
            found[:, here] = total

        loop(HALO, ext - HALO, G[4], gather)

    row0, row1 = found[:trim], found[padded : padded + trim]
    weight = turn[channels : channels + 1]
    curved0 = gram_of(row0, g3[:trim]) * weight
    curved1 = gram_of(row1, g3[:trim]) * weight
    real = lax.broadcasted_iota(jnp.int32, (trim, slots), 0) < channels
    first = jnp.where(real, turn[:trim], 0.0)

    def total(x):
        return jnp.sum(jnp.sum(x, axis=0, keepdims=True), axis=1, keepdims=True)

    sums = (total(first * row0), total(curved0 * row0), total(curved0 * row1), total(curved1 * row1))
    lane = lax.broadcasted_iota(jnp.int32, (1, LANES), 1)
    pieces = jnp.zeros((1, LANES), F32)
    for number, value in enumerate(sums):
        for third, piece in enumerate(split3(value)):
            pieces = jnp.where(lane == channels + 3 + 3 * number + third, piece.astype(F32), pieces)
    filler = jnp.zeros((LANES - trim, slots), F32)
    turned0 = jnp.concatenate([row0, filler], axis=0).T
    turned1 = jnp.concatenate([row1, filler], axis=0).T
    leads = lax.broadcasted_iota(jnp.int32, (slots, LANES), 0)
    is_lead = leads % cap == 0
    lanes = lax.broadcasted_iota(jnp.int32, (slots, LANES), 1)
    reply[:, :LANES] = jnp.where(lanes < channels, turned0, jnp.where(is_lead, pieces, 0.0)).astype(BF)
    reply[:, LANES:] = turned1.astype(BF)


def scalars(reply, channels):
    sums = jnp.sum(reply[:, :LANES].astype(F32), axis=0, keepdims=True)

    def value(number):
        at = channels + 3 + 3 * number
        return sums[:, at : at + 1] + sums[:, at + 1 : at + 2] + sums[:, at + 2 : at + 3]

    a00, a01, a11, d11 = (value(n) for n in range(4))
    step0 = a00 / (a00 + a01)
    keep = 1.0 - step0
    norm1 = keep * keep * a00 - 2.0 * step0 * keep * a01 + step0 * step0 * a11
    c0 = keep + norm1 / a00
    c1 = -step0
    curve = (c0 * c0 * (a00 + a01) + 2.0 * c0 * c1 * (a01 + a11) + c1 * c1 * (a11 + d11))
    step1 = norm1 / curve
    return step0 + step1 * c0, step1 * c1


def final_kernel(channels, back, slot, dep, jac, first, second, increment, departures, mixed, sems):
    slots = back.shape[0]
    rows = dep.shape[0]
    height = mixed.shape[0]
    a, b = scalars(back, channels)

    def copy(i):
        return pltpu.make_async_copy(mixed.at[i], increment.at[:, i], sems.at[i])

    for i in range(height):
        mixed[i] = a * first[i, :channels] + b * second[i, :channels]
        copy(i).start()
    slots_of = lax.broadcasted_iota(jnp.int32, (slots, rows), 0)
    place = (slots_of == slot[...]).astype(BF)
    own = mxu(place, back[...], ((0,), (0,)))
    state = a * own[:, :channels] + b * own[:, LANES : LANES + channels]
    departures[...] = dep[...] - mxu(state, jac[...], precision=lax.Precision.HIGHEST)
    for i in range(height):
        copy(i).wait()


def shift2(x, by_lat, by_lon):
    n_lat, n_lon = lax.axis_size("lat"), lax.axis_size("lon")
    pairs = [(i * n_lon + j, (i + by_lat) * n_lon + (j + by_lon) % n_lon)
             for i in range(n_lat) for j in range(n_lon) if 0 <= i + by_lat < n_lat]
    return lax.ppermute(x, ("lat", "lon"), pairs)


def on_device(departure_in, obs_owner, obs_cell, obs_count, qc_mask, channel_weight, jacobian,
              conv_taps, projection, slope):
    channels, hidden = projection.shape
    height, breadth = slope.shape[1], slope.shape[2]
    tiles = lax.axis_size(("lat", "lon"))
    rows, radiances = departure_in.shape
    cap = max(2, 3 * rows // (2 * tiles))
    slots = tiles * cap
    padded = -(-(channels + 1) // 16) * 16
    trim = -(-(channels + 1) // 8) * 8
    wide = breadth + LANES
    ext = height + 2 * HALO
    strip = -(-(ext * SIDE) // LANES) * LANES

    def shape(dims, kind=F32):
        return jax.ShapeDtypeStruct(dims, kind)

    weight = channel_weight[None, :]
    send, slot = call(
        functools.partial(pack_kernel, tiles, cap, breadth, channels),
        (shape((slots, LANES), BF), shape((1, rows), jnp.int32)),
        (obs_count, departure_in, jnp.stack([obs_owner[:, 0], obs_cell, qc_mask]),
         jnp.concatenate([jacobian, weight], axis=0)),
        smem=1,
    )

    def swap(x):
        return lax.all_to_all(x.reshape(tiles, cap, -1), ("lat", "lon"), split_axis=0, concat_axis=0,
                              tiled=True).reshape(slots, -1)

    got = swap(send)

    w_m, w_n, p_t, p_j, g3 = call(
        weights_kernel,
        (shape((3 * hidden, 3 * padded), BF), shape((3 * trim, 3 * hidden), BF), shape((hidden, padded), BF),
         shape((trim, hidden), BF), shape((trim + hidden, 3 * padded), BF)),
        (conv_taps, projection, jacobian, weight),
        staged=True,
    )

    slope_inner = jnp.transpose(slope, (1, 0, 2))
    slope_north = shift2(slope_inner[-HALO:], 1, 0)
    slope_south = shift2(slope_inner[:HALO], -1, 0)
    slope_west, slope_east = call(strip_kernel, (shape((hidden, strip), BF),) * 2,
                                  (slope_inner, slope_north, slope_south))

    north, south = call(
        functools.partial(edge_kernel, channels, height),
        (shape((HALO * trim, breadth), BF),) * 2,
        (got, slope_north, slope_south),
        unread=2,
    )
    from_south = shift2(north, -1, 0)
    from_north = shift2(south, 1, 0)
    west, east = call(
        functools.partial(side_kernel, channels, height, breadth), (shape((padded, strip), BF),) * 2, (got,))
    to_west, to_east = call(
        functools.partial(join_kernel, height),
        (shape((padded + hidden, strip), BF),) * 2,
        (west, east, from_north, from_south, slope_west, slope_east, p_t),
        unread=1,
    )
    from_east = shift2(to_west, 0, -1)
    from_west = shift2(to_east, 0, 1)
    inner = call(functools.partial(grid_kernel, channels), shape((height, trim, breadth)), (got,))

    at = lax.axis_index("lat")
    flags = jnp.stack([at > 0, at < lax.axis_size("lat") - 1]).astype(jnp.int32)
    first, second, reply = call(
        functools.partial(main_kernel, channels, hidden, cap),
        (shape((height, trim, breadth)),) * 2 + (shape((slots, 2 * LANES), BF),),
        (flags, got, inner, from_north, from_south, from_east, from_west, slope_inner, slope_north,
         slope_south, w_n, w_m, p_t, p_j, g3),
        scratch=[
            pltpu.VMEM((ext, trim, wide), F32),
            pltpu.VMEM((ext, hidden, wide), BF),
            pltpu.VMEM((ext, hidden, wide), BF),
            pltpu.VMEM((ext, padded, wide), BF),
            pltpu.VMEM((ext, trim, wide), F32),
            pltpu.VMEM((ext, 2 * padded, breadth), BF),
            pltpu.VMEM((2 * padded, slots), F32),
        ],
        smem=1,
        vmem=76,
    )
    back = swap(reply)
    return call(
        functools.partial(final_kernel, channels),
        (shape((channels, height, breadth)), shape((rows, radiances))),
        (back, slot, departure_in, jacobian, first, second),
        scratch=[pltpu.VMEM((height, channels, breadth), F32), pltpu.SemaphoreType.DMA((height,))],
        away=(0,),
        vmem=32,
    )


def solution(mesh):
    placed = (
        P(("lat", "lon"), None),
        P(("lat", "lon"), None),
        P(("lat", "lon")),
        P(("lat", "lon")),
        P(("lat", "lon")),
        P(),
        P(),
        P(),
        P(),
        P(None, "lat", "lon"),
    )
    return jax.shard_map(
        on_device,
        mesh=mesh,
        in_specs=placed,
        out_specs=(P(None, "lat", "lon"), P(("lat", "lon"), None)),
        check_vma=False,
    )
```

```python
import functools

import jax
import jax.numpy as jnp
import numpy as np
from jax import lax
from jax.experimental import pallas as pl
from jax.experimental.pallas import tpu as pltpu
from jax.sharding import PartitionSpec as P

ITERS = 2
HALO = 4
LANES = 128
SIDE = 2 * HALO
BF = jnp.bfloat16
F32 = jnp.float32
INTERPRET = False
G = (18, 26, 25, 24, 24, 24)


def mxu(a, b, dims=((1,), (0,)), precision=None):
    return lax.dot_general(a, b, (dims, ((), ())), precision=precision, preferred_element_type=F32)


def call(kernel, outs, args, scratch=(), smem=0, vmem=24, unread=0, staged=False, away=()):
    def space(i, x):
        if i < smem:
            return pl.BlockSpec(memory_space=pltpu.SMEM)
        if i >= len(args) - unread:
            return pl.BlockSpec(memory_space=pl.ANY)
        if staged:
            return pl.BlockSpec(x.shape, lambda _: (0,) * x.ndim)
        return pl.BlockSpec(memory_space=pltpu.VMEM)

    leaves, tree = jax.tree.flatten(outs)
    out_specs = [pl.BlockSpec(memory_space=pl.ANY if i in away else pltpu.VMEM) for i in range(len(leaves))]
    return pl.pallas_call(
        kernel,
        out_shape=outs,
        grid=(1,) if staged else (),
        in_specs=[space(i, x) for i, x in enumerate(args)],
        out_specs=jax.tree.unflatten(tree, out_specs),
        scratch_shapes=scratch,
        interpret=INTERPRET,
        compiler_params=pltpu.CompilerParams(vmem_limit_bytes=vmem * 2**20 // 2),
    )(*args)


def split3(x):
    hi = x.astype(BF)
    rest = x - hi.astype(F32)
    mid = rest.astype(BF)
    return hi, mid, (rest - mid.astype(F32)).astype(BF)


def pack_kernel(tiles, cap, lon_size, channels, count, dep, meta, tables, send, slot_out):
    owner_row, cell_row, qc_row = meta[0:1], meta[1:2], meta[2:3]
    jac, weight = tables[:channels], tables[channels : channels + 1]
    rows = dep.shape[0]
    slots = send.shape[0]
    hit = (lax.broadcasted_iota(jnp.int32, (tiles, rows), 0) == owner_row).astype(BF)
    before = (lax.broadcasted_iota(jnp.int32, (rows, rows), 0)
              < lax.broadcasted_iota(jnp.int32, (rows, rows), 1)).astype(BF)
    earlier = mxu(hit, before)
    rank = jnp.sum(earlier * hit.astype(F32), axis=0, keepdims=True)
    slot = owner_row * cap + rank.astype(jnp.int32)
    slot_out[...] = slot
    place = (lax.broadcasted_iota(jnp.int32, (slots, rows), 0) == slot).astype(BF)

    used = (lax.broadcasted_iota(jnp.int32, (1, rows), 1) < count[0]).astype(F32)
    row_weight = used * qc_row.astype(F32)
    terms = mxu(jac, dep[...] * weight, ((1,), (1,)), lax.Precision.HIGHEST) * row_weight
    lat = cell_row // lon_size
    lon = cell_row - lat * lon_size
    wide = lax.broadcasted_iota(jnp.int32, (LANES, rows), 0)
    terms = jnp.concatenate([terms, jnp.zeros((LANES - channels, rows), F32)], axis=0)
    terms = jnp.where(wide == channels, row_weight, terms)
    terms = jnp.where(wide == channels + 1, lat.astype(F32), terms)
    terms = jnp.where(wide == channels + 2, lon.astype(F32), terms)
    send[...] = mxu(place, terms.astype(BF), ((1,), (1,))).astype(BF)


def weights_kernel(taps, projection, jac, weight, w_m, w_n, p_t, p_j, g3):
    _, hidden, channels = taps.shape
    trim, padded = p_j.shape[0], p_t.shape[1]

    def shifted(rows, columns, by):
        return (lax.broadcasted_iota(jnp.int32, (rows, columns), 0) + by
                == lax.broadcasted_iota(jnp.int32, (rows, columns), 1)).astype(BF)

    wider, fuller = shifted(channels, padded, 0), shifted(channels, trim, 0)
    for b in range(3):
        total_m, total_n = 0.0, 0.0
        for a in range(3):
            tap = taps[3 * a + b]
            total_m = total_m + mxu(tap, shifted(channels, 3 * padded, a * padded))
            turned_tap = mxu(fuller, tap, ((0,), (1,))).astype(BF)
            total_n = total_n + mxu(turned_tap, shifted(hidden, 3 * hidden, (2 - a) * hidden))
        w_m[b * hidden : (b + 1) * hidden] = total_m.astype(BF)
        w_n[b * trim : (b + 1) * trim] = total_n.astype(BF)
    p_j[...] = mxu(fuller, projection[...], ((0,), (0,))).astype(BF)
    p_t[...] = mxu(projection[...], wider, ((0,), (0,))).astype(BF)
    tall = jnp.concatenate([jac[...], jnp.zeros((padded - channels, jac.shape[1]), F32)], axis=0)
    gram = mxu(tall * weight[...], tall, ((1,), (1,)), lax.Precision.HIGHEST)
    pulled = mxu(p_t[...].astype(F32), gram, precision=lax.Precision.HIGHEST)
    both = jnp.concatenate([gram[:trim], pulled], axis=0)
    hi = both.astype(BF)
    lo = (both - hi.astype(F32)).astype(BF)
    total = 0.0
    for k, value in enumerate((hi, lo, hi)):
        total = total + mxu(value, shifted(padded, 3 * padded, k * padded))
    g3[...] = total.astype(BF)


def turned(got, channels, padded):
    flat = got[...].astype(F32)
    turn = flat.T
    lat_row = turn[channels + 1 : channels + 2].astype(jnp.int32)
    lon_row = turn[channels + 2 : channels + 3].astype(jnp.int32)
    lat_col = flat[:, channels + 1 : channels + 2].astype(jnp.int32)
    lon_col = flat[:, channels + 2 : channels + 3].astype(jnp.int32)
    keep = lax.broadcasted_iota(jnp.int32, (padded, turn.shape[1]), 0) <= channels
    return jnp.where(keep, turn[:padded], 0.0), lat_row, lon_row, lat_col, lon_col


def edge_kernel(channels, height, got, _slope_north, _slope_south, north, south):
    tall, breadth = north.shape
    trim = tall // HALO
    slots = got.shape[0]
    turn, lat_row, _, _, lon = turned(got, channels, -(-trim // 16) * 16)
    values = turn.astype(BF)
    col_hot = (lax.broadcasted_iota(jnp.int32, (slots, breadth), 1) == lon).astype(BF)
    for out, first in ((north, 0), (south, height - HALO)):
        lhs = jnp.concatenate(
            [values * (lat_row == first + k).astype(F32).astype(BF) for k in range(HALO)], axis=0)
        rows = mxu(lhs, col_hot).reshape(HALO, values.shape[0], breadth)[:, :trim]
        out[...] = rows.reshape(tall, breadth).astype(BF)


def rows_of(message, padded):
    tall, breadth = message.shape
    rows = message[...].astype(F32).reshape(HALO, tall // HALO, breadth)
    if padded == tall // HALO:
        return rows
    return jnp.concatenate([rows, jnp.zeros((HALO, padded - tall // HALO, breadth), F32)], axis=1)


def side_kernel(channels, height, breadth, got, west, east):
    padded, strip = west.shape
    slots = got.shape[0]
    turn, _, _, lat, lon = turned(got, channels, padded)
    values = turn.astype(BF)
    for out, mask, col in (
        (west, lon < HALO, HALO + lon),
        (east, lon >= breadth - HALO, lon - (breadth - HALO)),
    ):
        target = jnp.where(mask, (lat + HALO) * SIDE + col, -1)
        hot = (lax.broadcasted_iota(jnp.int32, (slots, strip), 1) == target).astype(BF)
        out[...] = mxu(values, hot).astype(BF)


def grid_kernel(channels, got, out):
    height, trim, breadth = out.shape
    padded = -(-trim // 16) * 16
    slots = got.shape[0]
    turn, lat_row, _, _, lon = turned(got, channels, padded)
    values = turn.astype(BF)
    col_hot = (lax.broadcasted_iota(jnp.int32, (slots, breadth), 1) == lon).astype(BF)
    step = 8

    def body(block, _):
        lhs = jnp.concatenate(
            [values * (lat_row == block * step + k).astype(F32).astype(BF) for k in range(step)], axis=0)
        out[pl.ds(block * step, step)] = mxu(lhs, col_hot).reshape(step, padded, breadth)[:, :trim]
        return 0

    lax.fori_loop(0, height // step, body, 0)


def to_strip(rows, base, block):
    per = LANES // SIDE
    shape = (rows[0].shape[0], LANES)
    lane = lax.broadcasted_iota(jnp.int32, shape, 1)
    left, right = jnp.zeros(shape, F32), jnp.zeros(shape, F32)
    for k, row in enumerate(rows):
        at = base + k - block * per
        if not 0 <= at < per:
            continue
        row = row.astype(F32)
        by = (at * SIDE + HALO) % LANES
        mine = (lane >= at * SIDE) & (lane < (at + 1) * SIDE)
        left = jnp.where(mine & (lane % SIDE >= HALO), pltpu.roll(row[:, :LANES], by, 1), left)
        right = jnp.where(mine & (lane % SIDE < HALO), pltpu.roll(row[:, -LANES:], by, 1), right)
    return left, right


def strip_kernel(inner, north, south, west, east):
    height = inner.shape[0]
    rows = [north[k] for k in range(HALO)] + [inner[k] for k in range(height)] + [south[k] for k in range(HALO)]
    for block in range(west.shape[1] // LANES):
        left, right = to_strip(rows, 0, block)
        west[:, block * LANES : (block + 1) * LANES] = left.astype(BF)
        east[:, block * LANES : (block + 1) * LANES] = right.astype(BF)


def join_kernel(height, west, east, from_north, from_south, slope_west, slope_east, _token, to_west, to_east):
    padded, strip = west.shape
    last = (height + HALO) * SIDE // LANES
    above, below = rows_of(from_north, padded), rows_of(from_south, padded)
    above = to_strip([above[k] for k in range(HALO)], 0, 0)
    below = to_strip([below[k] for k in range(HALO)], HALO + height, last)
    for k, own, slope, out in ((0, west, slope_west, to_west), (1, east, slope_east, to_east)):
        for block in range(strip // LANES):
            part = pl.ds(block * LANES, LANES)
            q = own[:, part]
            if block == 0:
                q = q + above[k].astype(BF)
            if block == last:
                q = q + below[k].astype(BF)
            out[:padded, part] = q
        out[padded:] = slope[...]


def main_kernel(channels, hidden, cap, flags, got, inner, north, south, from_east, from_west, slope_inner,
                slope_north, slope_south, w_n, w_m, p_t, p_j, g3, first_out, second_out, reply,
                field, slope, ga, xb, vec, hi, found):
    height, trim, breadth = inner.shape
    padded = xb.shape[1]
    wide = breadth + LANES
    ext = height + 2 * HALO
    per = LANES // SIDE

    def is_in(i):
        above = (i >= HALO) | (flags[0] == 1)
        below = (i < height + HALO) | (flags[1] == 1)
        return (above & below).astype(F32)

    def join(parts):
        return jnp.concatenate(parts, axis=1)

    def part(x, k, lanes=wide):
        return x[:, k * lanes : (k + 1) * lanes]

    def fill(x):
        return jnp.concatenate([x, jnp.zeros((padded - trim, x.shape[1]), F32)], axis=0).astype(BF)

    def pull(i, ys):
        u = mxu(p_t[...], join([fill(y) for y in ys]))
        for k in range(len(ys)):
            ga[i + k] = (slope[i + k].astype(F32) * part(u, k)).astype(BF)

    lane = lax.broadcasted_iota(jnp.int32, (padded + hidden, LANES), 1)
    from_the_west = lane % SIDE < HALO

    def begin(i, mains, slopes):
        ys = []
        for k in range(len(mains)):
            if k % HALO == 0:
                at = pl.ds(pl.multiple_of((i + k) // per * LANES, LANES), LANES)
                both = jnp.where(from_the_west, from_west[:, at].astype(F32), from_east[:, at].astype(F32))
            shift = 2 * LANES - (i + k) % per * SIDE - HALO
            edge = pltpu.roll(both, shift % LANES, 1)
            y = join([mains[k].astype(F32), edge[:trim]])
            field[i + k] = y
            slope[i + k] = join([slopes[k], edge[padded:].astype(BF)])
            ys.append(y)
        pull(i, ys)

    above, below = rows_of(north, trim), rows_of(south, trim)
    begin(0, [above[k] for k in range(HALO)], [slope_north[k] for k in range(HALO)])
    begin(HALO + height, [below[k] for k in range(HALO)], [slope_south[k] for k in range(HALO)])

    def middle(n, _):
        i = n * G[5]
        begin(i + HALO, [inner[i + k] for k in range(G[5])], [slope_inner[i + k] for k in range(G[5])])
        return 0

    lax.fori_loop(0, height // G[5], middle, 0)

    def spread(i, ys):
        o = mxu(w_n[...], join([ga[pl.ds(i + k - 1, 3)].reshape(3 * hidden, wide) for k in range(len(ys))]))
        out = []
        for k, y in enumerate(ys):
            p = part(o, k)
            out.append(y + p[trim : 2 * trim] + pltpu.roll(p[:trim], wide - 1, 1)
                       + pltpu.roll(p[2 * trim :], 1, 1))
        return out

    def tangent(i, vs):
        lanes = vs[0].shape[1]
        o = mxu(w_m[...], join([xb[pl.ds(i + k - 1, 3)].reshape(3 * padded, wide) for k in range(len(vs))]))
        acts = []
        for k in range(len(vs)):
            p = part(o, k)
            h = (p[hidden : 2 * hidden] + pltpu.roll(p[:hidden], 1, 1)
                 + pltpu.roll(p[2 * hidden :], wide - 1, 1))
            acts.append((slope[i + k].astype(F32) * h).astype(BF)[:, :lanes])
        back = mxu(p_j[...], join(acts))
        return [v + part(back, k, lanes) for k, v in enumerate(vs)]

    def gram_of(s, matrix):
        s_hi = s.astype(BF).astype(F32)
        s_lo = fill(s - s_hi)
        s_hi = fill(s_hi)
        return mxu(matrix, jnp.concatenate([s_hi, s_hi, s_lo], axis=0))

    def loop(first, last, size, body):
        assert (last - first) % size == 0

        def step(n, _):
            body(first + n * size)
            return 0

        lax.fori_loop(0, (last - first) // size, step, 0)

    def n_first(i):
        for k, v in enumerate(spread(i, [field[i + k] for k in range(G[0])])):
            first_out[i + k] = v[:, :breadth]
            vec[i + k] = v[:, breadth:]
            xb[i + k] = fill(v * is_in(i + k))

    loop(1, ext - 1, G[0], n_first)

    def m_first(i):
        ss = tangent(i, [join([first_out[i + k], vec[i + k]]) for k in range(G[1])])
        gs = gram_of(join(ss), g3[...])
        for k, s in enumerate(ss):
            cell_weight = field[i + k][channels : channels + 1]
            both = part(gs, k)
            hi[i + k, :padded] = fill(s[:, :breadth])
            field[i + k] = cell_weight * both[:trim]
            ga[i + k] = (slope[i + k].astype(F32) * (cell_weight * both[trim:])).astype(BF)

    loop(2, ext - 2, G[1], m_first)

    def n_second(i):
        for k, v in enumerate(spread(i, [field[i + k] for k in range(G[2])])):
            second_out[i + k] = v[:, :breadth]
            xb[i + k] = fill(v * is_in(i + k))

    loop(3, ext - 3, G[2], n_second)

    def m_second(i):
        for k, s in enumerate(tangent(i, [second_out[i + k] for k in range(G[3])])):
            hi[i + k, padded:] = fill(s)

    loop(HALO, ext - HALO, G[3], m_second)

    turn, lat_row, lon_row, _, _ = turned(got, channels, padded)
    slots = got.shape[0]
    piece = 256
    for c in range(slots // piece):
        here = slice(c * piece, (c + 1) * piece)
        col_hot = (lax.broadcasted_iota(jnp.int32, (breadth, piece), 0) == lon_row[:, here]).astype(BF)
        found[:, here] = jnp.zeros((2 * padded, piece), F32)

        def gather(i, col_hot=col_hot, here=here):
            out = mxu(hi[pl.ds(i, G[4])].reshape(G[4] * 2 * padded, breadth), col_hot)
            total = found[:, here]
            for k in range(G[4]):
                mine = (lat_row[:, here] == i + k - HALO)
                total = total + jnp.where(mine, out[k * 2 * padded : (k + 1) * 2 * padded], 0.0)
            found[:, here] = total

        loop(HALO, ext - HALO, G[4], gather)

    row0, row1 = found[:trim], found[padded : padded + trim]
    weight = turn[channels : channels + 1]
    curved0 = gram_of(row0, g3[:trim]) * weight
    curved1 = gram_of(row1, g3[:trim]) * weight
    real = lax.broadcasted_iota(jnp.int32, (trim, slots), 0) < channels
    first = jnp.where(real, turn[:trim], 0.0)

    def total(x):
        return jnp.sum(jnp.sum(x, axis=0, keepdims=True), axis=1, keepdims=True)

    sums = (total(first * row0), total(curved0 * row0), total(curved0 * row1), total(curved1 * row1))
    lane = lax.broadcasted_iota(jnp.int32, (1, LANES), 1)
    pieces = jnp.zeros((1, LANES), F32)
    for number, value in enumerate(sums):
        for third, piece in enumerate(split3(value)):
            pieces = jnp.where(lane == channels + 3 + 3 * number + third, piece.astype(F32), pieces)
    filler = jnp.zeros((LANES - trim, slots), F32)
    turned0 = jnp.concatenate([row0, filler], axis=0).T
    turned1 = jnp.concatenate([row1, filler], axis=0).T
    leads = lax.broadcasted_iota(jnp.int32, (slots, LANES), 0)
    is_lead = leads % cap == 0
    lanes = lax.broadcasted_iota(jnp.int32, (slots, LANES), 1)
    reply[:, :LANES] = jnp.where(lanes < channels, turned0, jnp.where(is_lead, pieces, 0.0)).astype(BF)
    reply[:, LANES:] = turned1.astype(BF)


def scalars(reply, channels):
    sums = jnp.sum(reply[:, :LANES].astype(F32), axis=0, keepdims=True)

    def value(number):
        at = channels + 3 + 3 * number
        return sums[:, at : at + 1] + sums[:, at + 1 : at + 2] + sums[:, at + 2 : at + 3]

    a00, a01, a11, d11 = (value(n) for n in range(4))
    step0 = a00 / (a00 + a01)
    keep = 1.0 - step0
    norm1 = keep * keep * a00 - 2.0 * step0 * keep * a01 + step0 * step0 * a11
    c0 = keep + norm1 / a00
    c1 = -step0
    curve = (c0 * c0 * (a00 + a01) + 2.0 * c0 * c1 * (a01 + a11) + c1 * c1 * (a11 + d11))
    step1 = norm1 / curve
    return step0 + step1 * c0, step1 * c1


def final_kernel(channels, back, slot, dep, jac, first, second, increment, departures, mixed, sems):
    slots = back.shape[0]
    rows = dep.shape[0]
    height = mixed.shape[0]
    a, b = scalars(back, channels)

    def copy(i):
        return pltpu.make_async_copy(mixed.at[i], increment.at[:, i], sems.at[i])

    for i in range(height):
        mixed[i] = a * first[i + HALO, :channels] + b * second[i + HALO, :channels]
        copy(i).start()
    slots_of = lax.broadcasted_iota(jnp.int32, (slots, rows), 0)
    place = (slots_of == slot[...]).astype(BF)
    own = mxu(place, back[...], ((0,), (0,)))
    state = a * own[:, :channels] + b * own[:, LANES : LANES + channels]
    departures[...] = dep[...] - mxu(state, jac[...], precision=lax.Precision.HIGHEST)
    for i in range(height):
        copy(i).wait()


def shift2(x, by_lat, by_lon):
    n_lat, n_lon = lax.axis_size("lat"), lax.axis_size("lon")
    pairs = [(i * n_lon + j, (i + by_lat) * n_lon + (j + by_lon) % n_lon)
             for i in range(n_lat) for j in range(n_lon) if 0 <= i + by_lat < n_lat]
    return lax.ppermute(x, ("lat", "lon"), pairs)


def on_device(departure_in, obs_owner, obs_cell, obs_count, qc_mask, channel_weight, jacobian,
              conv_taps, projection, slope):
    channels, hidden = projection.shape
    height, breadth = slope.shape[1], slope.shape[2]
    tiles = lax.axis_size(("lat", "lon"))
    rows, radiances = departure_in.shape
    cap = max(2, 3 * rows // (2 * tiles))
    slots = tiles * cap
    padded = -(-(channels + 1) // 16) * 16
    trim = -(-(channels + 1) // 8) * 8
    wide = breadth + LANES
    ext = height + 2 * HALO
    strip = -(-(ext * SIDE) // LANES) * LANES

    def shape(dims, kind=F32):
        return jax.ShapeDtypeStruct(dims, kind)

    weight = channel_weight[None, :]
    send, slot = call(
        functools.partial(pack_kernel, tiles, cap, breadth, channels),
        (shape((slots, LANES), BF), shape((1, rows), jnp.int32)),
        (obs_count, departure_in, jnp.stack([obs_owner[:, 0], obs_cell, qc_mask]),
         jnp.concatenate([jacobian, weight], axis=0)),
        smem=1,
    )

    def swap(x):
        return lax.all_to_all(x.reshape(tiles, cap, -1), ("lat", "lon"), split_axis=0, concat_axis=0,
                              tiled=True).reshape(slots, -1)

    got = swap(send)

    w_m, w_n, p_t, p_j, g3 = call(
        weights_kernel,
        (shape((3 * hidden, 3 * padded), BF), shape((3 * trim, 3 * hidden), BF), shape((hidden, padded), BF),
         shape((trim, hidden), BF), shape((trim + hidden, 3 * padded), BF)),
        (conv_taps, projection, jacobian, weight),
        staged=True,
    )

    slope_inner = jnp.transpose(slope, (1, 0, 2))
    low, high = lax.optimization_barrier((slope[:, -HALO:], slope[:, :HALO]))
    slope_north = shift2(jnp.transpose(low, (1, 0, 2)), 1, 0)
    slope_south = shift2(jnp.transpose(high, (1, 0, 2)), -1, 0)
    slope_west, slope_east = call(strip_kernel, (shape((hidden, strip), BF),) * 2,
                                  (slope_inner, slope_north, slope_south))

    north, south = call(
        functools.partial(edge_kernel, channels, height),
        (shape((HALO * trim, breadth), BF),) * 2,
        (got, slope_north, slope_south),
        unread=2,
    )
    from_south = shift2(north, -1, 0)
    from_north = shift2(south, 1, 0)
    west, east = call(
        functools.partial(side_kernel, channels, height, breadth), (shape((padded, strip), BF),) * 2, (got,))
    to_west, to_east = call(
        functools.partial(join_kernel, height),
        (shape((padded + hidden, strip), BF),) * 2,
        (west, east, from_north, from_south, slope_west, slope_east, p_t),
        unread=1,
    )
    from_east = shift2(to_west, 0, -1)
    from_west = shift2(to_east, 0, 1)
    inner = call(functools.partial(grid_kernel, channels), shape((height, trim, breadth)), (got,))

    at = lax.axis_index("lat")
    flags = jnp.stack([at > 0, at < lax.axis_size("lat") - 1]).astype(jnp.int32)
    first, second, reply = call(
        functools.partial(main_kernel, channels, hidden, cap),
        (shape((ext, trim, breadth)),) * 2 + (shape((slots, 2 * LANES), BF),),
        (flags, got, inner, from_north, from_south, from_east, from_west, slope_inner, slope_north,
         slope_south, w_n, w_m, p_t, p_j, g3),
        scratch=[
            pltpu.VMEM((ext, trim, wide), F32),
            pltpu.VMEM((ext, hidden, wide), BF),
            pltpu.VMEM((ext, hidden, wide), BF),
            pltpu.VMEM((ext, padded, wide), BF),
            pltpu.VMEM((ext, trim, LANES), F32),
            pltpu.VMEM((ext, 2 * padded, breadth), BF),
            pltpu.VMEM((2 * padded, slots), F32),
        ],
        smem=1,
        vmem=76,
    )
    back = swap(reply)
    return call(
        functools.partial(final_kernel, channels),
        (shape((channels, height, breadth)), shape((rows, radiances))),
        (back, slot, departure_in, jacobian, first, second),
        scratch=[pltpu.VMEM((height, channels, breadth), F32), pltpu.SemaphoreType.DMA((height,))],
        away=(0,),
        vmem=32,
    )


def solution(mesh):
    placed = (
        P(("lat", "lon"), None),
        P(("lat", "lon"), None),
        P(("lat", "lon")),
        P(("lat", "lon")),
        P(("lat", "lon")),
        P(),
        P(),
        P(),
        P(),
        P(None, "lat", "lon"),
    )
    return jax.shard_map(
        on_device,
        mesh=mesh,
        in_specs=placed,
        out_specs=(P(None, "lat", "lon"), P(("lat", "lon"), None)),
        check_vma=False,
    )
```

```python
import functools

import jax
import jax.numpy as jnp
import numpy as np
from jax import lax
from jax.experimental import pallas as pl
from jax.experimental.pallas import tpu as pltpu
from jax.sharding import PartitionSpec as P

ITERS = 2
HALO = 4
LANES = 128
GROUP = 8
SIDE = 2 * HALO
BF = jnp.bfloat16
F32 = jnp.float32
INTERPRET = False
G = (18, 26, 25, 24, 24, 24)


def mxu(a, b, dims=((1,), (0,)), precision=None):
    return lax.dot_general(a, b, (dims, ((), ())), precision=precision, preferred_element_type=F32)


def call(kernel, outs, args, scratch=(), smem=0, vmem=24, unread=0, staged=False, away=()):
    def space(i, x):
        if i < smem:
            return pl.BlockSpec(memory_space=pltpu.SMEM)
        if i >= len(args) - unread:
            return pl.BlockSpec(memory_space=pl.ANY)
        if staged:
            return pl.BlockSpec(x.shape, lambda _: (0,) * x.ndim)
        return pl.BlockSpec(memory_space=pltpu.VMEM)

    leaves, tree = jax.tree.flatten(outs)
    out_specs = [pl.BlockSpec(memory_space=pl.ANY if i in away else pltpu.VMEM) for i in range(len(leaves))]
    return pl.pallas_call(
        kernel,
        out_shape=outs,
        grid=(1,) if staged else (),
        in_specs=[space(i, x) for i, x in enumerate(args)],
        out_specs=jax.tree.unflatten(tree, out_specs),
        scratch_shapes=scratch,
        interpret=INTERPRET,
        compiler_params=pltpu.CompilerParams(vmem_limit_bytes=vmem * 2**20 // 2),
    )(*args)


def split3(x):
    hi = x.astype(BF)
    rest = x - hi.astype(F32)
    mid = rest.astype(BF)
    return hi, mid, (rest - mid.astype(F32)).astype(BF)


def pack_kernel(tiles, cap, lon_size, channels, count, dep, meta, tables, send, slot_out):
    owner_row, cell_row, qc_row = meta[0:1], meta[1:2], meta[2:3]
    jac, weight = tables[:channels], tables[channels : channels + 1]
    rows = dep.shape[0]
    slots = send.shape[0]
    hit = (lax.broadcasted_iota(jnp.int32, (tiles, rows), 0) == owner_row).astype(BF)
    before = (lax.broadcasted_iota(jnp.int32, (rows, rows), 0)
              < lax.broadcasted_iota(jnp.int32, (rows, rows), 1)).astype(BF)
    earlier = mxu(hit, before)
    rank = jnp.sum(earlier * hit.astype(F32), axis=0, keepdims=True)
    slot = owner_row * cap + rank.astype(jnp.int32)
    slot_out[...] = slot
    place = (lax.broadcasted_iota(jnp.int32, (slots, rows), 0) == slot).astype(BF)

    used = (lax.broadcasted_iota(jnp.int32, (1, rows), 1) < count[0]).astype(F32)
    row_weight = used * qc_row.astype(F32)
    terms = mxu(jac, dep[...] * weight, ((1,), (1,)), lax.Precision.HIGHEST) * row_weight
    lat = cell_row // lon_size
    lon = cell_row - lat * lon_size
    wide = lax.broadcasted_iota(jnp.int32, (LANES, rows), 0)
    terms = jnp.concatenate([terms, jnp.zeros((LANES - channels, rows), F32)], axis=0)
    terms = jnp.where(wide == channels, row_weight, terms)
    terms = jnp.where(wide == channels + 1, lat.astype(F32), terms)
    terms = jnp.where(wide == channels + 2, lon.astype(F32), terms)
    send[...] = mxu(place, terms.astype(BF), ((1,), (1,))).astype(BF)


def weights_kernel(taps, projection, jac, weight, w_m, w_n, p_t, p_j, g3):
    _, hidden, channels = taps.shape
    trim, padded = p_j.shape[0], p_t.shape[1]

    def shifted(rows, columns, by):
        return (lax.broadcasted_iota(jnp.int32, (rows, columns), 0) + by
                == lax.broadcasted_iota(jnp.int32, (rows, columns), 1)).astype(BF)

    wider, fuller = shifted(channels, padded, 0), shifted(channels, trim, 0)
    for b in range(3):
        total_m, total_n = 0.0, 0.0
        for a in range(3):
            tap = taps[3 * a + b]
            total_m = total_m + mxu(tap, shifted(channels, 3 * padded, a * padded))
            turned_tap = mxu(fuller, tap, ((0,), (1,))).astype(BF)
            total_n = total_n + mxu(turned_tap, shifted(hidden, 3 * hidden, (2 - a) * hidden))
        w_m[b * hidden : (b + 1) * hidden] = total_m.astype(BF)
        w_n[b * trim : (b + 1) * trim] = total_n.astype(BF)
    p_j[...] = mxu(fuller, projection[...], ((0,), (0,))).astype(BF)
    p_t[...] = mxu(projection[...], wider, ((0,), (0,))).astype(BF)
    tall = jnp.concatenate([jac[...], jnp.zeros((padded - channels, jac.shape[1]), F32)], axis=0)
    gram = mxu(tall * weight[...], tall, ((1,), (1,)), lax.Precision.HIGHEST)
    pulled = mxu(p_t[...].astype(F32), gram, precision=lax.Precision.HIGHEST)
    both = jnp.concatenate([gram[:trim], pulled], axis=0)
    hi = both.astype(BF)
    lo = (both - hi.astype(F32)).astype(BF)
    total = 0.0
    for k, value in enumerate((hi, lo, hi)):
        total = total + mxu(value, shifted(padded, 3 * padded, k * padded))
    g3[...] = total.astype(BF)


def turned(got, channels, padded):
    flat = got[...].astype(F32)
    turn = flat.T
    lat_row = turn[channels + 1 : channels + 2].astype(jnp.int32)
    lon_row = turn[channels + 2 : channels + 3].astype(jnp.int32)
    lat_col = flat[:, channels + 1 : channels + 2].astype(jnp.int32)
    lon_col = flat[:, channels + 2 : channels + 3].astype(jnp.int32)
    keep = lax.broadcasted_iota(jnp.int32, (padded, turn.shape[1]), 0) <= channels
    return jnp.where(keep, turn[:padded], 0.0), lat_row, lon_row, lat_col, lon_col


def edge_kernel(channels, height, got, _slope_north, _slope_south, north, south):
    tall, breadth = north.shape
    trim = tall // HALO
    slots = got.shape[0]
    turn, lat_row, _, _, lon = turned(got, channels, -(-trim // 16) * 16)
    values = turn.astype(BF)
    col_hot = (lax.broadcasted_iota(jnp.int32, (slots, breadth), 1) == lon).astype(BF)
    for out, first in ((north, 0), (south, height - HALO)):
        lhs = jnp.concatenate(
            [values * (lat_row == first + k).astype(F32).astype(BF) for k in range(HALO)], axis=0)
        rows = mxu(lhs, col_hot).reshape(HALO, values.shape[0], breadth)[:, :trim]
        out[...] = rows.reshape(tall, breadth).astype(BF)


def rows_of(message, padded):
    tall, breadth = message.shape
    rows = message[...].astype(F32).reshape(HALO, tall // HALO, breadth)
    if padded == tall // HALO:
        return rows
    return jnp.concatenate([rows, jnp.zeros((HALO, padded - tall // HALO, breadth), F32)], axis=1)


def side_kernel(channels, height, breadth, got, west, east):
    padded, strip = west.shape
    slots = got.shape[0]
    turn, _, _, lat, lon = turned(got, channels, padded)
    values = turn.astype(BF)
    for out, mask, col in (
        (west, lon < HALO, HALO + lon),
        (east, lon >= breadth - HALO, lon - (breadth - HALO)),
    ):
        target = jnp.where(mask, (lat + HALO) * SIDE + col, -1)
        hot = (lax.broadcasted_iota(jnp.int32, (slots, strip), 1) == target).astype(BF)
        out[...] = mxu(values, hot).astype(BF)


def grid_kernel(channels, got, out):
    height, trim, breadth = out.shape
    padded = -(-trim // 16) * 16
    slots = got.shape[0]
    turn, lat_row, _, _, lon = turned(got, channels, padded)
    values = turn.astype(BF)
    col_hot = (lax.broadcasted_iota(jnp.int32, (slots, breadth), 1) == lon).astype(BF)
    step = 8

    def body(block, _):
        lhs = jnp.concatenate(
            [values * (lat_row == block * step + k).astype(F32).astype(BF) for k in range(step)], axis=0)
        out[pl.ds(block * step, step)] = mxu(lhs, col_hot).reshape(step, padded, breadth)[:, :trim]
        return 0

    lax.fori_loop(0, height // step, body, 0)


def to_strip(rows, base, block):
    per = LANES // SIDE
    shape = (rows[0].shape[0], LANES)
    lane = lax.broadcasted_iota(jnp.int32, shape, 1)
    left, right = jnp.zeros(shape, F32), jnp.zeros(shape, F32)
    for k, row in enumerate(rows):
        at = base + k - block * per
        if not 0 <= at < per:
            continue
        row = row.astype(F32)
        by = (at * SIDE + HALO) % LANES
        mine = (lane >= at * SIDE) & (lane < (at + 1) * SIDE)
        left = jnp.where(mine & (lane % SIDE >= HALO), pltpu.roll(row[:, :LANES], by, 1), left)
        right = jnp.where(mine & (lane % SIDE < HALO), pltpu.roll(row[:, -LANES:], by, 1), right)
    return left, right


def strip_kernel(inner, north, south, west, east):
    height = inner.shape[0]
    rows = [north[k] for k in range(HALO)] + [inner[k] for k in range(height)] + [south[k] for k in range(HALO)]
    for block in range(west.shape[1] // LANES):
        left, right = to_strip(rows, 0, block)
        west[:, block * LANES : (block + 1) * LANES] = left.astype(BF)
        east[:, block * LANES : (block + 1) * LANES] = right.astype(BF)


def join_kernel(height, west, east, from_north, from_south, slope_west, slope_east, _token, to_west, to_east):
    padded, strip = west.shape
    last = (height + HALO) * SIDE // LANES
    above, below = rows_of(from_north, padded), rows_of(from_south, padded)
    above = to_strip([above[k] for k in range(HALO)], 0, 0)
    below = to_strip([below[k] for k in range(HALO)], HALO + height, last)
    for k, own, slope, out in ((0, west, slope_west, to_west), (1, east, slope_east, to_east)):
        for block in range(strip // LANES):
            part = pl.ds(block * LANES, LANES)
            q = own[:, part]
            if block == 0:
                q = q + above[k].astype(BF)
            if block == last:
                q = q + below[k].astype(BF)
            out[:padded, part] = q
        out[padded:] = slope[...]


def main_kernel(channels, hidden, cap, flags, got, inner, north, south, from_east, from_west, slope_inner,
                slope_north, slope_south, w_n, w_m, p_t, p_j, g3, first_out, second_out, reply,
                field, slope, ga, xb, vec, hi, found):
    height, trim, breadth = inner.shape
    padded = xb.shape[1]
    wide = breadth + LANES
    ext = height + 2 * HALO
    per = LANES // SIDE

    def is_in(i):
        above = (i >= HALO) | (flags[0] == 1)
        below = (i < height + HALO) | (flags[1] == 1)
        return (above & below).astype(F32)

    def join(parts):
        return jnp.concatenate(parts, axis=1)

    def part(x, k, lanes=wide):
        return x[:, k * lanes : (k + 1) * lanes]

    def fill(x):
        return jnp.concatenate([x, jnp.zeros((padded - trim, x.shape[1]), F32)], axis=0).astype(BF)

    def pull(i, ys):
        u = mxu(p_t[...], join([fill(y) for y in ys]))
        for k in range(len(ys)):
            ga[i + k] = (slope[i + k].astype(F32) * part(u, k)).astype(BF)

    lane = lax.broadcasted_iota(jnp.int32, (padded + hidden, LANES), 1)
    from_the_west = lane % SIDE < HALO

    def begin(i, mains, slopes):
        ys = []
        for k in range(len(mains)):
            if k % HALO == 0:
                at = pl.ds(pl.multiple_of((i + k) // per * LANES, LANES), LANES)
                both = jnp.where(from_the_west, from_west[:, at].astype(F32), from_east[:, at].astype(F32))
            shift = 2 * LANES - (i + k) % per * SIDE - HALO
            edge = pltpu.roll(both, shift % LANES, 1)
            y = join([mains[k].astype(F32), edge[:trim]])
            field[i + k] = y
            slope[i + k] = join([slopes[k], edge[padded:].astype(BF)])
            ys.append(y)
        pull(i, ys)

    above, below = rows_of(north, trim), rows_of(south, trim)
    begin(0, [above[k] for k in range(HALO)], [slope_north[k] for k in range(HALO)])
    begin(HALO + height, [below[k] for k in range(HALO)], [slope_south[k] for k in range(HALO)])

    def middle(n, _):
        i = n * G[5]
        begin(i + HALO, [inner[i + k] for k in range(G[5])], [slope_inner[i + k] for k in range(G[5])])
        return 0

    lax.fori_loop(0, height // G[5], middle, 0)

    def spread(i, ys):
        o = mxu(w_n[...], join([ga[pl.ds(i + k - 1, 3)].reshape(3 * hidden, wide) for k in range(len(ys))]))
        out = []
        for k, y in enumerate(ys):
            p = part(o, k)
            out.append(y + p[trim : 2 * trim] + pltpu.roll(p[:trim], wide - 1, 1)
                       + pltpu.roll(p[2 * trim :], 1, 1))
        return out

    def tangent(i, vs):
        lanes = vs[0].shape[1]
        o = mxu(w_m[...], join([xb[pl.ds(i + k - 1, 3)].reshape(3 * padded, wide) for k in range(len(vs))]))
        acts = []
        for k in range(len(vs)):
            p = part(o, k)
            h = (p[hidden : 2 * hidden] + pltpu.roll(p[:hidden], 1, 1)
                 + pltpu.roll(p[2 * hidden :], wide - 1, 1))
            acts.append((slope[i + k].astype(F32) * h).astype(BF)[:, :lanes])
        back = mxu(p_j[...], join(acts))
        return [v + part(back, k, lanes) for k, v in enumerate(vs)]

    def gram_of(s, matrix):
        s_hi = s.astype(BF).astype(F32)
        s_lo = fill(s - s_hi)
        s_hi = fill(s_hi)
        return mxu(matrix, jnp.concatenate([s_hi, s_hi, s_lo], axis=0))

    def loop(first, last, size, body):
        assert (last - first) % size == 0

        def step(n, _):
            body(first + n * size)
            return 0

        lax.fori_loop(0, (last - first) // size, step, 0)

    def n_first(i):
        for k, v in enumerate(spread(i, [field[i + k] for k in range(G[0])])):
            first_out[i + k] = v[:, :breadth]
            vec[i + k] = v[:, breadth:]
            xb[i + k] = fill(v * is_in(i + k))

    loop(1, ext - 1, G[0], n_first)

    def m_first(i):
        ss = tangent(i, [join([first_out[i + k], vec[i + k]]) for k in range(G[1])])
        gs = gram_of(join(ss), g3[...])
        for k, s in enumerate(ss):
            cell_weight = field[i + k][channels : channels + 1]
            both = part(gs, k)
            hi[i + k, :padded] = fill(s[:, :breadth])
            field[i + k] = cell_weight * both[:trim]
            ga[i + k] = (slope[i + k].astype(F32) * (cell_weight * both[trim:])).astype(BF)

    loop(2, ext - 2, G[1], m_first)

    def n_second(i):
        for k, v in enumerate(spread(i, [field[i + k] for k in range(G[2])])):
            second_out[i + k] = v[:, :breadth]
            xb[i + k] = fill(v * is_in(i + k))

    loop(3, ext - 3, G[2], n_second)

    def m_second(i):
        for k, s in enumerate(tangent(i, [second_out[i + k] for k in range(G[3])])):
            hi[i + k, padded:] = fill(s)

    loop(HALO, ext - HALO, G[3], m_second)

    turn, lat_row, lon_row, _, _ = turned(got, channels, padded)
    slots = got.shape[0]
    piece = 256
    for c in range(slots // piece):
        here = slice(c * piece, (c + 1) * piece)
        col_hot = (lax.broadcasted_iota(jnp.int32, (breadth, piece), 0) == lon_row[:, here]).astype(BF)
        found[:, here] = jnp.zeros((2 * padded, piece), F32)

        def gather(i, col_hot=col_hot, here=here):
            out = mxu(hi[pl.ds(i, G[4])].reshape(G[4] * 2 * padded, breadth), col_hot)
            total = found[:, here]
            for k in range(G[4]):
                mine = (lat_row[:, here] == i + k - HALO)
                total = total + jnp.where(mine, out[k * 2 * padded : (k + 1) * 2 * padded], 0.0)
            found[:, here] = total

        loop(HALO, ext - HALO, G[4], gather)

    row0, row1 = found[:trim], found[padded : padded + trim]
    weight = turn[channels : channels + 1]
    curved0 = gram_of(row0, g3[:trim]) * weight
    curved1 = gram_of(row1, g3[:trim]) * weight
    real = lax.broadcasted_iota(jnp.int32, (trim, slots), 0) < channels
    first = jnp.where(real, turn[:trim], 0.0)

    def total(x):
        return jnp.sum(jnp.sum(x, axis=0, keepdims=True), axis=1, keepdims=True)

    sums = (total(first * row0), total(curved0 * row0), total(curved0 * row1), total(curved1 * row1))
    lane = lax.broadcasted_iota(jnp.int32, (1, LANES), 1)
    pieces = jnp.zeros((1, LANES), F32)
    for number, value in enumerate(sums):
        for third, piece in enumerate(split3(value)):
            pieces = jnp.where(lane == 3 * number + third, piece.astype(F32), pieces)
    size = reply.shape[0] * cap // slots
    slot = lax.broadcasted_iota(jnp.int32, (1, slots), 1)
    near, far, turn_of = reply_rows(slot, cap, size)
    start = jnp.concatenate([row0, row1[: LANES - trim]], axis=0).astype(BF)
    end = jnp.concatenate([row1[LANES - trim :]] * GROUP, axis=0)
    tail = LANES // GROUP
    end = jnp.where(lax.broadcasted_iota(jnp.int32, (LANES, slots), 0) // tail == turn_of, end, 0.0).astype(BF)
    at = lax.broadcasted_iota(jnp.int32, (reply.shape[0], slots), 0)
    packed = mxu((at == near).astype(BF), start, ((1,), (1,))) + mxu((at == far).astype(BF), end, ((1,), (1,)))
    row = lax.broadcasted_iota(jnp.int32, reply.shape, 0)
    reply[...] = jnp.where(row % size == size - 1, pieces, packed).astype(BF)


def reply_rows(slot, cap, size):
    block = slot // cap
    inside = slot - block * cap
    return block * size + inside, block * size + cap + inside // GROUP, inside % GROUP


def scalars(reply, size):
    row = lax.broadcasted_iota(jnp.int32, reply.shape, 0)
    sums = jnp.sum(jnp.where(row % size == size - 1, reply[...].astype(F32), 0.0), axis=0, keepdims=True)

    def value(number):
        at = 3 * number
        return sums[:, at : at + 1] + sums[:, at + 1 : at + 2] + sums[:, at + 2 : at + 3]

    a00, a01, a11, d11 = (value(n) for n in range(4))
    step0 = a00 / (a00 + a01)
    keep = 1.0 - step0
    norm1 = keep * keep * a00 - 2.0 * step0 * keep * a01 + step0 * step0 * a11
    c0 = keep + norm1 / a00
    c1 = -step0
    curve = (c0 * c0 * (a00 + a01) + 2.0 * c0 * c1 * (a01 + a11) + c1 * c1 * (a11 + d11))
    step1 = norm1 / curve
    return step0 + step1 * c0, step1 * c1


def final_kernel(channels, cap, size, back, slot, dep, jac, first, second, increment, departures, mixed, sems):
    rows = dep.shape[0]
    height = mixed.shape[0]
    a, b = scalars(back, size)

    def copy(i):
        return pltpu.make_async_copy(mixed.at[i], increment.at[:, i], sems.at[i])

    for i in range(height):
        mixed[i] = a * first[i + HALO, :channels] + b * second[i + HALO, :channels]
        copy(i).start()
    near, far, turn_of = reply_rows(slot[...], cap, size)
    at = lax.broadcasted_iota(jnp.int32, (back.shape[0], rows), 0)
    start = mxu(back[...], (at == near).astype(BF), ((0,), (0,)))
    end = mxu(back[...], (at == far).astype(BF), ((0,), (0,)))
    tail = LANES // GROUP
    end = jnp.where(lax.broadcasted_iota(jnp.int32, (LANES, rows), 0) // tail == turn_of, end, 0.0)
    end = functools.reduce(jnp.add, [end[k * tail : (k + 1) * tail] for k in range(GROUP)])
    trim = first.shape[1]
    state = a * start[:trim] + b * jnp.concatenate([start[trim:], end], axis=0)
    departures[...] = dep[...] - mxu(state[:channels], jac[...], ((0,), (0,)), lax.Precision.HIGHEST)
    for i in range(height):
        copy(i).wait()


def shift2(x, by_lat, by_lon):
    n_lat, n_lon = lax.axis_size("lat"), lax.axis_size("lon")
    pairs = [(i * n_lon + j, (i + by_lat) * n_lon + (j + by_lon) % n_lon)
             for i in range(n_lat) for j in range(n_lon) if 0 <= i + by_lat < n_lat]
    return lax.ppermute(x, ("lat", "lon"), pairs)


def on_device(departure_in, obs_owner, obs_cell, obs_count, qc_mask, channel_weight, jacobian,
              conv_taps, projection, slope):
    channels, hidden = projection.shape
    height, breadth = slope.shape[1], slope.shape[2]
    tiles = lax.axis_size(("lat", "lon"))
    rows, radiances = departure_in.shape
    cap = max(2, 3 * rows // (2 * tiles))
    slots = tiles * cap
    padded = -(-(channels + 1) // 16) * 16
    trim = -(-(channels + 1) // 8) * 8
    assert 2 * trim == LANES + LANES // GROUP
    size = -(-(cap + -(-cap // GROUP) + 1) // 8) * 8
    wide = breadth + LANES
    ext = height + 2 * HALO
    strip = -(-(ext * SIDE) // LANES) * LANES

    def shape(dims, kind=F32):
        return jax.ShapeDtypeStruct(dims, kind)

    weight = channel_weight[None, :]
    send, slot = call(
        functools.partial(pack_kernel, tiles, cap, breadth, channels),
        (shape((slots, LANES), BF), shape((1, rows), jnp.int32)),
        (obs_count, departure_in, jnp.stack([obs_owner[:, 0], obs_cell, qc_mask]),
         jnp.concatenate([jacobian, weight], axis=0)),
        smem=1,
    )

    def swap(x):
        return lax.all_to_all(x.reshape(tiles, -1, LANES), ("lat", "lon"), split_axis=0, concat_axis=0,
                              tiled=True).reshape(x.shape)

    got = swap(send)

    w_m, w_n, p_t, p_j, g3 = call(
        weights_kernel,
        (shape((3 * hidden, 3 * padded), BF), shape((3 * trim, 3 * hidden), BF), shape((hidden, padded), BF),
         shape((trim, hidden), BF), shape((trim + hidden, 3 * padded), BF)),
        (conv_taps, projection, jacobian, weight),
        staged=True,
    )

    slope_inner = jnp.transpose(slope, (1, 0, 2))
    low, high = lax.optimization_barrier((slope[:, -HALO:], slope[:, :HALO]))
    slope_north = shift2(jnp.transpose(low, (1, 0, 2)), 1, 0)
    slope_south = shift2(jnp.transpose(high, (1, 0, 2)), -1, 0)
    slope_west, slope_east = call(strip_kernel, (shape((hidden, strip), BF),) * 2,
                                  (slope_inner, slope_north, slope_south))

    north, south = call(
        functools.partial(edge_kernel, channels, height),
        (shape((HALO * trim, breadth), BF),) * 2,
        (got, slope_north, slope_south),
        unread=2,
    )
    from_south = shift2(north, -1, 0)
    from_north = shift2(south, 1, 0)
    west, east = call(
        functools.partial(side_kernel, channels, height, breadth), (shape((padded, strip), BF),) * 2, (got,))
    to_west, to_east = call(
        functools.partial(join_kernel, height),
        (shape((padded + hidden, strip), BF),) * 2,
        (west, east, from_north, from_south, slope_west, slope_east, p_t),
        unread=1,
    )
    from_east = shift2(to_west, 0, -1)
    from_west = shift2(to_east, 0, 1)
    inner = call(functools.partial(grid_kernel, channels), shape((height, trim, breadth)), (got,))

    at = lax.axis_index("lat")
    flags = jnp.stack([at > 0, at < lax.axis_size("lat") - 1]).astype(jnp.int32)
    first, second, reply = call(
        functools.partial(main_kernel, channels, hidden, cap),
        (shape((ext, trim, breadth)),) * 2 + (shape((tiles * size, LANES), BF),),
        (flags, got, inner, from_north, from_south, from_east, from_west, slope_inner, slope_north,
         slope_south, w_n, w_m, p_t, p_j, g3),
        scratch=[
            pltpu.VMEM((ext, trim, wide), F32),
            pltpu.VMEM((ext, hidden, wide), BF),
            pltpu.VMEM((ext, hidden, wide), BF),
            pltpu.VMEM((ext, padded, wide), BF),
            pltpu.VMEM((ext, trim, LANES), F32),
            pltpu.VMEM((ext, 2 * padded, breadth), BF),
            pltpu.VMEM((2 * padded, slots), F32),
        ],
        smem=1,
        vmem=76,
    )
    back = swap(reply)
    return call(
        functools.partial(final_kernel, channels, cap, size),
        (shape((channels, height, breadth)), shape((rows, radiances))),
        (back, slot, departure_in, jacobian, first, second),
        scratch=[pltpu.VMEM((height, channels, breadth), F32), pltpu.SemaphoreType.DMA((height,))],
        away=(0,),
        vmem=32,
    )


def solution(mesh):
    placed = (
        P(("lat", "lon"), None),
        P(("lat", "lon"), None),
        P(("lat", "lon")),
        P(("lat", "lon")),
        P(("lat", "lon")),
        P(),
        P(),
        P(),
        P(),
        P(None, "lat", "lon"),
    )
    return jax.shard_map(
        on_device,
        mesh=mesh,
        in_specs=placed,
        out_specs=(P(None, "lat", "lon"), P(("lat", "lon"), None)),
        check_vma=False,
    )
```

```python
import functools

import jax
import jax.numpy as jnp
import numpy as np
from jax import lax
from jax.experimental import pallas as pl
from jax.experimental.pallas import tpu as pltpu
from jax.sharding import PartitionSpec as P

ITERS = 2
HALO = 4
LANES = 128
GROUP = 8
SIDE = 2 * HALO
BF = jnp.bfloat16
F32 = jnp.float32
INTERPRET = False
G = (18, 26, 25, 24, 24, 24)


def mxu(a, b, dims=((1,), (0,)), precision=None):
    return lax.dot_general(a, b, (dims, ((), ())), precision=precision, preferred_element_type=F32)


def call(kernel, outs, args, scratch=(), smem=0, vmem=24, unread=0, staged=False, away=()):
    def space(i, x):
        if i < smem:
            return pl.BlockSpec(memory_space=pltpu.SMEM)
        if i >= len(args) - unread:
            return pl.BlockSpec(memory_space=pl.ANY)
        if staged:
            return pl.BlockSpec(x.shape, lambda _: (0,) * x.ndim)
        return pl.BlockSpec(memory_space=pltpu.VMEM)

    leaves, tree = jax.tree.flatten(outs)
    out_specs = [pl.BlockSpec(memory_space=pl.ANY if i in away else pltpu.VMEM) for i in range(len(leaves))]
    return pl.pallas_call(
        kernel,
        out_shape=outs,
        grid=(1,) if staged else (),
        in_specs=[space(i, x) for i, x in enumerate(args)],
        out_specs=jax.tree.unflatten(tree, out_specs),
        scratch_shapes=scratch,
        interpret=INTERPRET,
        compiler_params=pltpu.CompilerParams(vmem_limit_bytes=vmem * 2**20 // 2),
    )(*args)


def split3(x):
    hi = x.astype(BF)
    rest = x - hi.astype(F32)
    mid = rest.astype(BF)
    return hi, mid, (rest - mid.astype(F32)).astype(BF)


def pack_kernel(tiles, cap, lon_size, channels, count, meta, table, send, slot_out):
    owner_row, cell_row, qc_row = meta[0:1], meta[1:2], meta[2:3]
    rows = meta.shape[1]
    dep, jac, weight = table[:rows], table[rows : rows + channels], table[rows + channels :]
    slots = send.shape[0]
    hit = (lax.broadcasted_iota(jnp.int32, (tiles, rows), 0) == owner_row).astype(BF)
    before = (lax.broadcasted_iota(jnp.int32, (rows, rows), 0)
              < lax.broadcasted_iota(jnp.int32, (rows, rows), 1)).astype(BF)
    earlier = mxu(hit, before)
    rank = jnp.sum(earlier * hit.astype(F32), axis=0, keepdims=True)
    slot = owner_row * cap + rank.astype(jnp.int32)
    slot_out[...] = slot
    place = (lax.broadcasted_iota(jnp.int32, (slots, rows), 0) == slot).astype(BF)

    used = (lax.broadcasted_iota(jnp.int32, (1, rows), 1) < count[0]).astype(F32)
    row_weight = used * qc_row.astype(F32)
    terms = mxu(jac, dep * weight, ((1,), (1,)), lax.Precision.HIGHEST) * row_weight
    lat = cell_row // lon_size
    lon = cell_row - lat * lon_size
    wide = lax.broadcasted_iota(jnp.int32, (LANES, rows), 0)
    terms = jnp.concatenate([terms, jnp.zeros((LANES - channels, rows), F32)], axis=0)
    terms = jnp.where(wide == channels, row_weight, terms)
    terms = jnp.where(wide == channels + 1, lat.astype(F32), terms)
    terms = jnp.where(wide == channels + 2, lon.astype(F32), terms)
    send[...] = mxu(place, terms.astype(BF), ((1,), (1,))).astype(BF)


def weights_kernel(taps, projection, jac, weight, w_m, w_n, p_t, p_j, g3):
    _, hidden, channels = taps.shape
    trim, padded = p_j.shape[0], p_t.shape[1]

    def shifted(rows, columns, by):
        return (lax.broadcasted_iota(jnp.int32, (rows, columns), 0) + by
                == lax.broadcasted_iota(jnp.int32, (rows, columns), 1)).astype(BF)

    wider, fuller = shifted(channels, padded, 0), shifted(channels, trim, 0)
    for b in range(3):
        total_m, total_n = 0.0, 0.0
        for a in range(3):
            tap = taps[3 * a + b]
            total_m = total_m + mxu(tap, shifted(channels, 3 * padded, a * padded))
            turned_tap = mxu(fuller, tap, ((0,), (1,))).astype(BF)
            total_n = total_n + mxu(turned_tap, shifted(hidden, 3 * hidden, (2 - a) * hidden))
        w_m[b * hidden : (b + 1) * hidden] = total_m.astype(BF)
        w_n[b * trim : (b + 1) * trim] = total_n.astype(BF)
    p_j[...] = mxu(fuller, projection[...], ((0,), (0,))).astype(BF)
    p_t[...] = mxu(projection[...], wider, ((0,), (0,))).astype(BF)
    tall = jnp.concatenate([jac[...], jnp.zeros((padded - channels, jac.shape[1]), F32)], axis=0)
    gram = mxu(tall * weight[...], tall, ((1,), (1,)), lax.Precision.HIGHEST)
    pulled = mxu(p_t[...].astype(F32), gram, precision=lax.Precision.HIGHEST)
    both = jnp.concatenate([gram[:trim], pulled], axis=0)
    hi = both.astype(BF)
    lo = (both - hi.astype(F32)).astype(BF)
    total = 0.0
    for k, value in enumerate((hi, lo, hi)):
        total = total + mxu(value, shifted(padded, 3 * padded, k * padded))
    g3[...] = total.astype(BF)


def turned(got, channels, padded):
    flat = got[...].astype(F32)
    turn = flat.T
    lat_row = turn[channels + 1 : channels + 2].astype(jnp.int32)
    lon_row = turn[channels + 2 : channels + 3].astype(jnp.int32)
    lat_col = flat[:, channels + 1 : channels + 2].astype(jnp.int32)
    lon_col = flat[:, channels + 2 : channels + 3].astype(jnp.int32)
    keep = lax.broadcasted_iota(jnp.int32, (padded, turn.shape[1]), 0) <= channels
    return jnp.where(keep, turn[:padded], 0.0), lat_row, lon_row, lat_col, lon_col


def edge_kernel(channels, height, got, north, south):
    tall, breadth = north.shape
    trim = tall // HALO
    slots = got.shape[0]
    turn, lat_row, _, _, lon = turned(got, channels, -(-trim // 16) * 16)
    values = turn.astype(BF)
    col_hot = (lax.broadcasted_iota(jnp.int32, (slots, breadth), 1) == lon).astype(BF)
    for out, first in ((north, 0), (south, height - HALO)):
        lhs = jnp.concatenate(
            [values * (lat_row == first + k).astype(F32).astype(BF) for k in range(HALO)], axis=0)
        rows = mxu(lhs, col_hot).reshape(HALO, values.shape[0], breadth)[:, :trim]
        out[...] = rows.reshape(tall, breadth).astype(BF)


def rows_of(message, padded):
    tall, breadth = message.shape
    rows = message[...].astype(F32).reshape(HALO, tall // HALO, breadth)
    if padded == tall // HALO:
        return rows
    return jnp.concatenate([rows, jnp.zeros((HALO, padded - tall // HALO, breadth), F32)], axis=1)


def side_kernel(channels, height, breadth, got, west, east):
    padded, strip = west.shape
    slots = got.shape[0]
    turn, _, _, lat, lon = turned(got, channels, padded)
    values = turn.astype(BF)
    for out, mask, col in (
        (west, lon < HALO, HALO + lon),
        (east, lon >= breadth - HALO, lon - (breadth - HALO)),
    ):
        target = jnp.where(mask, (lat + HALO) * SIDE + col, -1)
        hot = (lax.broadcasted_iota(jnp.int32, (slots, strip), 1) == target).astype(BF)
        out[...] = mxu(values, hot).astype(BF)


def grid_kernel(channels, got, out):
    height, trim, breadth = out.shape
    padded = -(-trim // 16) * 16
    slots = got.shape[0]
    turn, lat_row, _, _, lon = turned(got, channels, padded)
    values = turn.astype(BF)
    col_hot = (lax.broadcasted_iota(jnp.int32, (slots, breadth), 1) == lon).astype(BF)
    step = 8

    def body(block, _):
        lhs = jnp.concatenate(
            [values * (lat_row == block * step + k).astype(F32).astype(BF) for k in range(step)], axis=0)
        out[pl.ds(block * step, step)] = mxu(lhs, col_hot).reshape(step, padded, breadth)[:, :trim]
        return 0

    lax.fori_loop(0, height // step, body, 0)


def to_strip(rows, base, block):
    per = LANES // SIDE
    shape = (rows[0].shape[0], LANES)
    lane = lax.broadcasted_iota(jnp.int32, shape, 1)
    left, right = jnp.zeros(shape, F32), jnp.zeros(shape, F32)
    for k, row in enumerate(rows):
        at = base + k - block * per
        if not 0 <= at < per:
            continue
        row = row.astype(F32)
        by = (at * SIDE + HALO) % LANES
        mine = (lane >= at * SIDE) & (lane < (at + 1) * SIDE)
        left = jnp.where(mine & (lane % SIDE >= HALO), pltpu.roll(row[:, :LANES], by, 1), left)
        right = jnp.where(mine & (lane % SIDE < HALO), pltpu.roll(row[:, -LANES:], by, 1), right)
    return left, right


def strip_kernel(inner, north, south, west, east):
    height = inner.shape[0]
    rows = [north[k] for k in range(HALO)] + [inner[k] for k in range(height)] + [south[k] for k in range(HALO)]
    for block in range(west.shape[1] // LANES):
        left, right = to_strip(rows, 0, block)
        west[:, block * LANES : (block + 1) * LANES] = left.astype(BF)
        east[:, block * LANES : (block + 1) * LANES] = right.astype(BF)


def join_kernel(height, west, east, from_north, from_south, slope_west, slope_east, _token, to_west, to_east):
    padded, strip = west.shape
    last = (height + HALO) * SIDE // LANES
    above, below = rows_of(from_north, padded), rows_of(from_south, padded)
    above = to_strip([above[k] for k in range(HALO)], 0, 0)
    below = to_strip([below[k] for k in range(HALO)], HALO + height, last)
    for k, own, slope, out in ((0, west, slope_west, to_west), (1, east, slope_east, to_east)):
        for block in range(strip // LANES):
            part = pl.ds(block * LANES, LANES)
            q = own[:, part]
            if block == 0:
                q = q + above[k].astype(BF)
            if block == last:
                q = q + below[k].astype(BF)
            out[:padded, part] = q
        out[padded:] = slope[...]


def main_kernel(channels, hidden, cap, flags, got, inner, north, south, from_east, from_west, slope_inner,
                slope_north, slope_south, w_n, w_m, p_t, p_j, g3, first_out, second_out, reply,
                field, slope, ga, xb, vec, hi, found):
    height, trim, breadth = inner.shape
    padded = xb.shape[1]
    wide = breadth + LANES
    ext = height + 2 * HALO
    per = LANES // SIDE

    def is_in(i):
        above = (i >= HALO) | (flags[0] == 1)
        below = (i < height + HALO) | (flags[1] == 1)
        return (above & below).astype(F32)

    def join(parts):
        return jnp.concatenate(parts, axis=1)

    def part(x, k, lanes=wide):
        return x[:, k * lanes : (k + 1) * lanes]

    def fill(x):
        return jnp.concatenate([x, jnp.zeros((padded - trim, x.shape[1]), F32)], axis=0).astype(BF)

    def pull(i, ys):
        u = mxu(p_t[...], join([fill(y) for y in ys]))
        for k in range(len(ys)):
            ga[i + k] = (slope[i + k].astype(F32) * part(u, k)).astype(BF)

    lane = lax.broadcasted_iota(jnp.int32, (padded + hidden, LANES), 1)
    from_the_west = lane % SIDE < HALO

    def begin(i, mains, slopes):
        ys = []
        for k in range(len(mains)):
            if k % HALO == 0:
                at = pl.ds(pl.multiple_of((i + k) // per * LANES, LANES), LANES)
                both = jnp.where(from_the_west, from_west[:, at].astype(F32), from_east[:, at].astype(F32))
            shift = 2 * LANES - (i + k) % per * SIDE - HALO
            edge = pltpu.roll(both, shift % LANES, 1)
            y = join([mains[k].astype(F32), edge[:trim]])
            field[i + k] = y
            slope[i + k] = join([slopes[k], edge[padded:].astype(BF)])
            ys.append(y)
        pull(i, ys)

    above, below = rows_of(north, trim), rows_of(south, trim)
    begin(0, [above[k] for k in range(HALO)], [slope_north[k] for k in range(HALO)])
    begin(HALO + height, [below[k] for k in range(HALO)], [slope_south[k] for k in range(HALO)])

    def middle(n, _):
        i = n * G[5]
        begin(i + HALO, [inner[i + k] for k in range(G[5])], [slope_inner[i + k] for k in range(G[5])])
        return 0

    lax.fori_loop(0, height // G[5], middle, 0)

    def spread(i, ys):
        o = mxu(w_n[...], join([ga[pl.ds(i + k - 1, 3)].reshape(3 * hidden, wide) for k in range(len(ys))]))
        out = []
        for k, y in enumerate(ys):
            p = part(o, k)
            out.append(y + p[trim : 2 * trim] + pltpu.roll(p[:trim], wide - 1, 1)
                       + pltpu.roll(p[2 * trim :], 1, 1))
        return out

    def tangent(i, vs):
        lanes = vs[0].shape[1]
        o = mxu(w_m[...], join([xb[pl.ds(i + k - 1, 3)].reshape(3 * padded, wide) for k in range(len(vs))]))
        acts = []
        for k in range(len(vs)):
            p = part(o, k)
            h = (p[hidden : 2 * hidden] + pltpu.roll(p[:hidden], 1, 1)
                 + pltpu.roll(p[2 * hidden :], wide - 1, 1))
            acts.append((slope[i + k].astype(F32) * h).astype(BF)[:, :lanes])
        back = mxu(p_j[...], join(acts))
        return [v + part(back, k, lanes) for k, v in enumerate(vs)]

    def gram_of(s, matrix):
        s_hi = s.astype(BF).astype(F32)
        s_lo = fill(s - s_hi)
        s_hi = fill(s_hi)
        return mxu(matrix, jnp.concatenate([s_hi, s_hi, s_lo], axis=0))

    def loop(first, last, size, body):
        assert (last - first) % size == 0

        def step(n, _):
            body(first + n * size)
            return 0

        lax.fori_loop(0, (last - first) // size, step, 0)

    def n_first(i):
        for k, v in enumerate(spread(i, [field[i + k] for k in range(G[0])])):
            first_out[i + k] = v[:, :breadth]
            vec[i + k] = v[:, breadth:]
            xb[i + k] = fill(v * is_in(i + k))

    loop(1, ext - 1, G[0], n_first)

    def m_first(i):
        ss = tangent(i, [join([first_out[i + k], vec[i + k]]) for k in range(G[1])])
        gs = gram_of(join(ss), g3[...])
        for k, s in enumerate(ss):
            cell_weight = field[i + k][channels : channels + 1]
            both = part(gs, k)
            hi[i + k, :padded] = fill(s[:, :breadth])
            field[i + k] = cell_weight * both[:trim]
            ga[i + k] = (slope[i + k].astype(F32) * (cell_weight * both[trim:])).astype(BF)

    loop(2, ext - 2, G[1], m_first)

    def n_second(i):
        for k, v in enumerate(spread(i, [field[i + k] for k in range(G[2])])):
            second_out[i + k] = v[:, :breadth]
            xb[i + k] = fill(v * is_in(i + k))

    loop(3, ext - 3, G[2], n_second)

    def m_second(i):
        for k, s in enumerate(tangent(i, [second_out[i + k] for k in range(G[3])])):
            hi[i + k, padded:] = fill(s)

    loop(HALO, ext - HALO, G[3], m_second)

    turn, lat_row, lon_row, _, _ = turned(got, channels, padded)
    slots = got.shape[0]
    piece = 256
    for c in range(slots // piece):
        here = slice(c * piece, (c + 1) * piece)
        col_hot = (lax.broadcasted_iota(jnp.int32, (breadth, piece), 0) == lon_row[:, here]).astype(BF)
        found[:, here] = jnp.zeros((2 * padded, piece), F32)

        def gather(i, col_hot=col_hot, here=here):
            out = mxu(hi[pl.ds(i, G[4])].reshape(G[4] * 2 * padded, breadth), col_hot)
            total = found[:, here]
            for k in range(G[4]):
                mine = (lat_row[:, here] == i + k - HALO)
                total = total + jnp.where(mine, out[k * 2 * padded : (k + 1) * 2 * padded], 0.0)
            found[:, here] = total

        loop(HALO, ext - HALO, G[4], gather)

    row0, row1 = found[:trim], found[padded : padded + trim]
    weight = turn[channels : channels + 1]
    curved0 = gram_of(row0, g3[:trim]) * weight
    curved1 = gram_of(row1, g3[:trim]) * weight
    real = lax.broadcasted_iota(jnp.int32, (trim, slots), 0) < channels
    first = jnp.where(real, turn[:trim], 0.0)

    def total(x):
        return jnp.sum(jnp.sum(x, axis=0, keepdims=True), axis=1, keepdims=True)

    sums = (total(first * row0), total(curved0 * row0), total(curved0 * row1), total(curved1 * row1))
    lane = lax.broadcasted_iota(jnp.int32, (1, LANES), 1)
    pieces = jnp.zeros((1, LANES), F32)
    for number, value in enumerate(sums):
        for third, piece in enumerate(split3(value)):
            pieces = jnp.where(lane == 3 * number + third, piece.astype(F32), pieces)
    size = reply.shape[0] * cap // slots
    slot = lax.broadcasted_iota(jnp.int32, (1, slots), 1)
    near, far, turn_of = reply_rows(slot, cap, size)
    start = jnp.concatenate([row0, row1[: LANES - trim]], axis=0).astype(BF)
    end = jnp.concatenate([row1[LANES - trim :]] * GROUP, axis=0)
    tail = LANES // GROUP
    end = jnp.where(lax.broadcasted_iota(jnp.int32, (LANES, slots), 0) // tail == turn_of, end, 0.0).astype(BF)
    at = lax.broadcasted_iota(jnp.int32, (reply.shape[0], slots), 0)
    packed = mxu((at == near).astype(BF), start, ((1,), (1,))) + mxu((at == far).astype(BF), end, ((1,), (1,)))
    row = lax.broadcasted_iota(jnp.int32, reply.shape, 0)
    reply[...] = jnp.where(row % size == size - 1, pieces, packed).astype(BF)


def reply_rows(slot, cap, size):
    block = slot // cap
    inside = slot - block * cap
    return block * size + inside, block * size + cap + inside // GROUP, inside % GROUP


def scalars(reply, size):
    row = lax.broadcasted_iota(jnp.int32, reply.shape, 0)
    sums = jnp.sum(jnp.where(row % size == size - 1, reply[...].astype(F32), 0.0), axis=0, keepdims=True)

    def value(number):
        at = 3 * number
        return sums[:, at : at + 1] + sums[:, at + 1 : at + 2] + sums[:, at + 2 : at + 3]

    a00, a01, a11, d11 = (value(n) for n in range(4))
    step0 = a00 / (a00 + a01)
    keep = 1.0 - step0
    norm1 = keep * keep * a00 - 2.0 * step0 * keep * a01 + step0 * step0 * a11
    c0 = keep + norm1 / a00
    c1 = -step0
    curve = (c0 * c0 * (a00 + a01) + 2.0 * c0 * c1 * (a01 + a11) + c1 * c1 * (a11 + d11))
    step1 = norm1 / curve
    return step0 + step1 * c0, step1 * c1


def final_kernel(channels, cap, size, back, slot, dep, jac, first, second, increment, departures, mixed, sems):
    rows = dep.shape[0]
    height = mixed.shape[0]
    a, b = scalars(back, size)

    def copy(i):
        return pltpu.make_async_copy(mixed.at[i], increment.at[:, i], sems.at[i])

    for i in range(height):
        mixed[i] = a * first[i + HALO, :channels] + b * second[i + HALO, :channels]
        copy(i).start()
    near, far, turn_of = reply_rows(slot[...], cap, size)
    at = lax.broadcasted_iota(jnp.int32, (back.shape[0], rows), 0)
    start = mxu(back[...], (at == near).astype(BF), ((0,), (0,)))
    end = mxu(back[...], (at == far).astype(BF), ((0,), (0,)))
    tail = LANES // GROUP
    end = jnp.where(lax.broadcasted_iota(jnp.int32, (LANES, rows), 0) // tail == turn_of, end, 0.0)
    end = functools.reduce(jnp.add, [end[k * tail : (k + 1) * tail] for k in range(GROUP)])
    trim = first.shape[1]
    state = a * start[:trim] + b * jnp.concatenate([start[trim:], end], axis=0)
    departures[...] = dep[...] - mxu(state[:channels], jac[...], ((0,), (0,)), lax.Precision.HIGHEST)
    for i in range(height):
        copy(i).wait()


def shift2(x, by_lat, by_lon):
    n_lat, n_lon = lax.axis_size("lat"), lax.axis_size("lon")
    pairs = [(i * n_lon + j, (i + by_lat) * n_lon + (j + by_lon) % n_lon)
             for i in range(n_lat) for j in range(n_lon) if 0 <= i + by_lat < n_lat]
    return lax.ppermute(x, ("lat", "lon"), pairs)


def on_device(departure_in, obs_owner, obs_cell, obs_count, qc_mask, channel_weight, jacobian,
              conv_taps, projection, slope):
    channels, hidden = projection.shape
    height, breadth = slope.shape[1], slope.shape[2]
    tiles = lax.axis_size(("lat", "lon"))
    rows, radiances = departure_in.shape
    cap = max(2, 3 * rows // (2 * tiles))
    slots = tiles * cap
    padded = -(-(channels + 1) // 16) * 16
    trim = -(-(channels + 1) // 8) * 8
    assert 2 * trim == LANES + LANES // GROUP
    size = -(-(cap + -(-cap // GROUP) + 1) // 8) * 8
    wide = breadth + LANES
    ext = height + 2 * HALO
    strip = -(-(ext * SIDE) // LANES) * LANES

    def shape(dims, kind=F32):
        return jax.ShapeDtypeStruct(dims, kind)

    weight = channel_weight[None, :]
    send, slot = call(
        functools.partial(pack_kernel, tiles, cap, breadth, channels),
        (shape((slots, LANES), BF), shape((1, rows), jnp.int32)),
        (obs_count, jnp.stack([obs_owner[:, 0], obs_cell, qc_mask]),
         jnp.concatenate([departure_in, jacobian, weight], axis=0)),
        smem=1,
    )

    def swap(x):
        return lax.all_to_all(x.reshape(tiles, -1, LANES), ("lat", "lon"), split_axis=0, concat_axis=0,
                              tiled=True).reshape(x.shape)

    got = swap(send)

    w_m, w_n, p_t, p_j, g3 = call(
        weights_kernel,
        (shape((3 * hidden, 3 * padded), BF), shape((3 * trim, 3 * hidden), BF), shape((hidden, padded), BF),
         shape((trim, hidden), BF), shape((trim + hidden, 3 * padded), BF)),
        (conv_taps, projection, jacobian, weight),
        staged=True,
    )

    slope_inner = jnp.transpose(slope, (1, 0, 2))
    low, high = lax.optimization_barrier((slope[:, -HALO:], slope[:, :HALO]))
    slope_north = shift2(jnp.transpose(low, (1, 0, 2)), 1, 0)
    slope_south = shift2(jnp.transpose(high, (1, 0, 2)), -1, 0)
    slope_west, slope_east = call(strip_kernel, (shape((hidden, strip), BF),) * 2,
                                  (slope_inner, slope_north, slope_south))

    north, south = call(
        functools.partial(edge_kernel, channels, height),
        (shape((HALO * trim, breadth), BF),) * 2,
        (got,),
    )
    from_south = shift2(north, -1, 0)
    south, slope_north, slope_south = lax.optimization_barrier((south, slope_north, slope_south))
    from_north = shift2(south, 1, 0)
    west, east = call(
        functools.partial(side_kernel, channels, height, breadth), (shape((padded, strip), BF),) * 2, (got,))
    to_west, to_east = call(
        functools.partial(join_kernel, height),
        (shape((padded + hidden, strip), BF),) * 2,
        (west, east, from_north, from_south, slope_west, slope_east, p_t),
        unread=1,
    )
    from_east = shift2(to_west, 0, -1)
    from_west = shift2(to_east, 0, 1)
    inner = call(functools.partial(grid_kernel, channels), shape((height, trim, breadth)), (got,))

    at = lax.axis_index("lat")
    flags = jnp.stack([at > 0, at < lax.axis_size("lat") - 1]).astype(jnp.int32)
    first, second, reply = call(
        functools.partial(main_kernel, channels, hidden, cap),
        (shape((ext, trim, breadth)),) * 2 + (shape((tiles * size, LANES), BF),),
        (flags, got, inner, from_north, from_south, from_east, from_west, slope_inner, slope_north,
         slope_south, w_n, w_m, p_t, p_j, g3),
        scratch=[
            pltpu.VMEM((ext, trim, wide), F32),
            pltpu.VMEM((ext, hidden, wide), BF),
            pltpu.VMEM((ext, hidden, wide), BF),
            pltpu.VMEM((ext, padded, wide), BF),
            pltpu.VMEM((ext, trim, LANES), F32),
            pltpu.VMEM((ext, 2 * padded, breadth), BF),
            pltpu.VMEM((2 * padded, slots), F32),
        ],
        smem=1,
        vmem=76,
    )
    back = swap(reply)
    return call(
        functools.partial(final_kernel, channels, cap, size),
        (shape((channels, height, breadth)), shape((rows, radiances))),
        (back, slot, departure_in, jacobian, first, second),
        scratch=[pltpu.VMEM((height, channels, breadth), F32), pltpu.SemaphoreType.DMA((height,))],
        away=(0,),
        vmem=32,
    )


def solution(mesh):
    placed = (
        P(("lat", "lon"), None),
        P(("lat", "lon"), None),
        P(("lat", "lon")),
        P(("lat", "lon")),
        P(("lat", "lon")),
        P(),
        P(),
        P(),
        P(),
        P(None, "lat", "lon"),
    )
    return jax.shard_map(
        on_device,
        mesh=mesh,
        in_specs=placed,
        out_specs=(P(None, "lat", "lon"), P(("lat", "lon"), None)),
        check_vma=False,
    )
```

```python
import functools

import jax
import jax.numpy as jnp
import numpy as np
from jax import lax
from jax.experimental import pallas as pl
from jax.experimental.pallas import tpu as pltpu
from jax.sharding import PartitionSpec as P

ITERS = 2
HALO = 4
LANES = 128
GROUP = 8
SIDE = 2 * HALO
BF = jnp.bfloat16
F32 = jnp.float32
INTERPRET = False
G = (27, 26, 25, 24, 48, 48)


def mxu(a, b, dims=((1,), (0,)), precision=None):
    return lax.dot_general(a, b, (dims, ((), ())), precision=precision, preferred_element_type=F32)


def call(kernel, outs, args, scratch=(), smem=0, vmem=24, unread=0, staged=False, away=()):
    def space(i, x):
        if i < smem:
            return pl.BlockSpec(memory_space=pltpu.SMEM)
        if i >= len(args) - unread:
            return pl.BlockSpec(memory_space=pl.ANY)
        if staged:
            return pl.BlockSpec(x.shape, lambda _: (0,) * x.ndim)
        return pl.BlockSpec(memory_space=pltpu.VMEM)

    leaves, tree = jax.tree.flatten(outs)
    out_specs = [pl.BlockSpec(memory_space=pl.ANY if i in away else pltpu.VMEM) for i in range(len(leaves))]
    return pl.pallas_call(
        kernel,
        out_shape=outs,
        grid=(1,) if staged else (),
        in_specs=[space(i, x) for i, x in enumerate(args)],
        out_specs=jax.tree.unflatten(tree, out_specs),
        scratch_shapes=scratch,
        interpret=INTERPRET,
        compiler_params=pltpu.CompilerParams(vmem_limit_bytes=vmem * 2**20 // 2),
    )(*args)


def split3(x):
    hi = x.astype(BF)
    rest = x - hi.astype(F32)
    mid = rest.astype(BF)
    return hi, mid, (rest - mid.astype(F32)).astype(BF)


def pack_kernel(tiles, cap, lon_size, channels, count, meta, table, send, slot_out):
    owner_row, cell_row, qc_row = meta[0:1], meta[1:2], meta[2:3]
    rows = meta.shape[1]
    dep, jac, weight = table[:rows], table[rows : rows + channels], table[rows + channels :]
    slots = send.shape[0]
    hit = (lax.broadcasted_iota(jnp.int32, (tiles, rows), 0) == owner_row).astype(BF)
    before = (lax.broadcasted_iota(jnp.int32, (rows, rows), 0)
              < lax.broadcasted_iota(jnp.int32, (rows, rows), 1)).astype(BF)
    earlier = mxu(hit, before)
    rank = jnp.sum(earlier * hit.astype(F32), axis=0, keepdims=True)
    slot = owner_row * cap + rank.astype(jnp.int32)
    slot_out[...] = slot
    place = (lax.broadcasted_iota(jnp.int32, (slots, rows), 0) == slot).astype(BF)

    used = (lax.broadcasted_iota(jnp.int32, (1, rows), 1) < count[0]).astype(F32)
    row_weight = used * qc_row.astype(F32)
    terms = mxu(jac, dep * weight, ((1,), (1,)), lax.Precision.HIGHEST) * row_weight
    lat = cell_row // lon_size
    lon = cell_row - lat * lon_size
    wide = lax.broadcasted_iota(jnp.int32, (LANES, rows), 0)
    terms = jnp.concatenate([terms, jnp.zeros((LANES - channels, rows), F32)], axis=0)
    terms = jnp.where(wide == channels, row_weight, terms)
    terms = jnp.where(wide == channels + 1, lat.astype(F32), terms)
    terms = jnp.where(wide == channels + 2, lon.astype(F32), terms)
    send[...] = mxu(place, terms.astype(BF), ((1,), (1,))).astype(BF)


def weights_kernel(taps, projection, jac, weight, w_m, w_n, p_t, p_j, g3):
    _, hidden, channels = taps.shape
    trim, padded = p_j.shape[0], p_t.shape[1]

    def shifted(rows, columns, by):
        return (lax.broadcasted_iota(jnp.int32, (rows, columns), 0) + by
                == lax.broadcasted_iota(jnp.int32, (rows, columns), 1)).astype(BF)

    wider, fuller = shifted(channels, padded, 0), shifted(channels, trim, 0)
    for b in range(3):
        total_m, total_n = 0.0, 0.0
        for a in range(3):
            tap = taps[3 * a + b]
            total_m = total_m + mxu(tap, shifted(channels, 3 * padded, a * padded))
            turned_tap = mxu(fuller, tap, ((0,), (1,))).astype(BF)
            total_n = total_n + mxu(turned_tap, shifted(hidden, 3 * hidden, (2 - a) * hidden))
        w_m[b * hidden : (b + 1) * hidden] = total_m.astype(BF)
        w_n[b * trim : (b + 1) * trim] = total_n.astype(BF)
    p_j[...] = mxu(fuller, projection[...], ((0,), (0,))).astype(BF)
    p_t[...] = mxu(projection[...], wider, ((0,), (0,))).astype(BF)
    tall = jnp.concatenate([jac[...], jnp.zeros((padded - channels, jac.shape[1]), F32)], axis=0)
    gram = mxu(tall * weight[...], tall, ((1,), (1,)), lax.Precision.HIGHEST)
    pulled = mxu(p_t[...].astype(F32), gram, precision=lax.Precision.HIGHEST)
    both = jnp.concatenate([gram[:trim], pulled], axis=0)
    hi = both.astype(BF)
    lo = (both - hi.astype(F32)).astype(BF)
    total = 0.0
    for k, value in enumerate((hi, lo, hi)):
        total = total + mxu(value, shifted(padded, 3 * padded, k * padded))
    g3[...] = total.astype(BF)


def turned(got, channels, padded):
    flat = got[...].astype(F32)
    turn = flat.T
    lat_row = turn[channels + 1 : channels + 2].astype(jnp.int32)
    lon_row = turn[channels + 2 : channels + 3].astype(jnp.int32)
    lat_col = flat[:, channels + 1 : channels + 2].astype(jnp.int32)
    lon_col = flat[:, channels + 2 : channels + 3].astype(jnp.int32)
    keep = lax.broadcasted_iota(jnp.int32, (padded, turn.shape[1]), 0) <= channels
    return jnp.where(keep, turn[:padded], 0.0), lat_row, lon_row, lat_col, lon_col


def edge_kernel(channels, height, got, north, south):
    tall, breadth = north.shape
    trim = tall // HALO
    slots = got.shape[0]
    turn, lat_row, _, _, lon = turned(got, channels, -(-trim // 16) * 16)
    values = turn.astype(BF)
    col_hot = (lax.broadcasted_iota(jnp.int32, (slots, breadth), 1) == lon).astype(BF)
    for out, first in ((north, 0), (south, height - HALO)):
        lhs = jnp.concatenate(
            [values * (lat_row == first + k).astype(F32).astype(BF) for k in range(HALO)], axis=0)
        rows = mxu(lhs, col_hot).reshape(HALO, values.shape[0], breadth)[:, :trim]
        out[...] = rows.reshape(tall, breadth).astype(BF)


def rows_of(message, padded):
    tall, breadth = message.shape
    rows = message[...].astype(F32).reshape(HALO, tall // HALO, breadth)
    if padded == tall // HALO:
        return rows
    return jnp.concatenate([rows, jnp.zeros((HALO, padded - tall // HALO, breadth), F32)], axis=1)


def side_kernel(channels, height, breadth, got, west, east):
    padded, strip = west.shape
    slots = got.shape[0]
    turn, _, _, lat, lon = turned(got, channels, padded)
    values = turn.astype(BF)
    for out, mask, col in (
        (west, lon < HALO, HALO + lon),
        (east, lon >= breadth - HALO, lon - (breadth - HALO)),
    ):
        target = jnp.where(mask, (lat + HALO) * SIDE + col, -1)
        hot = (lax.broadcasted_iota(jnp.int32, (slots, strip), 1) == target).astype(BF)
        out[...] = mxu(values, hot).astype(BF)


def grid_kernel(channels, got, out):
    height, trim, breadth = out.shape
    padded = -(-trim // 16) * 16
    slots = got.shape[0]
    turn, lat_row, _, _, lon = turned(got, channels, padded)
    values = turn.astype(BF)
    col_hot = (lax.broadcasted_iota(jnp.int32, (slots, breadth), 1) == lon).astype(BF)
    step = 8

    def body(block, _):
        lhs = jnp.concatenate(
            [values * (lat_row == block * step + k).astype(F32).astype(BF) for k in range(step)], axis=0)
        out[pl.ds(block * step, step)] = mxu(lhs, col_hot).reshape(step, padded, breadth)[:, :trim]
        return 0

    lax.fori_loop(0, height // step, body, 0)


def to_strip(rows, base, block):
    per = LANES // SIDE
    shape = (rows[0].shape[0], LANES)
    lane = lax.broadcasted_iota(jnp.int32, shape, 1)
    left, right = jnp.zeros(shape, F32), jnp.zeros(shape, F32)
    for k, row in enumerate(rows):
        at = base + k - block * per
        if not 0 <= at < per:
            continue
        row = row.astype(F32)
        by = (at * SIDE + HALO) % LANES
        mine = (lane >= at * SIDE) & (lane < (at + 1) * SIDE)
        left = jnp.where(mine & (lane % SIDE >= HALO), pltpu.roll(row[:, :LANES], by, 1), left)
        right = jnp.where(mine & (lane % SIDE < HALO), pltpu.roll(row[:, -LANES:], by, 1), right)
    return left, right


def strip_kernel(inner, north, south, west, east):
    height = inner.shape[0]
    rows = [north[k] for k in range(HALO)] + [inner[k] for k in range(height)] + [south[k] for k in range(HALO)]
    for block in range(west.shape[1] // LANES):
        left, right = to_strip(rows, 0, block)
        west[:, block * LANES : (block + 1) * LANES] = left.astype(BF)
        east[:, block * LANES : (block + 1) * LANES] = right.astype(BF)


def join_kernel(height, west, east, from_north, from_south, slope_west, slope_east, _token, to_west, to_east):
    padded, strip = west.shape
    last = (height + HALO) * SIDE // LANES
    above, below = rows_of(from_north, padded), rows_of(from_south, padded)
    above = to_strip([above[k] for k in range(HALO)], 0, 0)
    below = to_strip([below[k] for k in range(HALO)], HALO + height, last)
    for k, own, slope, out in ((0, west, slope_west, to_west), (1, east, slope_east, to_east)):
        for block in range(strip // LANES):
            part = pl.ds(block * LANES, LANES)
            q = own[:, part]
            if block == 0:
                q = q + above[k].astype(BF)
            if block == last:
                q = q + below[k].astype(BF)
            out[:padded, part] = q
        out[padded:] = slope[...]


def main_kernel(channels, hidden, cap, flags, got, inner, north, south, from_east, from_west, slope_inner,
                slope_north, slope_south, w_n, w_m, p_t, p_j, g3, first_out, second_out, reply,
                field, slope, ga, xb, vec, hi, found):
    height, trim, breadth = inner.shape
    padded = xb.shape[1]
    wide = breadth + LANES
    ext = height + 2 * HALO
    per = LANES // SIDE

    def is_in(i):
        above = (i >= HALO) | (flags[0] == 1)
        below = (i < height + HALO) | (flags[1] == 1)
        return (above & below).astype(F32)

    def join(parts):
        return jnp.concatenate(parts, axis=1)

    def part(x, k, lanes=wide):
        return x[:, k * lanes : (k + 1) * lanes]

    def fill(x):
        return jnp.concatenate([x, jnp.zeros((padded - trim, x.shape[1]), F32)], axis=0).astype(BF)

    def pull(i, ys):
        u = mxu(p_t[...], join([fill(y) for y in ys]))
        for k in range(len(ys)):
            ga[i + k] = (slope[i + k].astype(F32) * part(u, k)).astype(BF)

    lane = lax.broadcasted_iota(jnp.int32, (padded + hidden, LANES), 1)
    from_the_west = lane % SIDE < HALO

    def begin(i, mains, slopes):
        ys = []
        for k in range(len(mains)):
            if k % HALO == 0:
                at = pl.ds(pl.multiple_of((i + k) // per * LANES, LANES), LANES)
                both = jnp.where(from_the_west, from_west[:, at].astype(F32), from_east[:, at].astype(F32))
            shift = 2 * LANES - (i + k) % per * SIDE - HALO
            edge = pltpu.roll(both, shift % LANES, 1)
            y = join([mains[k].astype(F32), edge[:trim]])
            field[i + k] = y
            slope[i + k] = join([slopes[k], edge[padded:].astype(BF)])
            ys.append(y)
        pull(i, ys)

    above, below = rows_of(north, trim), rows_of(south, trim)
    begin(0, [above[k] for k in range(HALO)], [slope_north[k] for k in range(HALO)])
    begin(HALO + height, [below[k] for k in range(HALO)], [slope_south[k] for k in range(HALO)])

    def middle(n, _):
        i = n * G[5]
        begin(i + HALO, [inner[i + k] for k in range(G[5])], [slope_inner[i + k] for k in range(G[5])])
        return 0

    lax.fori_loop(0, height // G[5], middle, 0)

    def spread(i, ys):
        o = mxu(w_n[...], join([ga[pl.ds(i + k - 1, 3)].reshape(3 * hidden, wide) for k in range(len(ys))]))
        out = []
        for k, y in enumerate(ys):
            p = part(o, k)
            out.append(y + p[trim : 2 * trim] + pltpu.roll(p[:trim], wide - 1, 1)
                       + pltpu.roll(p[2 * trim :], 1, 1))
        return out

    def tangent(i, vs):
        lanes = vs[0].shape[1]
        o = mxu(w_m[...], join([xb[pl.ds(i + k - 1, 3)].reshape(3 * padded, wide) for k in range(len(vs))]))
        acts = []
        for k in range(len(vs)):
            p = part(o, k)
            h = (p[hidden : 2 * hidden] + pltpu.roll(p[:hidden], 1, 1)
                 + pltpu.roll(p[2 * hidden :], wide - 1, 1))
            acts.append((slope[i + k].astype(F32) * h).astype(BF)[:, :lanes])
        back = mxu(p_j[...], join(acts))
        return [v + part(back, k, lanes) for k, v in enumerate(vs)]

    def gram_of(s, matrix):
        s_hi = s.astype(BF).astype(F32)
        s_lo = fill(s - s_hi)
        s_hi = fill(s_hi)
        return mxu(matrix, jnp.concatenate([s_hi, s_hi, s_lo], axis=0))

    def loop(first, last, size, body):
        assert (last - first) % size == 0

        def step(n, _):
            body(first + n * size)
            return 0

        lax.fori_loop(0, (last - first) // size, step, 0)

    def n_first(i):
        for k, v in enumerate(spread(i, [field[i + k] for k in range(G[0])])):
            first_out[i + k] = v[:, :breadth]
            vec[i + k] = v[:, breadth:]
            xb[i + k] = fill(v * is_in(i + k))

    loop(1, ext - 1, G[0], n_first)

    def m_first(i):
        ss = tangent(i, [join([first_out[i + k], vec[i + k]]) for k in range(G[1])])
        gs = gram_of(join(ss), g3[...])
        for k, s in enumerate(ss):
            cell_weight = field[i + k][channels : channels + 1]
            both = part(gs, k)
            hi[i + k, :padded] = fill(s[:, :breadth])
            field[i + k] = cell_weight * both[:trim]
            ga[i + k] = (slope[i + k].astype(F32) * (cell_weight * both[trim:])).astype(BF)

    loop(2, ext - 2, G[1], m_first)

    def n_second(i):
        for k, v in enumerate(spread(i, [field[i + k] for k in range(G[2])])):
            second_out[i + k] = v[:, :breadth]
            xb[i + k] = fill(v * is_in(i + k))

    loop(3, ext - 3, G[2], n_second)

    def m_second(i):
        for k, s in enumerate(tangent(i, [second_out[i + k] for k in range(G[3])])):
            hi[i + k, padded:] = fill(s)

    loop(HALO, ext - HALO, G[3], m_second)

    turn, lat_row, lon_row, _, _ = turned(got, channels, padded)
    slots = got.shape[0]
    piece = 256
    for c in range(slots // piece):
        here = slice(c * piece, (c + 1) * piece)
        col_hot = (lax.broadcasted_iota(jnp.int32, (breadth, piece), 0) == lon_row[:, here]).astype(BF)
        found[:, here] = jnp.zeros((2 * padded, piece), F32)

        def gather(i, col_hot=col_hot, here=here):
            out = mxu(hi[pl.ds(i, G[4])].reshape(G[4] * 2 * padded, breadth), col_hot)
            total = found[:, here]
            for k in range(G[4]):
                mine = (lat_row[:, here] == i + k - HALO)
                total = total + jnp.where(mine, out[k * 2 * padded : (k + 1) * 2 * padded], 0.0)
            found[:, here] = total

        loop(HALO, ext - HALO, G[4], gather)

    row0, row1 = found[:trim], found[padded : padded + trim]
    weight = turn[channels : channels + 1]
    curved0 = gram_of(row0, g3[:trim]) * weight
    curved1 = gram_of(row1, g3[:trim]) * weight
    real = lax.broadcasted_iota(jnp.int32, (trim, slots), 0) < channels
    first = jnp.where(real, turn[:trim], 0.0)

    def total(x):
        return jnp.sum(jnp.sum(x, axis=0, keepdims=True), axis=1, keepdims=True)

    sums = (total(first * row0), total(curved0 * row0), total(curved0 * row1), total(curved1 * row1))
    lane = lax.broadcasted_iota(jnp.int32, (1, LANES), 1)
    pieces = jnp.zeros((1, LANES), F32)
    for number, value in enumerate(sums):
        for third, piece in enumerate(split3(value)):
            pieces = jnp.where(lane == 3 * number + third, piece.astype(F32), pieces)
    size = reply.shape[0] * cap // slots
    slot = lax.broadcasted_iota(jnp.int32, (1, slots), 1)
    near, far, turn_of = reply_rows(slot, cap, size)
    start = jnp.concatenate([row0, row1[: LANES - trim]], axis=0).astype(BF)
    end = jnp.concatenate([row1[LANES - trim :]] * GROUP, axis=0)
    tail = LANES // GROUP
    end = jnp.where(lax.broadcasted_iota(jnp.int32, (LANES, slots), 0) // tail == turn_of, end, 0.0).astype(BF)
    at = lax.broadcasted_iota(jnp.int32, (reply.shape[0], slots), 0)
    packed = mxu((at == near).astype(BF), start, ((1,), (1,))) + mxu((at == far).astype(BF), end, ((1,), (1,)))
    row = lax.broadcasted_iota(jnp.int32, reply.shape, 0)
    reply[...] = jnp.where(row % size == size - 1, pieces, packed).astype(BF)


def reply_rows(slot, cap, size):
    block = slot // cap
    inside = slot - block * cap
    return block * size + inside, block * size + cap + inside // GROUP, inside % GROUP


def scalars(reply, size):
    row = lax.broadcasted_iota(jnp.int32, reply.shape, 0)
    sums = jnp.sum(jnp.where(row % size == size - 1, reply[...].astype(F32), 0.0), axis=0, keepdims=True)

    def value(number):
        at = 3 * number
        return sums[:, at : at + 1] + sums[:, at + 1 : at + 2] + sums[:, at + 2 : at + 3]

    a00, a01, a11, d11 = (value(n) for n in range(4))
    step0 = a00 / (a00 + a01)
    keep = 1.0 - step0
    norm1 = keep * keep * a00 - 2.0 * step0 * keep * a01 + step0 * step0 * a11
    c0 = keep + norm1 / a00
    c1 = -step0
    curve = (c0 * c0 * (a00 + a01) + 2.0 * c0 * c1 * (a01 + a11) + c1 * c1 * (a11 + d11))
    step1 = norm1 / curve
    return step0 + step1 * c0, step1 * c1


def final_kernel(channels, cap, size, back, slot, dep, jac, first, second, increment, departures, mixed, sems):
    rows = dep.shape[0]
    height = mixed.shape[0]
    a, b = scalars(back, size)

    def copy(i):
        return pltpu.make_async_copy(mixed.at[i], increment.at[:, i], sems.at[i])

    for i in range(height):
        mixed[i] = a * first[i + HALO, :channels] + b * second[i + HALO, :channels]
        copy(i).start()
    near, far, turn_of = reply_rows(slot[...], cap, size)
    at = lax.broadcasted_iota(jnp.int32, (back.shape[0], rows), 0)
    start = mxu(back[...], (at == near).astype(BF), ((0,), (0,)))
    end = mxu(back[...], (at == far).astype(BF), ((0,), (0,)))
    tail = LANES // GROUP
    end = jnp.where(lax.broadcasted_iota(jnp.int32, (LANES, rows), 0) // tail == turn_of, end, 0.0)
    end = functools.reduce(jnp.add, [end[k * tail : (k + 1) * tail] for k in range(GROUP)])
    trim = first.shape[1]
    state = a * start[:trim] + b * jnp.concatenate([start[trim:], end], axis=0)
    departures[...] = dep[...] - mxu(state[:channels], jac[...], ((0,), (0,)), lax.Precision.HIGHEST)
    for i in range(height):
        copy(i).wait()


def shift2(x, by_lat, by_lon):
    n_lat, n_lon = lax.axis_size("lat"), lax.axis_size("lon")
    pairs = [(i * n_lon + j, (i + by_lat) * n_lon + (j + by_lon) % n_lon)
             for i in range(n_lat) for j in range(n_lon) if 0 <= i + by_lat < n_lat]
    return lax.ppermute(x, ("lat", "lon"), pairs)


def on_device(departure_in, obs_owner, obs_cell, obs_count, qc_mask, channel_weight, jacobian,
              conv_taps, projection, slope):
    channels, hidden = projection.shape
    height, breadth = slope.shape[1], slope.shape[2]
    tiles = lax.axis_size(("lat", "lon"))
    rows, radiances = departure_in.shape
    cap = max(2, 3 * rows // (2 * tiles))
    slots = tiles * cap
    padded = -(-(channels + 1) // 16) * 16
    trim = -(-(channels + 1) // 8) * 8
    assert 2 * trim == LANES + LANES // GROUP
    size = -(-(cap + -(-cap // GROUP) + 1) // 8) * 8
    wide = breadth + LANES
    ext = height + 2 * HALO
    strip = -(-(ext * SIDE) // LANES) * LANES

    def shape(dims, kind=F32):
        return jax.ShapeDtypeStruct(dims, kind)

    weight = channel_weight[None, :]
    send, slot = call(
        functools.partial(pack_kernel, tiles, cap, breadth, channels),
        (shape((slots, LANES), BF), shape((1, rows), jnp.int32)),
        (obs_count, jnp.stack([obs_owner[:, 0], obs_cell, qc_mask]),
         jnp.concatenate([departure_in, jacobian, weight], axis=0)),
        smem=1,
    )

    def swap(x):
        return lax.all_to_all(x.reshape(tiles, -1, LANES), ("lat", "lon"), split_axis=0, concat_axis=0,
                              tiled=True).reshape(x.shape)

    got = swap(send)

    w_m, w_n, p_t, p_j, g3 = call(
        weights_kernel,
        (shape((3 * hidden, 3 * padded), BF), shape((3 * trim, 3 * hidden), BF), shape((hidden, padded), BF),
         shape((trim, hidden), BF), shape((trim + hidden, 3 * padded), BF)),
        (conv_taps, projection, jacobian, weight),
        staged=True,
    )

    slope_inner = jnp.transpose(slope, (1, 0, 2))
    low, high = lax.optimization_barrier((slope[:, -HALO:], slope[:, :HALO]))
    slope_north = shift2(jnp.transpose(low, (1, 0, 2)), 1, 0)
    slope_south = shift2(jnp.transpose(high, (1, 0, 2)), -1, 0)
    slope_west, slope_east = call(strip_kernel, (shape((hidden, strip), BF),) * 2,
                                  (slope_inner, slope_north, slope_south))

    north, south = call(
        functools.partial(edge_kernel, channels, height),
        (shape((HALO * trim, breadth), BF),) * 2,
        (got,),
    )
    from_south = shift2(north, -1, 0)
    south, slope_north, slope_south = lax.optimization_barrier((south, slope_north, slope_south))
    from_north = shift2(south, 1, 0)
    west, east = call(
        functools.partial(side_kernel, channels, height, breadth), (shape((padded, strip), BF),) * 2, (got,))
    to_west, to_east = call(
        functools.partial(join_kernel, height),
        (shape((padded + hidden, strip), BF),) * 2,
        (west, east, from_north, from_south, slope_west, slope_east, p_t),
        unread=1,
    )
    from_east = shift2(to_west, 0, -1)
    from_west = shift2(to_east, 0, 1)
    inner = call(functools.partial(grid_kernel, channels), shape((height, trim, breadth)), (got,))

    at = lax.axis_index("lat")
    flags = jnp.stack([at > 0, at < lax.axis_size("lat") - 1]).astype(jnp.int32)
    first, second, reply = call(
        functools.partial(main_kernel, channels, hidden, cap),
        (shape((ext, trim, breadth)),) * 2 + (shape((tiles * size, LANES), BF),),
        (flags, got, inner, from_north, from_south, from_east, from_west, slope_inner, slope_north,
         slope_south, w_n, w_m, p_t, p_j, g3),
        scratch=[
            pltpu.VMEM((ext, trim, wide), F32),
            pltpu.VMEM((ext, hidden, wide), BF),
            pltpu.VMEM((ext, hidden, wide), BF),
            pltpu.VMEM((ext, padded, wide), BF),
            pltpu.VMEM((ext, trim, LANES), F32),
            pltpu.VMEM((ext, 2 * padded, breadth), BF),
            pltpu.VMEM((2 * padded, slots), F32),
        ],
        smem=1,
        vmem=76,
    )
    back = swap(reply)
    return call(
        functools.partial(final_kernel, channels, cap, size),
        (shape((channels, height, breadth)), shape((rows, radiances))),
        (back, slot, departure_in, jacobian, first, second),
        scratch=[pltpu.VMEM((height, channels, breadth), F32), pltpu.SemaphoreType.DMA((height,))],
        away=(0,),
        vmem=32,
    )


def solution(mesh):
    placed = (
        P(("lat", "lon"), None),
        P(("lat", "lon"), None),
        P(("lat", "lon")),
        P(("lat", "lon")),
        P(("lat", "lon")),
        P(),
        P(),
        P(),
        P(),
        P(None, "lat", "lon"),
    )
    return jax.shard_map(
        on_device,
        mesh=mesh,
        in_specs=placed,
        out_specs=(P(None, "lat", "lon"), P(("lat", "lon"), None)),
        check_vma=False,
    )
```
